32 devices in a mesh: fsdp: 8 (over z, x), seq: 4 (over y, core).
Axes of the slice: x: 2, y: 2, z: 4, core: 2. Of those that a mesh axis runs over, the one named last changes fastest.
Arguments:
- inputs: bfloat16 [8, 1024, 768], P('fsdp', 'seq'), may hold values from -6 to 6
- qkv_weight: bfloat16 [1769472], P(('fsdp', 'seq')), may hold values from -0.21875 to 0.21875
- q_bias: bfloat16 [768], P(('fsdp', 'seq')), may hold values from -1.796875 to 1.796875
- v_bias: bfloat16 [768], P(('fsdp', 'seq')), may hold values from -1.796875 to 1.796875
- out_weight: bfloat16 [589824], P(('fsdp', 'seq')), may hold values from -0.875 to 0.875
- out_bias: bfloat16 [768], P(('fsdp', 'seq')), may hold values from -1.796875 to 1.796875
- norm1_gain: bfloat16 [768], P(('fsdp', 'seq')), may hold values from 0.5 to 1.5
- norm1_bias: bfloat16 [768], P(('fsdp', 'seq')), may hold values from -1.796875 to 1.796875
- up_weight: bfloat16 [2359296], P(('fsdp', 'seq')), may hold values from -0.21875 to 0.21875
- up_bias: bfloat16 [3072], P(('fsdp', 'seq')), may hold values from -1.796875 to 1.796875
- down_weight: bfloat16 [2359296], P(('fsdp', 'seq')), may hold values from -0.109375 to 0.109375
- down_bias: bfloat16 [768], P(('fsdp', 'seq')), may hold values from -1.796875 to 1.796875
- norm2_gain: bfloat16 [768], P(('fsdp', 'seq')), may hold values from 0.5 to 1.5
- norm2_bias: bfloat16 [768], P(('fsdp', 'seq')), may hold values from -1.796875 to 1.796875
- cotangent: bfloat16 [8, 1024, 768], P('fsdp', 'seq'), may hold values from -6 to 6
- segment_ids: int32 [8, 1024], P('fsdp'), may hold values from 0 to 2, as said below
- pad_mask: int32 [8, 1024], P('fsdp'), may hold values from 0 to 1, as said below
- keep_flag: int32 [8], P('fsdp'), may hold values 0 or 1
Outputs:
- outputs: bfloat16 [8, 1024, 768], P('fsdp', 'seq')
- input_grad: bfloat16 [8, 1024, 768], P('fsdp', 'seq')
- grad_qkv_weight: float32 [1769472], P(('fsdp', 'seq'))
- grad_q_bias: float32 [768], P(('fsdp', 'seq'))
- grad_v_bias: float32 [768], P(('fsdp', 'seq'))
- grad_out_weight: float32 [589824], P(('fsdp', 'seq'))
- grad_out_bias: float32 [768], P(('fsdp', 'seq'))
- grad_norm1_gain: float32 [768], P(('fsdp', 'seq'))
- grad_norm1_bias: float32 [768], P(('fsdp', 'seq'))
- grad_up_weight: float32 [2359296], P(('fsdp', 'seq'))
- grad_up_bias: float32 [3072], P(('fsdp', 'seq'))
- grad_down_weight: float32 [2359296], P(('fsdp', 'seq'))
- grad_down_bias: float32 [768], P(('fsdp', 'seq'))
- grad_norm2_gain: float32 [768], P(('fsdp', 'seq'))
- grad_norm2_bias: float32 [768], P(('fsdp', 'seq'))
The draws below stay inside these ranges and needn't reach their ends.
Inputs may be any that keep to these rules, and one draw needn't show every extreme that they name: `segment_ids`: each row's ids never fall and start at 0; every row holds exactly three documents, the middle one starting within the first 256 tokens and ending within the last 256 tokens. `pad_mask`: Padding, if any, stands at the end of a row inside its last document, which keeps at least one real token.
All inputs are finite; a program needn't handle non-finite values. No bound on the sum of `keep_flag` on one device may be relied on, other than what follows from the above.
Results may differ from the reference program's by a relative error of at most 0.017.
Values may be sent and summed in bfloat16 or wider, within the bound.
A program may use at most 192 MiB of HBM per device.

```python
import jax
import jax.numpy as jnp
from jax import lax

D = 768
HEADS = 12
HD = 64
FF = 3072
BLK = 256
SEQUENCES = 8
LEN = 1024


def layout(key):
    first_key, tail_key, pad_key = jax.random.split(key, 3)
    first = jax.random.randint(first_key, (SEQUENCES, 1), 1, BLK)
    tail = jax.random.randint(tail_key, (SEQUENCES, 1), 1, max(BLK // 4, 2))
    padding = jax.random.randint(pad_key, (SEQUENCES, 1), 0, BLK // 4 + 1)
    position = jnp.arange(LEN, dtype=jnp.int32)[None, :]
    second_end = LEN - tail - padding
    segments = (position >= first).astype(jnp.int32) + (position >= second_end).astype(jnp.int32)
    real = (position < LEN - padding).astype(jnp.int32)
    return (segments, real)


def draw_segment_ids(key, part):
    return layout(key)[0]


def draw_pad_mask(key, part):
    return layout(key)[1]


def place_ends(values, stream_key, smallest, high):
    longest = values.shape.index(max(values.shape))
    spots = []
    for shift in (0, 1):
        where = [jax.random.randint(jax.random.fold_in(stream_key, axis), (), 0, length) for axis, length in enumerate(values.shape)]
        where[longest] = (where[longest] + shift) % values.shape[longest]
        spots.append(tuple(where))
    return values.at[spots[0]].set(smallest).at[spots[1]].set(high)


def levels(rng, extent, cuts, smallest, largest):
    def one(dim, shards_of):
        draws = jax.random.uniform(jax.random.fold_in(jax.random.fold_in(rng, 6), dim), (shards_of,), jnp.float32, smallest / len(cuts), largest / len(cuts))
        return jnp.repeat(jnp.exp(draws), extent[dim] // shards_of).reshape((-1,) + (1,) * (len(extent) - dim - 1))

    loudness = one(*cuts[0])
    for cut in cuts[1:]:
        loudness = loudness * one(*cut)
    return loudness


def bell_draw(rng, shape, scale, reach, shards=(), kind=jnp.bfloat16):
    values = scale * jax.random.normal(rng, shape, jnp.float32)
    if shards:
        values = values * levels(rng, shape, shards, -0.22, 0.18)
    return jnp.clip(values, -reach, reach).astype(kind)


def setup_inputs(seed: int = 0) -> dict:
    arg_keys = jax.random.split(jax.random.key(seed), 19)
    return {
        "inputs": bell_draw(arg_keys[0], (SEQUENCES, LEN, D), 1.0, 6.0, ((0, 8), (1, 4))),
        "qkv_weight": bell_draw(arg_keys[1], (3 * D * D,), D ** -0.5, 0.21875, ((0, 32),)),
        "q_bias": bell_draw(arg_keys[2], (D,), 0.3, 1.796875, ((0, 32),)),
        "v_bias": bell_draw(arg_keys[3], (D,), 0.3, 1.796875, ((0, 32),)),
        "out_weight": bell_draw(arg_keys[4], (D * D,), (D // 16) ** -0.5, 0.875, ((0, 32),)),
        "out_bias": bell_draw(arg_keys[5], (D,), 0.3, 1.796875, ((0, 32),)),
        "norm1_gain": jnp.clip(1.0 + 0.1 * jax.random.normal(arg_keys[6], (D,), jnp.float32), 0.5, 1.5).astype(jnp.bfloat16),
        "norm1_bias": bell_draw(arg_keys[7], (D,), 0.3, 1.796875, ((0, 32),)),
        "up_weight": bell_draw(arg_keys[8], (D * FF,), D ** -0.5, 0.21875, ((0, 32),)),
        "up_bias": bell_draw(arg_keys[9], (FF,), 0.3, 1.796875, ((0, 32),)),
        "down_weight": bell_draw(arg_keys[10], (FF * D,), FF ** -0.5, 0.109375, ((0, 32),)),
        "down_bias": bell_draw(arg_keys[11], (D,), 0.3, 1.796875, ((0, 32),)),
        "norm2_gain": jnp.clip(1.0 + 0.1 * jax.random.normal(arg_keys[12], (D,), jnp.float32), 0.5, 1.5).astype(jnp.bfloat16),
        "norm2_bias": bell_draw(arg_keys[13], (D,), 0.3, 1.796875, ((0, 32),)),
        "cotangent": bell_draw(arg_keys[14], (SEQUENCES, LEN, D), 1.0, 6.0, ((0, 8), (1, 4))),
        "segment_ids": draw_segment_ids(jax.random.fold_in(arg_keys[18], 71), 0),
        "pad_mask": draw_pad_mask(jax.random.fold_in(arg_keys[18], 71), 0),
        "keep_flag": place_ends((jax.random.randint(arg_keys[17], (SEQUENCES,), 0, 4) < 3).astype(jnp.int32), jax.random.fold_in(arg_keys[17], 1), 0, 1),
    }


epsilon = 1e-05
masked_score = -1000000000.0
score_scale = 0.125

@jax.custom_vjp
def low(v):
    return lax.optimization_barrier(v.astype(jnp.bfloat16)).astype(jnp.float32)

@jax.custom_vjp
def low_back(v):
    return v

def low_keep(v):
    return (low(v), None)

def low_pass(kept, grad):
    return (grad,)

def back_keep(v):
    return (v, None)

def back_low(kept, grad):
    return (low(grad),)
low.defvjp(low_keep, low_pass)
low_back.defvjp(back_keep, back_low)

def product(left, right):
    return jnp.matmul(left, right, precision=lax.Precision.HIGHEST)

def normalize(hidden, gain, shift):
    centre = lax.optimization_barrier(jnp.mean(hidden, -1, keepdims=True))
    centred = hidden - centre
    variance = lax.optimization_barrier(jnp.mean(centred * centred, -1, keepdims=True))
    return centred * lax.rsqrt(variance + epsilon) * gain + shift

def gelu_exact(value):
    return jax.nn.gelu(value, approximate=False)

def layer(inputs, params, segments, padding, keep):
    qkv_w, query_shift, value_shift, out_w, out_shift, gain_one, shift_one, up_w, up_shift, down_w, down_shift, gain_two, shift_two = params
    groups, length, width = inputs.shape
    qkv = product(inputs, qkv_w)
    queries = low_back(low(qkv[..., :width] + query_shift))
    keys = low_back(low(qkv[..., width:2 * width]))
    values = low_back(low(qkv[..., 2 * width:] + value_shift))
    query_heads = queries.reshape(groups, length, HEADS, HD)
    key_heads = keys.reshape(groups, length, HEADS, HD)
    value_heads = values.reshape(groups, length, HEADS, HD)
    scores = low_back(jnp.einsum('gihd,gjhd->ghij', query_heads, key_heads, precision=lax.Precision.HIGHEST) * score_scale)
    allowed = (segments[:, :, None] == segments[:, None, :]) & (padding[:, None, :] > 0)
    scores = jnp.where(allowed[:, None], scores, masked_score)
    peak = lax.optimization_barrier(jnp.max(scores, -1, keepdims=True))
    expd = jnp.exp(scores - peak)
    probs = low(expd / lax.optimization_barrier(jnp.sum(expd, -1, keepdims=True)))
    attended = jnp.einsum('ghij,gjhd->gihd', probs, value_heads, precision=lax.Precision.HIGHEST)
    attended = low_back(low(attended.reshape(groups, length, width)))
    attn_out = low_back(product(attended, out_w) + out_shift)
    normed = normalize(inputs + attn_out, gain_one, shift_one)
    before = low_back(product(low(normed), up_w) + up_shift)
    activated = low_back(low(gelu_exact(before)))
    branch = low_back(product(activated, down_w) + down_shift)
    final = normalize(normed + branch, gain_two, shift_two)
    return jnp.where(keep[:, None, None] > 0, final, inputs)

def add_up(first, second):
    return first + second

def reference(inputs, qkv_weight, q_bias, v_bias, out_weight, out_bias, norm1_gain, norm1_bias, up_weight, up_bias, down_weight, down_bias, norm2_gain, norm2_bias, cotangent, segment_ids, pad_mask, keep_flag):
    params = (qkv_weight.astype(jnp.float32).reshape(D, 3 * D), q_bias.astype(jnp.float32), v_bias.astype(jnp.float32), out_weight.astype(jnp.float32).reshape(D, D), out_bias.astype(jnp.float32), norm1_gain.astype(jnp.float32), norm1_bias.astype(jnp.float32), up_weight.astype(jnp.float32).reshape(D, FF), up_bias.astype(jnp.float32), down_weight.astype(jnp.float32).reshape(FF, D), down_bias.astype(jnp.float32), norm2_gain.astype(jnp.float32), norm2_bias.astype(jnp.float32))
    sequences = inputs.shape[0]
    couples = sequences // 2

    def grouped(array):
        return array.reshape((couples, 2) + array.shape[1:])

    def step(carry, slab):
        block_in, block_cot, block_seg, block_pad, block_keep = slab

        def forward(values, weights):
            return layer(values, weights, block_seg, block_pad, block_keep)
        result, pullback = jax.vjp(forward, block_in.astype(jnp.float32), params)
        grad_in, grad_params = pullback(block_cot.astype(jnp.float32))
        carry = jax.tree.map(add_up, carry, grad_params)
        return (carry, (result.astype(jnp.bfloat16), grad_in.astype(jnp.bfloat16)))
    zeros = jax.tree.map(jnp.zeros_like, params)
    totals, (results, grads) = lax.scan(step, zeros, (grouped(inputs), grouped(cotangent), grouped(segment_ids), grouped(pad_mask), grouped(keep_flag)))
    return (results.reshape(inputs.shape), grads.reshape(inputs.shape), totals[0].reshape(-1), totals[1], totals[2], totals[3].reshape(-1), totals[4], totals[5], totals[6], totals[7].reshape(-1), totals[8], totals[9].reshape(-1), totals[10], totals[11], totals[12])
```

```python
import functools
import jax
import jax.numpy as jnp
import numpy as np
from jax import lax
from jax.experimental import pallas as pl
from jax.experimental.pallas import tpu as pltpu
from jax.sharding import Mesh, PartitionSpec as P

MESH = pl.DeviceIdType.MESH
D = 768
FF = 3072
BF = jnp.bfloat16
F32 = jnp.float32
LINES = (432, 144, 576, 576, 16)
BASE = (0, 432, 576, 1152, 1728)
TOTAL = 1744


class Place:
    def __init__(self):
        o = lax.axis_index("outer")
        s = lax.axis_index("seq")
        self.z, self.x, self.y, self.c = o // 2, o % 2, s // 2, s % 2

    def to(self, way):
        z, x, y, c = self.z, self.x, self.y, self.c
        return {
            "up": {"outer": (z + 1) * 2 + x},
            "down": {"outer": (z - 1) * 2 + x},
            "x": {"outer": z * 2 + 1 - x},
            "y": {"seq": (1 - y) * 2 + c},
            "core": {"seq": y * 2 + 1 - c},
        }[way]


def enter(me):
    bar = pltpu.get_barrier_semaphore()
    for way in ("x", "y", "core"):
        pl.semaphore_signal(bar, 1, device_id=me.to(way), device_id_type=MESH)

    @pl.when(me.z < 3)
    def _():
        pl.semaphore_signal(bar, 1, device_id=me.to("up"), device_id_type=MESH)

    @pl.when(me.z > 0)
    def _():
        pl.semaphore_signal(bar, 1, device_id=me.to("down"), device_id_type=MESH)

    both = jnp.where(me.z < 3, 1, 0) + jnp.where(me.z > 0, 1, 0)
    pl.semaphore_wait(bar, 3 + both)


WAYS = ("up", "down", "x", "y", "core")

PARTS = (
    ("small", "zxy"),
    ("qkv0", "zxy"),
    ("qkv1", "zyx"),
    ("out", "zxy"),
    ("up0", "xzy"),
    ("up1", "yzx"),
    ("down0", "xzy"),
    ("down1", "yzx"),
)
NAMES = [p[0] for p in PARTS]
ORDER = dict(PARTS)


class Gather:
    def __init__(self, me, refs, send, recv, crecv):
        self.me = me
        self.refs = refs
        self.send, self.recv, self.crecv = send, recv, crecv

    def block(self, part, chip, c):
        wqkv, wo, wu, wd, sm = self.refs
        m = pl.multiple_of
        if part == "small":
            return sm.at[pl.ds(m((chip * 2 + c) * 16, 16), 16), :]
        if part == "qkv0":
            return wqkv.at[pl.ds(m(chip * 48, 16), 48), pl.ds(m(c * 1152, 128), 640)]
        if part == "qkv1":
            return wqkv.at[pl.ds(m(chip * 48, 16), 48), pl.ds(m(c * 1152 + 640, 128), 512)]
        if part == "out":
            return wo.at[pl.ds(m(chip * 48, 16), 48), pl.ds(m(c * 384, 128), 384)]
        if part == "up0":
            return wu.at[pl.ds(m(chip * 48, 16), 48), pl.ds(m(c * 1536, 128), 768)]
        if part == "up1":
            return wu.at[pl.ds(m(chip * 48, 16), 48), pl.ds(m(c * 1536 + 768, 128), 768)]
        if part == "down0":
            return wd.at[pl.ds(m(chip * 192, 16), 96), pl.ds(m(c * 384, 128), 384)]
        if part == "down1":
            return wd.at[pl.ds(m(chip * 192 + 96, 16), 96), pl.ds(m(c * 384, 128), 384)]

    def chip(self, x, y, z):
        return (z * 2 + x) * 2 + y

    def copy(self, part, chip, way, arrival=None):
        i = NAMES.index(part)
        me = self.me
        ref = self.block(part, chip, me.c)
        sems = self.crecv if way == "core" else self.recv
        return pltpu.make_async_remote_copy(
            ref, ref, self.send.at[i, chip, WAYS.index(way)], sems.at[i, chip],
            device_id=me.to(way), device_id_type=MESH)

    def core_receipt(self, part, chip):
        i = NAMES.index(part)
        me = self.me
        ref = self.block(part, chip, 1 - me.c)
        return pltpu.make_async_remote_copy(
            ref, ref, self.send.at[i, chip, 4], self.crecv.at[i, chip],
            device_id=me.to("core"), device_id_type=MESH)

    def onward(self, part, chip, axes):
        me = self.me
        for axis in axes:
            if axis == "z":
                pl.when(me.z < 3)(lambda: self.copy(part, chip, "up").start())
                pl.when(me.z > 0)(lambda: self.copy(part, chip, "down").start())
            else:
                self.copy(part, chip, axis).start()

    def own(self, part):
        me = self.me
        chip = self.chip(me.x, me.y, me.z)
        self.onward(part, chip, ORDER[part])
        self.copy(part, chip, "core").start()

    def origins(self, fx, fy, k, act):
        me = self.me
        x = 1 - me.x if fx else me.x
        y = 1 - me.y if fy else me.y
        if k == 0:
            act(self.chip(x, y, me.z), 0)
        else:
            pl.when(me.z >= k)(lambda: act(self.chip(x, y, me.z - k), -1))
            pl.when(me.z + k <= 3)(lambda: act(self.chip(x, y, me.z + k), 1))

    def arrival(self, part, fx, fy, k):
        moved = {"x": fx, "y": fy, "z": k}
        return max(i for i in range(3) if moved[ORDER[part][i]])

    def serve(self, part, fx, fy, k):
        me = self.me
        order = ORDER[part]
        stage = self.arrival(part, fx, fy, k)
        axis = order[stage]

        def act(chip, sign):
            if axis == "z":
                way, more = ("up", me.z < 3) if sign < 0 else ("down", me.z > 0)
                self.copy(part, chip, way).wait_recv()
                pl.when(more)(lambda: self.copy(part, chip, way).start())
            else:
                self.copy(part, chip, axis).wait_recv()
            self.onward(part, chip, order[stage + 1:])
            self.copy(part, chip, "core").start()

        self.origins(fx, fy, k, act)

    def arrived(self, part):
        def body(chip, _):
            self.core_receipt(part, chip).wait_recv()
            return 0
        lax.fori_loop(0, 16, body, 0)

    def drain(self, part):
        me = self.me
        order = ORDER[part]

        def body(chip, _):
            self.copy(part, chip, "core").wait_send()
            return 0
        lax.fori_loop(0, 16, body, 0)

        def sent(chip, axes, sign):
            for axis in axes:
                if axis == "z":
                    if sign <= 0:
                        pl.when(me.z < 3)(lambda: self.copy(part, chip, "up").wait_send())
                    if sign >= 0:
                        pl.when(me.z > 0)(lambda: self.copy(part, chip, "down").wait_send())
                else:
                    self.copy(part, chip, axis).wait_send()

        for fx in (0, 1):
            for fy in (0, 1):
                for k in range(4):
                    if fx + fy + k == 0:
                        sent(self.chip(me.x, me.y, me.z), order, 0)
                        continue
                    stage = self.arrival(part, fx, fy, k)
                    axes = order[stage:] if order[stage] == "z" else order[stage + 1:]
                    self.origins(fx, fy, k, lambda chip, sign: sent(
                        chip, axes, sign if order[stage] == "z" else 0))


def relayout(me, flats, wide, refs, part_list=("qkv", "out", "up", "down")):
    wqkv, wo, wu, wd, sm = refs
    chip = (me.z * 2 + me.x) * 2 + me.y
    m = pl.multiple_of
    for name, ref, base, rows, tiles in (
        ("qkv", wqkv, 0, 24, 18), ("out", wo, 432, 24, 6), ("up", wu, 576, 24, 24), ("down", wd, 1152, 96, 6)):
        half = tiles // 2
        for j in range(half):
            both = [wide[d, pl.ds(base + me.c * half + j, rows, stride=tiles), :] for d in range(2)]
            column = m(me.c * half * 128 + j * 128, 128)
            ref[pl.ds(m(chip * 2 * rows, 16), 2 * rows), pl.ds(column, 128)] = (
                jnp.concatenate(both, 0).astype(BF))


def sequence():
    steps = []
    for i, p in enumerate(NAMES):
        for fx in (0, 1):
            for fy in (0, 1):
                for k in range(4):
                    if fx + fy + k:
                        steps.append(((fx + fy + k, i), p, fx, fy, k))
    steps.sort()
    return [s[1:] for s in steps]


def gather_kernel(flat, wqkv_o, wo_o, wu_o, wd_o, sm_o, flats, wide, wqkv, wo, wu, wd, sm, fsend, frecv, send, recv, crecv, osem):
    me = Place()
    enter(me)
    refs = (wqkv, wo, wu, wd, sm)
    g = Gather(me, refs, send, recv, crecv)
    swap = pltpu.make_async_remote_copy(flat, flats.at[1], fsend, frecv, device_id=me.to("core"), device_id_type=MESH)
    swap.start()
    chip = (me.z * 2 + me.x) * 2 + me.y
    sm[pl.ds(pl.multiple_of((chip * 2 + me.c) * 16, 16), 16), :] = flat[1728:1744, :]
    g.own("small")
    wide[me.c] = flat[...].astype(F32)
    swap.wait()
    wide[1 - me.c] = flats[1].astype(F32)
    relayout(me, flats, wide, refs)
    for p in NAMES[1:]:
        g.own(p)
    for p, fx, fy, k in sequence():
        g.serve(p, fx, fy, k)
    for p in NAMES:
        g.arrived(p)
    outs = [pltpu.make_async_copy(a, b, osem.at[i]) for i, (a, b) in enumerate(zip(refs, (wqkv_o, wo_o, wu_o, wd_o, sm_o)))]
    for o in outs: o.start()
    for p in NAMES: g.drain(p)
    for o in outs: o.wait()


def gather_call(flat):
    anyspec = pl.BlockSpec(memory_space=pl.ANY)
    v = pl.BlockSpec(memory_space=pltpu.VMEM)
    n = len(PARTS)
    shapes = [(768, 2304), (768, 768), (768, 3072), (3072, 768), (512, 128)]
    return pl.pallas_call(
        gather_kernel,
        out_shape=[jax.ShapeDtypeStruct(s, BF) for s in shapes],
        in_specs=[v],
        out_specs=[anyspec] * 5,
        scratch_shapes=[pltpu.VMEM((2, TOTAL, 128), BF), pltpu.VMEM((2, TOTAL, 128), F32)]
        + [pltpu.VMEM(s, BF) for s in shapes]
        + [pltpu.SemaphoreType.DMA, pltpu.SemaphoreType.DMA,
           pltpu.SemaphoreType.DMA((n, 16, 5)), pltpu.SemaphoreType.DMA((n, 16)), pltpu.SemaphoreType.DMA((n, 16)),
           pltpu.SemaphoreType.DMA((5,))],
        compiler_params=pltpu.CompilerParams(collective_id=1, has_side_effects=True, vmem_limit_bytes=60 << 20),
        name="gather",
    )(flat)


RPARTS = (
    ("down0", 3, "xzy", 96, 0, 0, 384),
    ("down1", 3, "yzx", 96, 96, 0, 384),
    ("up0", 2, "xzy", 48, 0, 0, 768),
    ("up1", 2, "yzx", 48, 0, 768, 768),
    ("out", 1, "zxy", 48, 0, 0, 384),
    ("qkv0", 0, "zxy", 48, 0, 0, 640),
    ("qkv1", 0, "zyx", 48, 0, 640, 512),
)
HALF = (1152, 384, 1536, 384)
CHIPROWS = (48, 48, 48, 192)
MATS = ((768, 2304), (768, 768), (768, 3072), (3072, 768))
SIZES = {"x": 2, "y": 2, "z": 4}


def slots(order, axis):
    n = 4 if axis == "z" else 1
    for a in order[: order.index(axis)]:
        n *= SIZES[a]
    return n


def landing_shapes():
    shapes = []
    for name, mat, order, rows, ro, co, cols in RPARTS:
        for way in ("up", "down", "x", "y"):
            axis = "z" if way in ("up", "down") else way
            shapes.append(pltpu.VMEM((slots(order, axis), rows, cols), BF))
    return shapes


class Scatter:
    def __init__(self, me, grads, half, lands, finals, send, recv):
        self.me, self.grads, self.half, self.lands, self.finals = me, grads, half, lands, finals
        self.send, self.recv = send, recv

    def chip(self, x, y, z):
        return (z * 2 + x) * 2 + y

    def cols(self, i, c):
        name, mat, order, rows, ro, co, cols = RPARTS[i]
        return pl.ds(pl.multiple_of(c * HALF[mat] + co, 128), cols)

    def block(self, i, dest):
        name, mat, order, rows, ro, co, cols = RPARTS[i]
        chip = self.chip(*dest)
        return self.grads[mat].at[pl.ds(pl.multiple_of(chip * CHIPROWS[mat] + ro, 16), rows), self.cols(i, self.me.c)]

    def slot(self, i, way, dest):
        order = RPARTS[i][2]
        axis = "z" if way in ("up", "down") else way
        coords = dict(zip("xyz", dest))
        index = coords["z"] if axis == "z" else 0
        for a in order[: order.index(axis)]:
            index = index * SIZES[a] + coords[a]
        return index

    def land(self, i, way, dest):
        return self.lands[i * 4 + ("up", "down", "x", "y").index(way)].at[self.slot(i, way, dest)]

    def copy(self, i, way, dest):
        w = ("up", "down", "x", "y").index(way)
        chip = self.chip(*dest)
        return pltpu.make_async_remote_copy(
            self.block(i, dest), self.land(i, way, dest), self.send.at[i, chip], self.recv.at[i, w, chip],
            device_id=self.me.to(way), device_id_type=MESH)

    def stage(self, i, fx, fy, k):
        moved = {"x": fx, "y": fy, "z": k}
        return max(s for s in range(3) if moved[RPARTS[i][2][s]])

    def take(self, i, way, dest):
        self.copy(i, way, dest).wait_recv()
        ref = self.block(i, dest)
        ref[...] = (ref[...].astype(F32) + self.land(i, way, dest)[...].astype(F32)).astype(BF)

    def serve(self, i, fx, fy, k):
        me = self.me
        order = RPARTS[i][2]
        stage = self.stage(i, fx, fy, k)
        axis = order[stage]

        def act(dest, sign):
            if axis == "z":
                if sign < 0:
                    way, more = "down", me.z < 3
                else:
                    way, more = "up", me.z > 0
                pl.when(more)(lambda: self.take(i, way, dest))
            else:
                way = axis
            self.gather_in(i, order[stage + 1:], dest)
            self.copy(i, way, dest).start()

        self.dests(fx, fy, k, act)

    def gather_in(self, i, axes, dest):
        me = self.me
        for a in axes:
            if a == "z":
                pl.when(me.z < 3)(lambda: self.take(i, "down", dest))
                pl.when(me.z > 0)(lambda: self.take(i, "up", dest))
            else:
                self.take(i, a, dest)

    def dests(self, fx, fy, k, act):
        me = self.me
        x = 1 - me.x if fx else me.x
        y = 1 - me.y if fy else me.y
        if k == 0:
            act((x, y, me.z), 0)
        else:
            pl.when(me.z >= k)(lambda: act((x, y, me.z - k), -1))
            pl.when(me.z + k <= 3)(lambda: act((x, y, me.z + k), 1))

    def finish(self, i):
        name, mat, order, rows, ro, co, cols = RPARTS[i]
        me = self.me
        dest = (me.x, me.y, me.z)
        fin = self.finals[mat].at[pl.ds(ro, rows), pl.ds(co, cols)]
        fin[...] = self.block(i, dest)[...].astype(F32)
        for axis in order:
            if axis == "z":
                for way, more in (("down", me.z < 3), ("up", me.z > 0)):
                    @pl.when(more)
                    def _():
                        self.copy(i, way, dest).wait_recv()
                        fin[...] += self.land(i, way, dest)[...].astype(F32)
            else:
                self.copy(i, axis, dest).wait_recv()
                fin[...] += self.land(i, axis, dest)[...].astype(F32)

    def drain(self, i):
        me = self.me
        for fx in (0, 1):
            for fy in (0, 1):
                for k in range(4):
                    if fx + fy + k:
                        axis = RPARTS[i][2][self.stage(i, fx, fy, k)]
                        self.dests(fx, fy, k, lambda dest, sign: self.copy(
                            i, axis if axis != "z" else ("down" if sign < 0 else "up"), dest).wait_send())

    def swap(self, i, csend, crecv):
        name, mat, order, rows, ro, co, cols = RPARTS[i]
        if mat == 3:
            src = self.grads[3].at[:, pl.ds(pl.multiple_of((1 - self.me.c) * 384, 128), 384)]
            dst = self.half[3]
        else:
            src = self.grads[mat].at[:, self.cols(i, 1 - self.me.c)]
            dst = self.half[mat].at[:, pl.ds(co, cols)]
        return pltpu.make_async_remote_copy(src, dst, csend.at[i], crecv.at[i], device_id=self.me.to("core"), device_id_type=MESH)

    def merge(self, i):
        name, mat, order, rows, ro, co, cols = RPARTS[i]
        n = MATS[mat][0]
        if mat == 3:
            ref, src = self.grads[3].at[:, pl.ds(pl.multiple_of(self.me.c * 384, 128), 384)], self.half[3]
        else:
            ref, src = self.grads[mat].at[:, self.cols(i, self.me.c)], self.half[mat].at[:, pl.ds(co, cols)]

        def body(r, _):
            rr = pl.ds(pl.multiple_of(r * 32, 32), 32)
            ref[rr, :] = (ref[rr, :].astype(F32) + src[rr, :].astype(F32)).astype(BF)
            return 0
        lax.fori_loop(0, n // 32, body, 0)


def order_of_service(parts):
    steps = []
    for i in parts:
        for fx in (0, 1):
            for fy in (0, 1):
                for k in range(4):
                    if fx + fy + k:
                        steps.append(((-(fx + fy + k), i), i, fx, fy, k))
    steps.sort()
    return [s[1:] for s in steps]


FLATROWS = ((24, 18, 432), (24, 6, 144), (24, 24, 576), (96, 6, 576))


def last_swap(me, finals, sides, fsend, frecv):
    copies = []
    for mat in range(4):
        rows = FLATROWS[mat][0]
        src = finals[mat].at[pl.ds(pl.multiple_of((1 - me.c) * rows, 8), rows), :]
        copies.append(pltpu.make_async_remote_copy(src, sides[mat], fsend.at[mat], frecv.at[mat], device_id=me.to("core"), device_id_type=MESH))
    return copies


def flatten(me, mat, finals, sides, out):
    rows, tiles, lines = FLATROWS[mat]
    half = tiles // 2
    for j in range(half):
        mine = finals[mat][pl.ds(pl.multiple_of(me.c * rows, 8), rows), pl.ds(j * 128, 128)]
        out[pl.ds(me.c * half + j, rows, stride=tiles), :] = mine
        out[pl.ds((1 - me.c) * half + j, rows, stride=tiles), :] = sides[mat][:, pl.ds(j * 128, 128)]


def scatter_kernel(gq, go, gu, gd, oq, oo, ou, od, *rest):
    lands, rest = rest[:28], rest[28:]
    grads, rest = rest[:4], rest[4:]
    half, rest = rest[:4], rest[4:]
    finals, rest = rest[:4], rest[4:]
    sides, rest = rest[:4], rest[4:]
    isem, csend, crecv, send, recv, fsend, frecv = rest
    me = Place()
    ins = [pltpu.make_async_copy(a, b, isem.at[i]) for i, (a, b) in enumerate(zip((gq, go, gu, gd), grads))]
    for i in (3, 2, 1, 0): ins[i].start()
    enter(me)
    s = Scatter(me, grads, half, lands, finals, send, recv)
    loaded = set()
    swaps = [i for i in range(7) if i != 1]
    for i in swaps:
        mat = RPARTS[i][1]
        if mat not in loaded:
            ins[mat].wait()
            loaded.add(mat)
        s.swap(i, csend, crecv).start()
    for i in swaps:
        s.swap(i, csend, crecv).wait_recv()
        s.merge(i)
        for j in ((0, 1) if i == 0 else (i,)):
            for st in order_of_service((j,)):
                if st[1] + st[2] + st[3] == 5:
                    s.serve(*st)
    for st in order_of_service(range(7)):
        if st[1] + st[2] + st[3] < 5:
            s.serve(*st)
    for i in range(7):
        s.finish(i)
    fs = last_swap(me, finals, sides, fsend, frecv)
    for f in fs: f.start()
    for i in range(7): s.drain(i)
    for i in swaps: s.swap(i, csend, crecv).wait_send()
    for mat, f in enumerate(fs):
        f.wait()
        flatten(me, mat, finals, sides, (oq, oo, ou, od)[mat])


def scatter_call(gq, go, gu, gd):
    a = pl.BlockSpec(memory_space=pl.ANY)
    v = pl.BlockSpec(memory_space=pltpu.VMEM)
    return pl.pallas_call(
        scatter_kernel,
        out_shape=[jax.ShapeDtypeStruct((FLATROWS[m][2], 128), F32) for m in range(4)],
        in_specs=[a] * 4,
        out_specs=[v] * 4,
        scratch_shapes=landing_shapes()
        + [pltpu.VMEM(m, BF) for m in MATS]
        + [pltpu.VMEM((MATS[m][0], HALF[m]), BF) for m in range(4)]
        + [pltpu.VMEM((CHIPROWS[m], HALF[m]), F32) for m in range(4)]
        + [pltpu.VMEM((FLATROWS[m][0], HALF[m]), F32) for m in range(4)]
        + [pltpu.SemaphoreType.DMA((4,)), pltpu.SemaphoreType.DMA((7,)), pltpu.SemaphoreType.DMA((7,)),
           pltpu.SemaphoreType.DMA((7, 16)), pltpu.SemaphoreType.DMA((7, 4, 16)),
           pltpu.SemaphoreType.DMA((4,)), pltpu.SemaphoreType.DMA((4,))],
        compiler_params=pltpu.CompilerParams(collective_id=2, has_side_effects=True, vmem_limit_bytes=62 << 20),
        name="scatter",
    )(gq, go, gu, gd)


HEADS = 12
HD = 64
epsilon = 1e-05
masked_score = -1000000000.0
score_scale = 0.125


def matmul(left, right):
    return jnp.dot(left, right, preferred_element_type=jnp.float32)


def matmul_back(left, right):
    return lax.dot_general(
        left, right, (((1,), (1,)), ((), ())), preferred_element_type=jnp.float32
    )


def outer_sum(left, right):
    return lax.dot_general(
        left, right, (((0,), (0,)), ((), ())), preferred_element_type=jnp.float32
    )


def normalize(hidden, gain, shift):
    centre = jnp.mean(hidden, -1, keepdims=True)
    centred = hidden - centre
    variance = jnp.mean(centred * centred, -1, keepdims=True)
    return centred * lax.rsqrt(variance + epsilon) * gain + shift


def gelu_exact(value):
    return jax.nn.gelu(value, approximate=False)


AXES = ("outer", "inner", "seq")
SMALLS = (1, 2, 4, 5, 6, 8, 10, 11, 12)


def to_part(flat):
    inner = lax.axis_size("inner")
    if inner == 1:
        return flat
    every = lax.all_gather(flat, ("inner", "seq"), axis=0, tiled=True)
    size = flat.shape[0] * inner
    return lax.dynamic_slice_in_dim(every, lax.axis_index("seq") * size, size, 0)


def whole_scatter(part):
    inner = lax.axis_size("inner")
    if inner == 1:
        return part
    every = lax.psum(lax.all_gather(part, "seq", axis=0, tiled=True), "inner")
    size = part.shape[0] // inner
    index = lax.axis_index("inner") * lax.axis_size("seq") + lax.axis_index("seq")
    return lax.dynamic_slice_in_dim(every, index * size, size, 0)


def whole_weights(params):
    parts = [to_part(p) for p in params]
    small = jnp.concatenate([parts[i] for i in SMALLS])
    used = small.shape[0]
    small = jnp.pad(small, (0, 16 * 128 - used))
    flat = jnp.concatenate(
        [parts[i].reshape(-1, 128) for i in (0, 3, 7, 9)] + [small.reshape(16, 128)], 0
    )
    wqkv, wo, wu, wd, sm = gather_call(flat)
    sm = sm.reshape(32, 16 * 128).astype(F32)
    vectors = []
    at = 0
    for i in SMALLS:
        size = parts[i].shape[0]
        vectors.append(sm[:, at : at + size].reshape(-1))
        at += size
    q, v, ob, g1, b1, ub, db, g2, b2 = vectors
    return (wqkv, q, v, wo, ob, g1, b1, wu, ub, wd, db, g2, b2)


def small_sums(vectors):
    total = lax.psum(jnp.concatenate(vectors), AXES)
    index = lax.axis_index(AXES)
    shares = []
    at = 0
    for v in vectors:
        size = v.shape[0] // lax.axis_size(AXES)
        shares.append(lax.dynamic_slice_in_dim(total, at + index * size, size, 0))
        at += v.shape[0]
    return shares


def project(rows, weights, groups):
    qkv = matmul(rows, weights[0])
    queries = (qkv[:, :D] + weights[1]).astype(jnp.bfloat16)
    keys = qkv[:, D : 2 * D].astype(jnp.bfloat16)
    values = (qkv[:, 2 * D :] + weights[2]).astype(jnp.bfloat16)
    return (
        queries.reshape(groups, -1, D),
        keys.reshape(groups, -1, D),
        values.reshape(groups, -1, D),
    )


def head_block(array, index):
    return array[:, :, index * 2 * HD : (index + 1) * 2 * HD].reshape(
        array.shape[0], array.shape[1], 2, HD
    )


def pair_scores(query_pair, key_pair, allowed):
    scores = (
        jnp.einsum("sihd,sjhd->shij", query_pair, key_pair, preferred_element_type=jnp.float32)
        * score_scale
    )
    return jnp.where(allowed[:, None], scores, masked_score)


def attend_forward(queries, keys_all, values_all, allowed):
    groups, block, _ = queries.shape
    pieces = []
    logsums = []
    for index in range(HEADS // 2):
        query_pair = head_block(queries, index)
        scores = pair_scores(query_pair, head_block(keys_all, index), allowed)
        peak = jnp.max(scores, -1, keepdims=True)
        expd = jnp.exp(scores - peak)
        total = jnp.sum(expd, -1, keepdims=True)
        probs_low = (expd / total).astype(jnp.bfloat16)
        result = jnp.einsum(
            "shij,sjhd->sihd",
            probs_low,
            head_block(values_all, index),
            preferred_element_type=jnp.float32,
        )
        pieces.append(result.reshape(groups, block, 2 * HD))
        logsums.append(peak + jnp.log(total))
    return (jnp.concatenate(pieces, -1).astype(jnp.bfloat16), logsums)


def attend_backward(queries, keys_all, values_all, allowed, logsums, grad_attended):
    groups, block, _ = queries.shape
    length = keys_all.shape[1]
    query_terms, key_terms, value_terms = ([], [], [])
    for index in range(HEADS // 2):
        query_pair = head_block(queries, index)
        key_pair = head_block(keys_all, index)
        value_pair = head_block(values_all, index)
        grad_pair = head_block(grad_attended, index)
        scores = pair_scores(query_pair, key_pair, allowed)
        probs = jnp.exp(scores - logsums[index])
        probs_low = probs.astype(jnp.bfloat16)
        grad_probs = jnp.einsum(
            "sihd,sjhd->shij", grad_pair, value_pair, preferred_element_type=jnp.float32
        )
        inner = jnp.sum(probs * grad_probs, -1, keepdims=True)
        grad_scores = (probs * (grad_probs - inner)).astype(jnp.bfloat16)
        query_terms.append(
            (
                jnp.einsum(
                    "shij,sjhd->sihd", grad_scores, key_pair, preferred_element_type=jnp.float32
                )
                * score_scale
            ).reshape(groups, block, 2 * HD)
        )
        key_terms.append(
            (
                jnp.einsum(
                    "shij,sihd->sjhd", grad_scores, query_pair, preferred_element_type=jnp.float32
                )
                * score_scale
            ).reshape(groups, length, 2 * HD)
        )
        value_terms.append(
            jnp.einsum(
                "shij,sihd->sjhd", probs_low, grad_pair, preferred_element_type=jnp.float32
            ).reshape(groups, length, 2 * HD)
        )
    return (
        jnp.concatenate(query_terms, -1),
        jnp.concatenate(key_terms, -1),
        jnp.concatenate(value_terms, -1),
    )


def dense_forward(rows_wide, attended, weights):
    attn_out = matmul(attended, weights[3]) + weights[4]
    first_sum = rows_wide + attn_out
    normed = normalize(first_sum, weights[5], weights[6])
    normed_low = normed.astype(jnp.bfloat16)
    before = matmul(normed_low, weights[7]) + weights[8]
    activated = gelu_exact(before).astype(jnp.bfloat16)
    branch = matmul(activated, weights[9]) + weights[10]
    second_sum = normed + branch
    final = normalize(second_sum, weights[11], weights[12])
    return (first_sum, normed, normed_low, before, activated, second_sum, final)


def shards(
    inputs,
    qkv_weight,
    q_bias,
    v_bias,
    out_weight,
    out_bias,
    norm1_gain,
    norm1_bias,
    up_weight,
    up_bias,
    down_weight,
    down_bias,
    norm2_gain,
    norm2_bias,
    cotangent,
    segment_ids,
    pad_mask,
    keep_flag,
):
    groups, block, width = inputs.shape
    rows = inputs.reshape(groups * block, width)
    rows_wide = rows.astype(jnp.float32)
    params = (
        qkv_weight,
        q_bias,
        v_bias,
        out_weight,
        out_bias,
        norm1_gain,
        norm1_bias,
        up_weight,
        up_bias,
        down_weight,
        down_bias,
        norm2_gain,
        norm2_bias,
    )
    start = lax.axis_index("seq") * block
    query_segments = lax.dynamic_slice_in_dim(segment_ids, start, block, 1)
    allowed = (query_segments[:, :, None] == segment_ids[:, None, :]) & (pad_mask[:, None, :] > 0)
    keep_rows = jnp.broadcast_to(keep_flag[:, None] > 0, (groups, block)).reshape(groups * block, 1)
    weights = whole_weights(params)
    queries, keys, values = project(rows, weights, groups)
    keys_all, values_all = (
        lax.all_gather(keys, "seq", axis=1, tiled=True),
        lax.all_gather(values, "seq", axis=1, tiled=True),
    )
    attended, logsums = attend_forward(queries, keys_all, values_all, allowed)
    attended_rows = attended.reshape(groups * block, width)
    first_sum, normed, normed_low, before, activated, second_sum, final = dense_forward(
        rows_wide, attended_rows, weights
    )
    outputs = (
        jnp.where(keep_rows, final, rows_wide).astype(jnp.bfloat16).reshape(groups, block, width)
    )
    cot_wide = cotangent.reshape(groups * block, width).astype(jnp.float32)
    grad_final = jnp.where(keep_rows, cot_wide, 0.0)
    _, second_pull = jax.vjp(normalize, second_sum, weights[11], weights[12])
    grad_second, grad_gain_two, grad_shift_two = second_pull(grad_final)
    grad_branch = grad_second.astype(jnp.bfloat16)
    grad_down = outer_sum(activated, grad_branch)
    grad_down_shift = jnp.sum(grad_branch.astype(jnp.float32), 0)
    grad_activated = matmul_back(grad_branch, weights[9]).astype(jnp.bfloat16)
    _, gelu_pull = jax.vjp(gelu_exact, before)
    grad_before = gelu_pull(grad_activated.astype(jnp.float32))[0].astype(jnp.bfloat16)
    grad_up = outer_sum(normed_low, grad_before)
    grad_up_shift = jnp.sum(grad_before.astype(jnp.float32), 0)
    grad_normed = grad_second + matmul_back(grad_before, weights[7])
    _, first_pull = jax.vjp(normalize, first_sum, weights[5], weights[6])
    grad_first, grad_gain_one, grad_shift_one = first_pull(grad_normed)
    grad_attn = grad_first.astype(jnp.bfloat16)
    grad_out = outer_sum(attended_rows, grad_attn)
    grad_out_shift = jnp.sum(grad_attn.astype(jnp.float32), 0)
    grad_attended = (
        matmul_back(grad_attn, weights[3]).astype(jnp.bfloat16).reshape(groups, block, width)
    )
    query_terms, key_terms, value_terms = attend_backward(
        queries, keys_all, values_all, allowed, logsums, grad_attended
    )
    key_sums, value_sums = (
        lax.psum_scatter(
            key_terms.astype(jnp.bfloat16), "seq", scatter_dimension=1, tiled=True
        ).astype(jnp.float32),
        lax.psum_scatter(
            value_terms.astype(jnp.bfloat16), "seq", scatter_dimension=1, tiled=True
        ).astype(jnp.float32),
    )
    grad_queries = query_terms.astype(jnp.bfloat16).reshape(groups * block, width)
    grad_keys = key_sums.astype(jnp.bfloat16).reshape(groups * block, width)
    grad_values = value_sums.astype(jnp.bfloat16).reshape(groups * block, width)
    grad_qkv = jnp.concatenate([grad_queries, grad_keys, grad_values], -1)
    grad_qkv_full = outer_sum(rows, grad_qkv)
    grad_query_shift = jnp.sum(grad_queries.astype(jnp.float32), 0)
    grad_value_shift = jnp.sum(grad_values.astype(jnp.float32), 0)
    grad_rows = grad_first + matmul_back(grad_qkv, weights[0])
    input_grad = (
        jnp.where(keep_rows, grad_rows, cot_wide).astype(jnp.bfloat16).reshape(groups, block, width)
    )
    big = scatter_call(
        grad_qkv_full.astype(BF), grad_out.astype(BF), grad_up.astype(BF), grad_down.astype(BF)
    )
    big = [whole_scatter(part.reshape(-1)) for part in big]
    small = small_sums(
        (grad_query_shift, grad_value_shift, grad_out_shift, grad_gain_one, grad_shift_one,
         grad_up_shift, grad_down_shift, grad_gain_two, grad_shift_two)
    )
    reduced = (
        big[0], small[0], small[1], big[1], small[2], small[3], small[4], big[2], small[5],
        big[3], small[6], small[7], small[8],
    )
    return (
        outputs,
        input_grad,
        reduced[0],
        reduced[1],
        reduced[2],
        reduced[3],
        reduced[4],
        reduced[5],
        reduced[6],
        reduced[7],
        reduced[8],
        reduced[9],
        reduced[10],
        reduced[11],
        reduced[12],
    )


def solution(mesh):
    fsdp, seq = mesh.shape["fsdp"], mesh.shape["seq"]
    mesh = Mesh(mesh.devices.reshape(8, fsdp // 8, seq), AXES)
    tokens = P(("outer", "inner"), "seq", None)
    flat = P(AXES)
    rows = P(("outer", "inner"), None)
    return jax.shard_map(
        shards,
        mesh=mesh,
        in_specs=(tokens,) + (flat,) * 13 + (tokens, rows, rows, P(("outer", "inner"))),
        out_specs=(tokens, tokens) + (flat,) * 13,
        check_vma=False,
    )
```

```python
import functools
import jax
import jax.numpy as jnp
from jax import lax
from jax.experimental import pallas as pl
from jax.experimental.pallas import tpu as pltpu
from jax.sharding import Mesh, PartitionSpec as P

MESH = pl.DeviceIdType.MESH
D = 768
FF = 3072
BF = jnp.bfloat16
F32 = jnp.float32
LINES = (432, 144, 576, 576, 16)
BASE = (0, 432, 576, 1152, 1728)
TOTAL = 1744


class Place:
    def __init__(self):
        o = lax.axis_index("outer")
        s = lax.axis_index("seq")
        self.z, self.x, self.y, self.c = o // 2, o % 2, s // 2, s % 2

    def to(self, way):
        z, x, y, c = self.z, self.x, self.y, self.c
        return {
            "up": {"outer": (z + 1) * 2 + x},
            "down": {"outer": (z - 1) * 2 + x},
            "x": {"outer": z * 2 + 1 - x},
            "y": {"seq": (1 - y) * 2 + c},
            "core": {"seq": y * 2 + 1 - c},
            "far": {"outer": (3 - z) * 2 + x},
        }[way]


def enter(me):
    bar = pltpu.get_barrier_semaphore()

    def greet(to):
        pl.semaphore_signal(bar, 1, device_id=to, device_id_type=MESH)

    for way in ("x", "y", "core"):
        greet(me.to(way))
    pl.when(me.z < 3)(lambda: greet(me.to("up")))
    pl.when(me.z > 0)(lambda: greet(me.to("down")))
    pl.when((me.z == 0) | (me.z == 3))(lambda: greet(me.to("far")))
    pl.semaphore_wait(bar, 5)


WAYS = ("up", "down", "x", "y", "core")

PARTS = (
    ("small", "zxy"),
    ("qkv0", "zxy"),
    ("qkv1", "zyx"),
    ("out", "zxy"),
    ("up0", "xzy"),
    ("up1", "yzx"),
    ("down0", "xzy"),
    ("down1", "yzx"),
)
NAMES = [p[0] for p in PARTS]
ORDER = dict(PARTS)


class Gather:
    def __init__(self, me, refs, send, recv, crecv):
        self.me = me
        self.refs = refs
        self.send, self.recv, self.crecv = send, recv, crecv

    def block(self, part, chip, c):
        wqkv, wo, wu, wd, sm = self.refs
        m = pl.multiple_of
        if part == "small":
            return sm.at[pl.ds(m((chip * 2 + c) * 16, 16), 16), :]
        if part == "qkv0":
            return wqkv.at[pl.ds(m(chip * 48, 16), 48), pl.ds(m(c * 1152, 128), 640)]
        if part == "qkv1":
            return wqkv.at[pl.ds(m(chip * 48, 16), 48), pl.ds(m(c * 1152 + 640, 128), 512)]
        if part == "out":
            return wo.at[pl.ds(m(chip * 48, 16), 48), pl.ds(m(c * 384, 128), 384)]
        if part == "up0":
            return wu.at[pl.ds(m(chip * 48, 16), 48), pl.ds(m(c * 1536, 128), 768)]
        if part == "up1":
            return wu.at[pl.ds(m(chip * 48, 16), 48), pl.ds(m(c * 1536 + 768, 128), 768)]
        if part == "down0":
            return wd.at[pl.ds(m(chip * 192, 16), 96), pl.ds(m(c * 384, 128), 384)]
        if part == "down1":
            return wd.at[pl.ds(m(chip * 192 + 96, 16), 96), pl.ds(m(c * 384, 128), 384)]

    def chip(self, x, y, z):
        return (z * 2 + x) * 2 + y

    def copy(self, part, chip, way, arrival=None):
        i = NAMES.index(part)
        me = self.me
        ref = self.block(part, chip, me.c)
        sems = self.crecv if way == "core" else self.recv
        return pltpu.make_async_remote_copy(
            ref, ref, self.send.at[i, chip, WAYS.index(way)], sems.at[i, chip],
            device_id=me.to(way), device_id_type=MESH)

    def core_receipt(self, part, chip):
        i = NAMES.index(part)
        me = self.me
        ref = self.block(part, chip, 1 - me.c)
        return pltpu.make_async_remote_copy(
            ref, ref, self.send.at[i, chip, 4], self.crecv.at[i, chip],
            device_id=me.to("core"), device_id_type=MESH)

    def onward(self, part, chip, axes):
        me = self.me
        for axis in axes:
            if axis == "z":
                pl.when(me.z < 3)(lambda: self.copy(part, chip, "up").start())
                pl.when(me.z > 0)(lambda: self.copy(part, chip, "down").start())
            else:
                self.copy(part, chip, axis).start()

    def own(self, part):
        me = self.me
        chip = self.chip(me.x, me.y, me.z)
        self.onward(part, chip, ORDER[part])
        self.copy(part, chip, "core").start()

    def origins(self, fx, fy, k, act):
        me = self.me
        x = 1 - me.x if fx else me.x
        y = 1 - me.y if fy else me.y
        if k == 0:
            act(self.chip(x, y, me.z), 0)
        else:
            pl.when(me.z >= k)(lambda: act(self.chip(x, y, me.z - k), -1))
            pl.when(me.z + k <= 3)(lambda: act(self.chip(x, y, me.z + k), 1))

    def arrival(self, part, fx, fy, k):
        moved = {"x": fx, "y": fy, "z": k}
        return max(i for i in range(3) if moved[ORDER[part][i]])

    def serve(self, part, fx, fy, k):
        me = self.me
        order = ORDER[part]
        stage = self.arrival(part, fx, fy, k)
        axis = order[stage]

        def act(chip, sign):
            if axis == "z":
                way, more = ("up", me.z < 3) if sign < 0 else ("down", me.z > 0)
                self.copy(part, chip, way).wait_recv()
                pl.when(more)(lambda: self.copy(part, chip, way).start())
            else:
                self.copy(part, chip, axis).wait_recv()
            self.onward(part, chip, order[stage + 1:])
            self.copy(part, chip, "core").start()

        self.origins(fx, fy, k, act)

    def arrived(self, part):
        def body(chip, _):
            self.core_receipt(part, chip).wait_recv()
            return 0
        lax.fori_loop(0, 16, body, 0)

    def drain(self, part):
        me = self.me
        order = ORDER[part]

        def body(chip, _):
            self.copy(part, chip, "core").wait_send()
            return 0
        lax.fori_loop(0, 16, body, 0)

        def sent(chip, axes, sign):
            for axis in axes:
                if axis == "z":
                    if sign <= 0:
                        pl.when(me.z < 3)(lambda: self.copy(part, chip, "up").wait_send())
                    if sign >= 0:
                        pl.when(me.z > 0)(lambda: self.copy(part, chip, "down").wait_send())
                else:
                    self.copy(part, chip, axis).wait_send()

        for fx in (0, 1):
            for fy in (0, 1):
                for k in range(4):
                    if fx + fy + k == 0:
                        sent(self.chip(me.x, me.y, me.z), order, 0)
                        continue
                    stage = self.arrival(part, fx, fy, k)
                    axes = order[stage:] if order[stage] == "z" else order[stage + 1:]
                    self.origins(fx, fy, k, lambda chip, sign: sent(
                        chip, axes, sign if order[stage] == "z" else 0))


def relayout(me, wide, refs, mat):
    m = pl.multiple_of
    chip = (me.z * 2 + me.x) * 2 + me.y
    base, (rows, tiles) = BASE[mat], ((24, 18), (24, 6), (24, 24), (96, 6))[mat]
    half = tiles // 2
    for j in range(half):
        both = [wide[d, pl.ds(base + me.c * half + j, rows, stride=tiles), :] for d in range(2)]
        refs[mat][pl.ds(m(chip * 2 * rows, 16), 2 * rows), pl.ds(m((me.c * half + j) * 128, 128), 128)] = (
            jnp.concatenate(both, 0).astype(BF))


def sequence():
    steps = []
    for i, p in enumerate(NAMES):
        for fx in (0, 1):
            for fy in (0, 1):
                for k in range(4):
                    if fx + fy + k:
                        steps.append(((fx + fy + k, i), p, fx, fy, k))
    steps.sort()
    return [s[1:] for s in steps]


HEADS = 12
HD = 64
EPS = 1e-05
PAIRS = HEADS // 2
VECTORS = ("q", "v", "ob", "g1", "b1", "db", "g2", "b2", "ub")


def nt(left, right):
    return lax.dot_general(left, right, (((1,), (1,)), ((), ())), preferred_element_type=F32)


def nn(left, right):
    return jnp.dot(left, right, preferred_element_type=F32)


def tn(left, right):
    return lax.dot_general(left, right, (((0,), (0,)), ((), ())), preferred_element_type=F32)


def tile(i, size):
    return pl.ds(pl.multiple_of(i * size, size), size)


def spread(rows, size, width):
    lane = lax.broadcasted_iota(jnp.int32, (128, width), 0)
    col = lax.broadcasted_iota(jnp.int32, (128, width), 1)
    owner = ((col.astype(F32) + 0.5) * (1.0 / size)).astype(jnp.int32)
    pick = (col - owner * size == lane).astype(F32).astype(BF)
    every = nn(rows.astype(BF), pick)
    dev = lax.broadcasted_iota(jnp.int32, (32, width), 0)
    col = lax.broadcasted_iota(jnp.int32, (32, width), 1)
    owner = ((col.astype(F32) + 0.5) * (1.0 / size)).astype(jnp.int32)
    return jnp.sum(jnp.where(owner == dev, every, 0.0), 0, keepdims=True)


def swap_rows(me, ref, s, send, recv):
    width = 256

    def block(index):
        return ref.at[tile(index, width), :]

    def copy(index, way, n):
        return pltpu.make_async_remote_copy(
            block(index), block(index), send.at[n], recv.at[n], device_id=me.to(way), device_id_type=MESH)

    mine = me.y * 2 + me.c
    over = (1 - me.y) * 2 + me.c
    return (copy(mine, "core", 0), copy(mine, "y", 1), copy(over, "core", 2)), (
        copy(me.y * 2 + 1 - me.c, "core", 0), copy(over, "y", 1), copy((1 - me.y) * 2 + 1 - me.c, "core", 2))


def head_rows(array, axis):
    lane = lax.broadcasted_iota(jnp.int32, array.shape, 1)
    zero = jnp.zeros_like(array)
    return jnp.concatenate([jnp.where(lane < HD, array, zero), jnp.where(lane >= HD, array, zero)], axis)


def forward_kernel(
    fq, fo, fu, fd, fs, x, cot, seg, pad, keep,
    out, hq, ho, hu, hd, hxt, hv, hkt, he, hq8, hot, hr, hactt, hgp, hnlt, hn1, hr1, hgs, hsm,
    flats, wide, wqkv, wo, wu, wd, sm, smf, xall, kk, vv, kt, vt, st, ee, mask, vec, vecu, n2, xt, act, nl,
    fsend, frecv, send, recv, crecv, osem, xsend, xrecv, esem,
):
    me = Place()
    s = me.y * 2 + me.c
    enter(me)
    refs = (wqkv, wo, wu, wd, sm)
    g = Gather(me, refs, send, recv, crecv)
    swaps = [
        pltpu.make_async_remote_copy(
            src, flats.at[pl.ds(b, n), :], fsend.at[i], frecv.at[i], device_id=me.to("core"), device_id_type=MESH)
        for i, (src, b, n) in enumerate(zip((fq, fo, fu, fd), BASE, LINES))
    ]
    for c in swaps:
        c.start()
    chip = (me.z * 2 + me.x) * 2 + me.y
    sm[pl.ds(pl.multiple_of((chip * 2 + me.c) * 16, 16), 16), :] = fs[...]
    xall[tile(s, 256), :] = x[...]
    xs, xr = swap_rows(me, xall, s, xsend, xrecv)
    xs[0].start()
    xs[1].start()
    g.own("small")
    done = []
    for i, (src, b, n) in enumerate(zip((fq, fo, fu, fd), BASE, LINES)):
        wide[me.c, pl.ds(b, n), :] = src[...].astype(F32)
        swaps[i].wait_recv()
        wide[1 - me.c, pl.ds(b, n), :] = flats[pl.ds(b, n), :].astype(F32)
        relayout(me, wide, refs, i)
        for p in (("qkv0", "qkv1"), ("out",), ("up0", "up1"), ("down0", "down1"))[i]:
            g.own(p)

    codes = jnp.where(pad[...] > 0, seg[...], -1).astype(F32)
    mine = seg[:, tile(s, 256)].astype(F32)
    for j in range(8):
        column = jnp.broadcast_to(codes[:, j * 128:(j + 1) * 128], (128, 128)).T
        for i in range(2):
            row = jnp.broadcast_to(mine[:, i * 128:(i + 1) * 128], (128, 128))
            mask[pl.ds(j * 128, 128), pl.ds(i * 128, 128)] = jnp.where(column == row, 0.0, -1e9)

    steps = sequence()
    at = [0]

    def pump(n):
        for p, fx, fy, k in steps[at[0]:at[0] + n]:
            g.serve(p, fx, fy, k)
        at[0] += n

    def pump_through(parts):
        while any(q[0] in parts for q in steps[at[0]:]):
            pump(1)

    xr[1].wait_recv()
    xs[2].start()
    pump_through(("small", "qkv0", "qkv1"))
    for p in ("small", "qkv0", "qkv1"):
        g.arrived(p)
    xr[0].wait_recv()
    xr[2].wait_recv()
    outs = [pltpu.make_async_copy(wqkv, hq, osem.at[1])]
    outs[0].start()
    for j in range(4):
        xt[:, pl.ds(j * 256, 256)] = xall[pl.ds(j * 256, 256), :].T

    smf[...] = sm[...].astype(F32)
    vec[...] = jnp.zeros_like(vec)
    for i in range(8):
        vec[pl.ds(i, 1), :] = spread(smf[pl.ds(i, 32, stride=16), :], 24, 768)
    vecu[...] = spread(smf[pl.ds(8, 32, stride=16), :], 96, 3072)

    def q_tile(j, _):
        w = tile(j, 256)
        hq8[:, w] = ((nn(x[...], wqkv[:, w]) + vec[0:1, w]).astype(BF).astype(F32) * 0.125).astype(BF)
        return 0
    lax.fori_loop(0, 3, q_tile, 0)

    def kv_tile(j, _):
        w = tile(j, 256)
        for r in range(2):
            rows = pl.ds(r * 512, 512)
            k = nn(xall[rows, :], wqkv[:, pl.ds(pl.multiple_of(768 + j * 256, 256), 256)]).astype(BF)
            kk[rows, w] = k
            kt[w, rows] = k.T
            v = (nn(xall[rows, :], wqkv[:, pl.ds(pl.multiple_of(1536 + j * 256, 256), 256)]) + vec[1:2, w]).astype(BF)
            vv[rows, w] = v
            vt[w, rows] = v.T
        return 0
    lax.fori_loop(0, 3, kv_tile, 0)
    for i, (a, b) in enumerate(((xt, hxt), (vv, hv), (kt, hkt))):
        outs.append(pltpu.make_async_copy(a, b, osem.at[2 + i]))
        outs[-1].start()

    per = -(-(len(steps) - at[0]) // 7)
    for p in range(PAIRS):
        w = pl.ds(p * 128, 128)
        qm = head_rows(hq8[:, w], 0)

        def score(c, m):
            rows = tile(c, 128)
            one = mask[rows, :]
            v = nt(kk[rows, w], qm) + jnp.concatenate([one, one], 1)
            st[rows, :] = v
            return jnp.maximum(m, jnp.max(v.reshape(16, 8, 512), 0))
        top = lax.fori_loop(0, 8, score, jnp.full((8, 512), -3e38, F32))
        top = jnp.max(top, 0, keepdims=True)

        def power(c, total):
            rows = tile(c, 128)
            v = jnp.exp(st[rows, :] - top)
            ee[p, rows, :] = v.astype(BF)
            return total + jnp.sum(v.reshape(16, 8, 512), 0)
        total = lax.fori_loop(0, 8, power, jnp.zeros((8, 512), F32))
        inverse = 1.0 / jnp.sum(total, 0, keepdims=True)
        hr[pl.ds(p, 1), :] = inverse
        for h in range(2):
            o = nn(vt[pl.ds(p * 128 + h * 64, 64), :], ee[p, :, pl.ds(h * 256, 256)])
            hot[pl.ds(p * 128 + h * 64, 64), :] = (o * inverse[:, h * 256:(h + 1) * 256]).astype(BF)
        outs.append(pltpu.make_async_copy(ee.at[p], he.at[p], esem.at[p]))
        outs[-1].start()
        pump(per)
    pump(len(steps) - at[0])

    g.arrived("out")
    outs.append(pltpu.make_async_copy(wo, ho, osem.at[5]))
    outs[-1].start()
    attn = tn(hot[...], wo[...]) + vec[2:3, :]
    first = x[...].astype(F32) + attn
    centred = first - jnp.mean(first, -1, keepdims=True)
    r1 = lax.rsqrt(jnp.mean(centred * centred, -1, keepdims=True) + EPS)
    n1 = centred * r1
    hn1[...] = n1
    hr1[...] = jnp.broadcast_to(r1, (256, 128))
    normed = n1 * vec[3:4, :] + vec[4:5, :]
    n2[...] = normed
    nl[...] = normed.astype(BF)
    hnlt[...] = nl[...].T

    g.arrived("up0")
    g.arrived("up1")
    outs.append(pltpu.make_async_copy(wu, hu, osem.at[6]))
    outs[-1].start()

    def up_tile(j, _):
        w = tile(j, 256)
        before = nn(nl[...], wu[:, w]) + vecu[:, w]
        phi = 0.5 * (1.0 + lax.erf(before * 0.7071067811865476))
        a = (before * phi).astype(BF)
        act[:, w] = a
        hactt[w, :] = a.T
        hgp[:, w] = (phi + before * 0.3989422804014327 * jnp.exp(-0.5 * before * before)).astype(BF)
        return 0
    lax.fori_loop(0, 12, up_tile, 0)

    g.arrived("down0")
    g.arrived("down1")
    outs.append(pltpu.make_async_copy(wd, hd, osem.at[7]))
    outs[-1].start()

    def down_tile(j, _):
        w = tile(j, 256)
        n2[:, w] += nn(act[...], wd[:, w]) + vec[5:6, w]
        return 0
    lax.fori_loop(0, 3, down_tile, 0)
    second = n2[...]
    centred = second - jnp.mean(second, -1, keepdims=True)
    r2 = lax.rsqrt(jnp.mean(centred * centred, -1, keepdims=True) + EPS)
    n = centred * r2
    kept = keep[...] > 0
    out[...] = jnp.where(kept, n * vec[6:7, :] + vec[7:8, :], x[...].astype(F32)).astype(BF)
    grad = jnp.where(kept, cot[...].astype(F32), 0.0)
    hsm[...] = jnp.zeros_like(hsm)
    hsm[0:1, :] = jnp.sum(grad * n, 0, keepdims=True)
    hsm[1:2, :] = jnp.sum(grad, 0, keepdims=True)
    hsm[2:3, :] = vec[3:4, :]
    c = grad * vec[6:7, :]
    hgs[...] = r2 * (c - jnp.mean(c, -1, keepdims=True) - n * jnp.mean(c * n, -1, keepdims=True))

    for p in NAMES:
        g.drain(p)
    for c in swaps:
        c.wait_send()
    for c in xs:
        c.wait_send()
    for o in outs:
        o.wait()


FORWARD_OUT = (
    ((256, 768), BF, True), ((768, 2304), BF, False), ((768, 768), BF, False), ((768, 3072), BF, False),
    ((3072, 768), BF, False), ((768, 1024), BF, False), ((1024, 768), BF, False),
    ((768, 1024), BF, False), ((PAIRS, 1024, 512), BF, False), ((256, 768), BF, True), ((768, 256), BF, True),
    ((8, 512), F32, True), ((3072, 256), BF, True), ((256, 3072), BF, True), ((768, 256), BF, True),
    ((256, 768), F32, True), ((256, 128), F32, True), ((256, 768), F32, True), ((8, 768), F32, True),
)


def forward_call(fq, fo, fu, fd, fs, x, cot, seg, pad, keep):
    a = pl.BlockSpec(memory_space=pl.ANY)
    v = pl.BlockSpec(memory_space=pltpu.VMEM)
    n = len(PARTS)
    dma = pltpu.SemaphoreType.DMA
    return pl.pallas_call(
        forward_kernel,
        out_shape=[jax.ShapeDtypeStruct(s, d) for s, d, _ in FORWARD_OUT],
        in_specs=[v] * 10,
        out_specs=[v if near else a for _, _, near in FORWARD_OUT],
        scratch_shapes=[
            pltpu.VMEM((1728, 128), BF), pltpu.VMEM((2, 1728, 128), F32),
            pltpu.VMEM((768, 2304), BF), pltpu.VMEM((768, 768), BF), pltpu.VMEM((768, 3072), BF),
            pltpu.VMEM((3072, 768), BF), pltpu.VMEM((512, 128), BF), pltpu.VMEM((512, 128), F32),
            pltpu.VMEM((1024, 768), BF), pltpu.VMEM((1024, 768), BF), pltpu.VMEM((1024, 768), BF),
            pltpu.VMEM((768, 1024), BF), pltpu.VMEM((768, 1024), BF), pltpu.VMEM((1024, 512), F32),
            pltpu.VMEM((PAIRS, 1024, 512), BF), pltpu.VMEM((1024, 256), F32), pltpu.VMEM((8, 768), F32),
            pltpu.VMEM((1, 3072), F32), pltpu.VMEM((256, 768), F32), pltpu.VMEM((768, 1024), BF),
            pltpu.VMEM((256, 3072), BF), pltpu.VMEM((256, 768), BF),
            dma((4,)), dma((4,)), dma((n, 16, 5)), dma((n, 16)), dma((n, 16)), dma((8,)), dma((3,)), dma((3,)),
            dma((PAIRS,)),
        ],
        compiler_params=pltpu.CompilerParams(collective_id=1, has_side_effects=True, vmem_limit_bytes=62 << 20),
        name="forward",
    )(fq, fo, fu, fd, fs, x, cot, seg, pad, keep)


RPARTS = (
    ("down0", 3, "xzy", 96, 0, 0, 384),
    ("down1", 3, "yzx", 96, 96, 0, 384),
    ("up0", 2, "xzy", 48, 0, 0, 768),
    ("up1", 2, "yzx", 48, 0, 768, 768),
    ("out", 1, "zxy", 48, 0, 0, 384),
    ("qkv0", 0, "zxy", 48, 0, 0, 640),
    ("qkv1", 0, "zyx", 48, 0, 640, 512),
)
HALF = (1152, 384, 1536, 384)
CHIPROWS = (48, 48, 48, 192)
ROWS = (768, 768, 768, 3072)
SIZES = {"x": 2, "y": 2, "z": 4}
LINKS = ("up", "down", "x", "y")


def slots(order, axis):
    n = 4 if axis == "z" else 1
    for a in order[: order.index(axis)]:
        n *= SIZES[a]
    return n


def landing_shapes():
    shapes = []
    for name, mat, order, rows, ro, co, cols in RPARTS:
        for way in LINKS:
            axis = "z" if way in ("up", "down") else way
            shapes.append(pltpu.VMEM((slots(order, axis), rows, cols), BF))
    return shapes


class Scatter:
    def __init__(self, me, grads, lands, finals, send, recv):
        self.me, self.grads, self.lands, self.finals = me, grads, lands, finals
        self.send, self.recv = send, recv

    def chip(self, x, y, z):
        return (z * 2 + x) * 2 + y

    def block(self, i, dest):
        name, mat, order, rows, ro, co, cols = RPARTS[i]
        first = pl.multiple_of(self.chip(*dest) * CHIPROWS[mat] + ro, 16)
        return self.grads[mat].at[pl.ds(first, rows), pl.ds(co, cols)]

    def slot(self, i, way, dest):
        order = RPARTS[i][2]
        axis = "z" if way in ("up", "down") else way
        coords = dict(zip("xyz", dest))
        index = coords["z"] if axis == "z" else 0
        for a in order[: order.index(axis)]:
            index = index * SIZES[a] + coords[a]
        return index

    def land(self, i, way, dest):
        return self.lands[i * 4 + LINKS.index(way)].at[self.slot(i, way, dest)]

    def copy(self, i, way, dest):
        chip = self.chip(*dest)
        return pltpu.make_async_remote_copy(
            self.block(i, dest), self.land(i, way, dest), self.send.at[i, chip],
            self.recv.at[i, LINKS.index(way), chip], device_id=self.me.to(way), device_id_type=MESH)

    def stage(self, i, fx, fy, k):
        moved = {"x": fx, "y": fy, "z": k}
        return max(s for s in range(3) if moved[RPARTS[i][2][s]])

    def take(self, i, way, dest):
        self.copy(i, way, dest).wait_recv()
        ref = self.block(i, dest)
        ref[...] = (ref[...].astype(F32) + self.land(i, way, dest)[...].astype(F32)).astype(BF)

    def serve(self, i, fx, fy, k):
        me = self.me
        order = RPARTS[i][2]
        stage = self.stage(i, fx, fy, k)
        axis = order[stage]

        def act(dest, sign):
            way = axis
            if axis == "z":
                way, more = ("down", me.z < 3) if sign < 0 else ("up", me.z > 0)
                pl.when(more)(lambda: self.take(i, way, dest))
            for a in order[stage + 1:]:
                if a == "z":
                    pl.when(me.z < 3)(lambda: self.take(i, "down", dest))
                    pl.when(me.z > 0)(lambda: self.take(i, "up", dest))
                else:
                    self.take(i, a, dest)
            self.copy(i, way, dest).start()

        self.dests(fx, fy, k, act)

    def dests(self, fx, fy, k, act):
        me = self.me
        x = 1 - me.x if fx else me.x
        y = 1 - me.y if fy else me.y
        if k == 0:
            act((x, y, me.z), 0)
        else:
            pl.when(me.z >= k)(lambda: act((x, y, me.z - k), -1))
            pl.when(me.z + k <= 3)(lambda: act((x, y, me.z + k), 1))

    def finish(self, i):
        name, mat, order, rows, ro, co, cols = RPARTS[i]
        me = self.me
        dest = (me.x, me.y, me.z)
        fin = self.finals[mat].at[pl.ds(ro, rows), pl.ds(co, cols)]
        fin[...] = self.block(i, dest)[...].astype(F32)

        def add(way):
            self.copy(i, way, dest).wait_recv()
            fin[...] += self.land(i, way, dest)[...].astype(F32)
        for axis in order:
            if axis == "z":
                pl.when(me.z < 3)(lambda: add("down"))
                pl.when(me.z > 0)(lambda: add("up"))
            else:
                add(axis)

    def drain(self, i):
        for fx in (0, 1):
            for fy in (0, 1):
                for k in range(4):
                    if fx + fy + k:
                        axis = RPARTS[i][2][self.stage(i, fx, fy, k)]
                        self.dests(fx, fy, k, lambda dest, sign: self.copy(
                            i, axis if axis != "z" else ("down" if sign < 0 else "up"), dest).wait_send())


def service(parts):
    steps = []
    for i in parts:
        for fx in (0, 1):
            for fy in (0, 1):
                for k in range(4):
                    if fx + fy + k:
                        steps.append(((-(fx + fy + k), i), i, fx, fy, k))
    steps.sort()
    return [s[1:] for s in steps]


FLATROWS = ((24, 18, 432), (24, 6, 144), (24, 24, 576), (96, 6, 576))


def flatten(me, mat, finals, sides, out):
    rows, tiles, lines = FLATROWS[mat]
    half = tiles // 2
    for j in range(half):
        mine = finals[mat][pl.ds(pl.multiple_of(me.c * rows, 8), rows), pl.ds(j * 128, 128)]
        out[pl.ds(me.c * half + j, rows, stride=tiles), :] = mine
        out[pl.ds((1 - me.c) * half + j, rows, stride=tiles), :] = sides[mat][:, pl.ds(j * 128, 128)]


def colsum(array):
    return jnp.sum(array.astype(F32), 0, keepdims=True)


def backward_kernel(
    hq, ho, hu, hd, hxt, hv, hkt, he, q8, ot, rr, actt, gp, nlt, n1, r1, gs, sm0, cot, keep,
    ingrad, oq, oo, ou, od, osm, *rest,
):
    lands, rest = rest[:28], rest[28:]
    grads, rest = rest[:4], rest[4:]
    stage, rest = rest[:3], rest[3:]
    stage = (stage[1].at[:, pl.ds(0, HALF[0])],) + tuple(stage)
    half, rest = rest[:3], rest[3:]
    half = (half[1].at[:, pl.ds(0, HALF[0])],) + tuple(half)
    finals, rest = rest[:4], rest[4:]
    sides, rest = rest[:4], rest[4:]
    (wbig, wo, xt, vv, kt, ee, ds, gbr, gbef, first, gts, gsa, dq, dkv, dx, dxc, dxy, acc, sland,
     wsem, isem, esem, csend, crecv, send, recv, fsend, frecv, dsend, drecv, asend, arecv, free) = rest
    me = Place()
    s = me.y * 2 + me.c
    wds = [pltpu.make_async_copy(hd.at[pl.ds(q * 768, 768), :], wbig.at[pl.ds(q * 768, 768), :], wsem.at[q]) for q in range(4)]
    wus = [pltpu.make_async_copy(hu.at[:, pl.ds(q * 768, 768)], wbig.at[pl.ds(q * 768, 768), :], wsem.at[4 + q]) for q in range(4)]
    wqs = [pltpu.make_async_copy(hq.at[:, pl.ds(q * 768, 768)], wbig.at[pl.ds(q * 768, 768), :], wsem.at[8 + q]) for q in range(3)]
    others = [pltpu.make_async_copy(a, b, isem.at[i]) for i, (a, b) in enumerate(((ho, wo), (hv, vv), (hkt, kt), (hxt, xt)))]
    ees = [pltpu.make_async_copy(he.at[p], ee.at[p % 2], esem.at[p]) for p in range(PAIRS)]
    for c in wds:
        c.start()
    for c in others:
        c.start()
    ees[0].start()
    ees[1].start()
    enter(me)

    sc = Scatter(me, grads, lands, finals, send, recv)

    def swap(mat):
        return pltpu.make_async_remote_copy(
            stage[mat], half[mat], csend.at[mat], crecv.at[mat], device_id=me.to("core"), device_id_type=MESH)

    def merge(mat):
        swap(mat).wait_recv()

        def body(r, _):
            w = tile(r, 48)
            grads[mat][w, :] = (grads[mat][w, :].astype(F32) + half[mat][w, :].astype(F32)).astype(BF)
            return 0
        lax.fori_loop(0, ROWS[mat] // 48, body, 0)

    steps = []

    def pump(n=1000):
        for st in steps[:n]:
            sc.serve(*st)
        del steps[:n]

    def arrange(value_ref, to):
        to[:, 0:384] = value_ref[:, pl.ds(pl.multiple_of(me.c * 384, 128), 384)]
        to[:, 384:768] = value_ref[:, pl.ds(pl.multiple_of((1 - me.c) * 384, 128), 384)]

    osm[...] = jnp.zeros_like(osm)
    osm[6:8, :] = sm0[0:2, :]
    gsa[...] = gs[...].astype(BF)
    osm[5:6, :] = colsum(gsa[...])
    arrange(gsa, gbr)

    def down_grad(j, _):
        w = tile(j, 256)
        v = nn(actt[w, :], gbr[...]).astype(BF)
        grads[3][w, :] = v[:, 0:384]
        stage[3][w, :] = v[:, 384:768]
        return 0
    lax.fori_loop(0, 12, down_grad, 0)
    swap(3).start()

    for q in range(4):
        wds[q].wait()

        def up_back(j, _):
            w = tile(q * 3 + j, 256)
            ga = nt(gsa[...], wbig[w, :]).astype(BF).astype(F32)
            gb = (ga * gp[:, w].astype(F32)).astype(BF)
            gbef[:, w] = gb
            osm[8 + q:9 + q, tile(j, 256)] = colsum(gb)
            return 0
        lax.fori_loop(0, 3, up_back, 0)
        wus[q].start()
    merge(3)
    steps += service((0, 1))
    pump(8)

    def up_grad(j, _):
        w = tile(j, 256)
        stage[2][:, w] = nn(nlt[...], gbef[:, pl.ds(pl.multiple_of((1 - me.c) * 1536 + j * 256, 256), 256)]).astype(BF)
        return 0
    lax.fori_loop(0, 6, up_grad, 0)
    swap(2).start()

    def up_own(j, _):
        w = tile(j, 256)
        grads[2][:, w] = nn(nlt[...], gbef[:, pl.ds(pl.multiple_of(me.c * 1536 + j * 256, 256), 256)]).astype(BF)
        return 0
    lax.fori_loop(0, 6, up_own, 0)
    for c in wus:
        c.wait()

    def normed_back(j, _):
        w = tile(j, 256)
        total = gs[:, w]
        for q in range(4):
            total += nt(gbef[:, pl.ds(q * 768, 768)], wbig[pl.ds(pl.multiple_of(q * 768 + j * 256, 256), 256), :])
        first[:, w] = total
        return 0
    lax.fori_loop(0, 3, normed_back, 0)
    for c in wqs:
        c.start()
    pump(6)
    merge(2)
    pl.semaphore_signal(free, 1, device_id=me.to("core"), device_id_type=MESH)
    steps += service((2, 3))
    pump(8)

    gn = first[...]
    n = n1[...]
    osm[3:4, :] = jnp.sum(gn * n, 0, keepdims=True)
    osm[4:5, :] = jnp.sum(gn, 0, keepdims=True)
    c1 = gn * sm0[2:3, :]
    gf = r1[:, 0:1] * (c1 - jnp.mean(c1, -1, keepdims=True) - n * jnp.mean(c1 * n, -1, keepdims=True))
    first[...] = gf
    gsa[...] = gf.astype(BF)
    osm[2:3, :] = colsum(gsa[...])
    arrange(gsa, gbr)

    def out_grad(j, _):
        w = tile(j, 256)
        v = nn(ot[w, :], gbr[...]).astype(BF)
        grads[1][w, :] = v[:, 0:384]
        stage[1][w, :] = v[:, 384:768]
        return 0
    lax.fori_loop(0, 3, out_grad, 0)
    swap(1).start()
    for c in others:
        c.wait()
    for p in range(PAIRS):
        w = pl.ds(p * 128, 128)
        g = nt(wo[w, :], gsa[...]).astype(BF).astype(F32)
        scale = jnp.concatenate(
            [jnp.broadcast_to(rr[p:p + 1, h * 256:(h + 1) * 256], (64, 256)) for h in range(2)], 0)
        gts[w, :] = (g * scale).astype(BF)
    merge(1)
    steps += service((4,))

    for p in range(PAIRS):
        w = pl.ds(p * 128, 128)
        g = gts[w, :]
        both = ot[w, :].astype(F32) * g.astype(F32)
        delta = jnp.concatenate([jnp.sum(both[0:64], 0, keepdims=True), jnp.sum(both[64:128], 0, keepdims=True)], 1)
        gm = head_rows(g.T, 0)
        qm = head_rows(q8[:, w], 0)
        ees[p].wait()
        e = ee.at[p % 2]

        def score_back(c, _):
            rows = tile(c, 128)
            dp = nt(vv[rows, w], gm)
            ds[rows, :] = (e[rows, :].astype(F32) * (dp - delta)).astype(BF)
            return 0
        lax.fori_loop(0, 8, score_back, 0)

        def kv_back(c, _):
            rows = tile(c, 256)
            dkv[rows, w] = nn(ds[rows, :], qm).astype(BF)
            dkv[rows, pl.ds(768 + p * 128, 128)] = nn(e[rows, :], gm).astype(BF)
            return 0
        lax.fori_loop(0, 4, kv_back, 0)
        dqt = jnp.concatenate([
            nn(kt[pl.ds(p * 128 + h * 64, 64), :], ds[:, pl.ds(h * 256, 256)]) for h in range(2)], 0)
        dq[:, w] = (dqt * 0.125).astype(BF).T
        if p + 2 < PAIRS:
            ees[p + 2].start()
        pump(8)

    osm[0:1, :] = colsum(dq[...])
    osm[1:2, :] = colsum(dkv[:, pl.ds(768, 768)])

    swap(2).wait_send()
    mine = xt.at[:, tile(s, 256)]

    def qkv_block(b, to):
        col = pl.ds((b % 3) * 384, 384)
        for r in range(3):
            rows = pl.ds(r * 256, 256)
            if b < 2:
                to[rows, col] = nn(mine[rows, :], dq[:, pl.ds(b * 384, 384)]).astype(BF)
            else:
                to[rows, col] = nn(xt[rows, :], dkv[:, pl.ds((b - 2) * 384, 384)]).astype(BF)

    for h in range(2):
        @pl.when(me.c == h)
        def _():
            for b in range(3):
                qkv_block(3 * (1 - h) + b, stage[0])
    pl.semaphore_wait(free, 1)
    swap(0).start()
    for h in range(2):
        @pl.when(me.c == h)
        def _():
            for b in range(3):
                qkv_block(3 * h + b, grads[0])

    for c in wqs:
        c.wait()

    def dx_tile(j, _):
        w = tile(j, 256)
        for r in range(2):
            rows = pl.ds(r * 512, 512)
            dx[rows, w] = (
                nt(dkv[rows, 0:768], wbig[pl.ds(pl.multiple_of(768 + j * 256, 256), 256), :])
                + nt(dkv[rows, 768:1536], wbig[pl.ds(pl.multiple_of(1536 + j * 256, 256), 256), :])).astype(BF)
        first[:, w] += nt(dq[...], wbig[w, :])
        return 0
    lax.fori_loop(0, 3, dx_tile, 0)

    def dx_copy(n):
        if n < 2:
            yy = me.y if n == 0 else 1 - me.y
            return pltpu.make_async_remote_copy(
                dx.at[tile(yy * 2 + 1 - me.c, 256), :], dxc.at[n], dsend.at[n], drecv.at[n],
                device_id=me.to("core"), device_id_type=MESH)
        return pltpu.make_async_remote_copy(
            dx.at[tile((1 - me.y) * 2 + me.c, 256), :], dxy, dsend.at[2], drecv.at[2],
            device_id=me.to("y"), device_id_type=MESH)
    dx_copy(1).start()
    dx_copy(0).start()
    merge(0)
    steps += service((5, 6))
    pump(8)
    dx_copy(1).wait_recv()
    over = tile((1 - me.y) * 2 + me.c, 256)
    dx[over, :] = (dx[over, :].astype(F32) + dxc[1].astype(F32)).astype(BF)
    dx_copy(2).start()

    acc[0] = osm[...]
    pairz = {"outer": (me.z + 1 - 2 * (me.z % 2)) * 2 + me.x}
    smalls = [
        pltpu.make_async_remote_copy(acc.at[i], sland.at[i], asend.at[i], arecv.at[i], device_id=to, device_id_type=MESH)
        for i, to in enumerate((me.to("core"), me.to("x"), me.to("y"), pairz, me.to("far")))
    ]
    smalls[0].start()
    hop = 0

    def small_step(i):
        smalls[i].wait_recv()
        acc[i + 1] = acc[i] + sland[i]
        if i < 4:
            smalls[i + 1].start()

    for i in range(5):
        pump(5)
        small_step(i)
    pump()
    osm[...] = acc[5]
    for i in range(7):
        sc.finish(i)
    lasts = []
    for mat in range(4):
        rows = FLATROWS[mat][0]
        src = finals[mat].at[pl.ds(pl.multiple_of((1 - me.c) * rows, 8), rows), :]
        lasts.append(pltpu.make_async_remote_copy(
            src, sides[mat], fsend.at[mat], frecv.at[mat], device_id=me.to("core"), device_id_type=MESH))
        lasts[-1].start()
    dx_copy(0).wait_recv()
    dx_copy(2).wait_recv()
    total = first[...] + dx[tile(s, 256), :].astype(F32) + dxc[0].astype(F32) + dxy[...].astype(F32)
    ingrad[...] = jnp.where(keep[...] > 0, total, cot[...].astype(F32)).astype(BF)
    for i in range(7):
        sc.drain(i)
    for mat in (3, 1, 0):
        swap(mat).wait_send()
    for n in range(3):
        dx_copy(n).wait_send()
    for c in smalls:
        c.wait_send()
    for mat, c in enumerate(lasts):
        c.wait()
        flatten(me, mat, finals, sides, (oq, oo, ou, od)[mat])


def backward_call(*args):
    a = pl.BlockSpec(memory_space=pl.ANY)
    v = pl.BlockSpec(memory_space=pltpu.VMEM)
    dma = pltpu.SemaphoreType.DMA
    outs = [((256, 768), BF)] + [((FLATROWS[m][2], 128), F32) for m in range(4)] + [((16, 768), F32)]
    halves = [(ROWS[m], HALF[m]) for m in range(4)]
    return pl.pallas_call(
        backward_kernel,
        out_shape=[jax.ShapeDtypeStruct(s, d) for s, d in outs],
        in_specs=[a] * 8 + [v] * 12,
        out_specs=[v] * 6,
        scratch_shapes=landing_shapes()
        + [pltpu.VMEM(h, BF) for h in halves + halves[1:] + halves[1:]]
        + [pltpu.VMEM((CHIPROWS[m], HALF[m]), F32) for m in range(4)]
        + [pltpu.VMEM((FLATROWS[m][0], HALF[m]), F32) for m in range(4)]
        + [
            pltpu.VMEM((3072, 768), BF), pltpu.VMEM((768, 768), BF), pltpu.VMEM((768, 1024), BF),
            pltpu.VMEM((1024, 768), BF), pltpu.VMEM((768, 1024), BF), pltpu.VMEM((2, 1024, 512), BF),
            pltpu.VMEM((1024, 512), BF), pltpu.VMEM((256, 768), BF), pltpu.VMEM((256, 3072), BF),
            pltpu.VMEM((256, 768), F32), pltpu.VMEM((768, 256), BF), pltpu.VMEM((256, 768), BF),
            pltpu.VMEM((256, 768), BF), pltpu.VMEM((1024, 1536), BF), pltpu.VMEM((1024, 768), BF),
            pltpu.VMEM((2, 256, 768), BF), pltpu.VMEM((256, 768), BF), pltpu.VMEM((6, 16, 768), F32),
            pltpu.VMEM((5, 16, 768), F32),
            dma((11,)), dma((4,)), dma((PAIRS,)), dma((4,)), dma((4,)), dma((7, 16)), dma((7, 4, 16)),
            dma((4,)), dma((4,)), dma((3,)), dma((3,)), dma((5,)), dma((5,)),
            pltpu.SemaphoreType.REGULAR,
        ],
        compiler_params=pltpu.CompilerParams(collective_id=2, has_side_effects=True, vmem_limit_bytes=62 << 20),
        name="backward",
    )(*args)


AXES = ("outer", "inner", "seq")
SMALLS = (1, 2, 4, 5, 6, 10, 11, 12, 8)


def to_part(flat):
    inner = lax.axis_size("inner")
    if inner == 1:
        return flat
    every = lax.all_gather(flat, ("inner", "seq"), axis=0, tiled=True)
    size = flat.shape[0] * inner
    return lax.dynamic_slice_in_dim(every, lax.axis_index("seq") * size, size, 0)


def whole_scatter(part):
    inner = lax.axis_size("inner")
    if inner == 1:
        return part
    every = lax.psum(lax.all_gather(part, "seq", axis=0, tiled=True), "inner")
    size = part.shape[0] // inner
    index = lax.axis_index("inner") * lax.axis_size("seq") + lax.axis_index("seq")
    return lax.dynamic_slice_in_dim(every, index * size, size, 0)


def shards(inputs, *rest):
    params, (cotangent, segment_ids, pad_mask, keep_flag) = rest[:13], rest[13:]
    parts = [to_part(p) for p in params]
    small = sum(
        jnp.pad(parts[i][None, :], ((row, 15 - row), (0, 128 - parts[i].shape[0])))
        for row, i in enumerate(SMALLS)
    )
    x, cot = inputs[0], cotangent[0]
    keep = keep_flag.reshape(1, 1)
    out, *held = forward_call(
        *(parts[i].reshape(-1, 128) for i in (0, 3, 7, 9)), small, x, cot, segment_ids, pad_mask, keep
    )
    grad, *big, sums = backward_call(*held, cot, keep)
    big = [whole_scatter(part.reshape(-1)) for part in big]
    if lax.axis_size("inner") > 1:
        sums = lax.psum(sums, "inner")
    index = lax.axis_index(AXES)
    count = lax.axis_size(AXES)
    mine = lax.dynamic_slice_in_dim(sums[:8].reshape(8, count, D // count), index, 1, 1)[:, 0]
    mine_up = lax.dynamic_slice_in_dim(sums[8:12].reshape(count, FF // count), index, 1, 0)[0]
    q, v, ob, g1, b1, db, g2, b2 = (mine[i] for i in range(8))
    return (out[None], grad[None], big[0], q, v, big[1], ob, g1, b1, big[2], mine_up, big[3], db, g2, b2)


def solution(mesh):
    fsdp, seq = mesh.shape["fsdp"], mesh.shape["seq"]
    mesh = Mesh(mesh.devices.reshape(8, fsdp // 8, seq), AXES)
    tokens = P(("outer", "inner"), "seq", None)
    flat = P(AXES)
    rows = P(("outer", "inner"), None)
    return jax.shard_map(
        shards,
        mesh=mesh,
        in_specs=(tokens,) + (flat,) * 13 + (tokens, rows, rows, P(("outer", "inner"))),
        out_specs=(tokens, tokens) + (flat,) * 13,
        check_vma=False,
    )
```

```python
import functools
import jax
import jax.numpy as jnp
from jax import lax
from jax.experimental import pallas as pl
from jax.experimental.pallas import tpu as pltpu
from jax.sharding import Mesh, PartitionSpec as P

MESH = pl.DeviceIdType.MESH
D = 768
FF = 3072
BF = jnp.bfloat16
F32 = jnp.float32
LINES = (432, 144, 576, 576)
BASE = (0, 432, 576, 1152)
WIDE = 1664


class Place:
    def __init__(self):
        o = lax.axis_index("outer")
        s = lax.axis_index("seq")
        self.z, self.x, self.y, self.c = o // 2, o % 2, s // 2, s % 2

    def to(self, way):
        z, x, y, c = self.z, self.x, self.y, self.c
        return {
            "up": {"outer": (z + 1) * 2 + x},
            "down": {"outer": (z - 1) * 2 + x},
            "x": {"outer": z * 2 + 1 - x},
            "y": {"seq": (1 - y) * 2 + c},
            "core": {"seq": y * 2 + 1 - c},
            "far": {"outer": (3 - z) * 2 + x},
        }[way]


def enter(me):
    bar = pltpu.get_barrier_semaphore()

    def greet(to):
        pl.semaphore_signal(bar, 1, device_id=to, device_id_type=MESH)

    for way in ("x", "y", "core"):
        greet(me.to(way))
    pl.when(me.z < 3)(lambda: greet(me.to("up")))
    pl.when(me.z > 0)(lambda: greet(me.to("down")))
    pl.when((me.z == 0) | (me.z == 3))(lambda: greet(me.to("far")))
    pl.semaphore_wait(bar, 5)


WAYS = ("up", "down", "x", "y")

PARTS = (
    ("attn0", "yzx"),
    ("attn1", "zxy"),
    ("up0", "yzx"),
    ("up1", "yzx"),
    ("down0", "xzy"),
    ("down1", "zxy"),
)
NAMES = [p[0] for p in PARTS]
ORDER = dict(PARTS)


class Gather:
    def __init__(self, me, refs, send, recv, csend, crecv):
        self.me = me
        self.refs = refs
        self.send, self.recv, self.csend, self.crecv = send, recv, csend, crecv

    def block(self, part, chip, c):
        wa, wu, wd = self.refs
        m = pl.multiple_of
        if part == "down0":
            return wd.at[chip, pl.ds(0, 96), pl.ds(m(c * 384, 128), 384)]
        if part == "down1":
            return wd.at[chip, pl.ds(96, 96), pl.ds(m(c * 384, 128), 384)]
        rows = pl.ds(m(chip * 48, 16), 48)
        if part == "attn0":
            return wa.at[rows, pl.ds(m(c * WIDE, 128), 768)]
        if part == "attn1":
            return wa.at[rows, pl.ds(m(c * WIDE + 768, 128), 896)]
        if part == "up0":
            return wu.at[rows, pl.ds(m(c * 1536, 128), 768)]
        return wu.at[rows, pl.ds(m(c * 1536 + 768, 128), 768)]

    def half(self, part, c):
        wa, wu, wd = self.refs
        m = pl.multiple_of
        if part == "down0":
            return wd.at[:, pl.ds(0, 96), pl.ds(m(c * 384, 128), 384)]
        if part == "down1":
            return wd.at[:, pl.ds(96, 96), pl.ds(m(c * 384, 128), 384)]
        if part == "attn0":
            return wa.at[:, pl.ds(m(c * WIDE, 128), 768)]
        if part == "attn1":
            return wa.at[:, pl.ds(m(c * WIDE + 768, 128), 896)]
        if part == "up0":
            return wu.at[:, pl.ds(m(c * 1536, 128), 768)]
        return wu.at[:, pl.ds(m(c * 1536 + 768, 128), 768)]

    def chip(self, x, y, z):
        return (z * 2 + x) * 2 + y

    def copy(self, part, chip, way):
        i = NAMES.index(part)
        ref = self.block(part, chip, self.me.c)
        return pltpu.make_async_remote_copy(
            ref, ref, self.send.at[i, chip, WAYS.index(way)], self.recv.at[i, chip],
            device_id=self.me.to(way), device_id_type=MESH)

    def across(self, part, c):
        i = NAMES.index(part)
        ref = self.half(part, c)
        return pltpu.make_async_remote_copy(
            ref, ref, self.csend.at[i], self.crecv.at[i], device_id=self.me.to("core"), device_id_type=MESH)

    def onward(self, part, chip, axes):
        me = self.me
        for axis in axes:
            if axis == "z":
                pl.when(me.z < 3)(lambda: self.copy(part, chip, "up").start())
                pl.when(me.z > 0)(lambda: self.copy(part, chip, "down").start())
            else:
                self.copy(part, chip, axis).start()

    def own(self, part):
        me = self.me
        chip = self.chip(me.x, me.y, me.z)
        self.onward(part, chip, ORDER[part])

    def origins(self, fx, fy, k, act):
        me = self.me
        x = 1 - me.x if fx else me.x
        y = 1 - me.y if fy else me.y
        if k == 0:
            act(self.chip(x, y, me.z), 0)
        else:
            pl.when(me.z >= k)(lambda: act(self.chip(x, y, me.z - k), -1))
            pl.when(me.z + k <= 3)(lambda: act(self.chip(x, y, me.z + k), 1))

    def arrival(self, part, fx, fy, k):
        moved = {"x": fx, "y": fy, "z": k}
        return max(i for i in range(3) if moved[ORDER[part][i]])

    def serve(self, part, fx, fy, k):
        me = self.me
        order = ORDER[part]
        stage = self.arrival(part, fx, fy, k)
        axis = order[stage]

        def act(chip, sign):
            if axis == "z":
                way, more = ("up", me.z < 3) if sign < 0 else ("down", me.z > 0)
                self.copy(part, chip, way).wait_recv()
                pl.when(more)(lambda: self.copy(part, chip, way).start())
            else:
                self.copy(part, chip, axis).wait_recv()
            self.onward(part, chip, order[stage + 1:])

        self.origins(fx, fy, k, act)

    def arrived(self, part):
        self.across(part, 1 - self.me.c).wait_recv()

    def drain(self, part):
        me = self.me
        order = ORDER[part]

        self.across(part, me.c).wait_send()

        def sent(chip, axes, sign):
            for axis in axes:
                if axis == "z":
                    if sign <= 0:
                        pl.when(me.z < 3)(lambda: self.copy(part, chip, "up").wait_send())
                    if sign >= 0:
                        pl.when(me.z > 0)(lambda: self.copy(part, chip, "down").wait_send())
                else:
                    self.copy(part, chip, axis).wait_send()

        for fx in (0, 1):
            for fy in (0, 1):
                for k in range(4):
                    if fx + fy + k == 0:
                        sent(self.chip(me.x, me.y, me.z), order, 0)
                        continue
                    stage = self.arrival(part, fx, fy, k)
                    axes = order[stage:] if order[stage] == "z" else order[stage + 1:]
                    self.origins(fx, fy, k, lambda chip, sign: sent(
                        chip, axes, sign if order[stage] == "z" else 0))


def relayout(me, wide, refs, name):
    m = pl.multiple_of
    chip = (me.z * 2 + me.x) * 2 + me.y
    wa, wu, wd = refs

    def rows(base, count, stride):
        both = [wide[d, pl.ds(base, count, stride=stride), :] for d in range(2)]
        return jnp.concatenate(both, 0).astype(BF)

    if name == "up":
        for j in range(12):
            wu[pl.ds(m(chip * 48, 16), 48), pl.ds(m((me.c * 12 + j) * 128, 128), 128)] = rows(
                BASE[2] + me.c * 12 + j, 24, 24)
    elif name == "down":
        for j in range(3):
            wd[chip, :, pl.ds(m((me.c * 3 + j) * 128, 128), 128)] = rows(BASE[3] + me.c * 3 + j, 96, 6)
    else:
        for j in range(6):
            wa[pl.ds(m(chip * 48, 16), 48), pl.ds(m(me.c * WIDE + j * 128, 128), 128)] = rows(
                BASE[0] + me.c * 12 + j, 24, 18)
            to = wa.at[pl.ds(m(chip * 48, 16), 48), pl.ds(m(me.c * WIDE + 768 + j * 128, 128), 128)]

            @pl.when(me.c == 0)
            def _():
                to[...] = rows(BASE[0] + 6 + j, 24, 18)

            @pl.when(me.c == 1)
            def _():
                to[...] = rows(BASE[1] + j, 24, 6)


GATHER_PLAN = (

    (16, 0, 64, 17, 4, 72, 48, 18, 1, 5, 24, 19, 49, 2, 68, 65, 56, 50, 25, 26, 52, 73, 12, 32, 6, 57, 80, 51, 69, 27, 3, 66, 7, 53, 22, 23, 40, 20, 8, 9, 14, 67, 81, 60, 58, 30, 15, 13, 54, 29, 88, 74, 28, 21, 76, 77, 11, 10, 82, 61, 36, 33, 31, 89, 84, 55),
    (), (75, 70, 62, 83, 90, 71, 37), (), (), (), (), (), (), (), (), (), (34, 85, 38), (), (), (), (), (), (), (),
    (), (), (), (45, 35, 91, 92, 93, 39), (), (), (), (78, 79, 42, 43, 59, 87, 95, 46, 44, 94, 63, 86, 41, 47), (),
    (), (), (), (), (), (), (), (), (), (), (), (),
)


HEADS = 12
HD = 64
EPS = 1e-05
PAIRS = HEADS // 2

def nt(left, right):
    return lax.dot_general(left, right, (((1,), (1,)), ((), ())), preferred_element_type=F32)


def nn(left, right):
    return jnp.dot(left, right, preferred_element_type=F32)


def tn(left, right):
    return lax.dot_general(left, right, (((0,), (0,)), ((), ())), preferred_element_type=F32)


def tile(i, size):
    return pl.ds(pl.multiple_of(i * size, size), size)


def spread(sides, size, width):
    lane = lax.broadcasted_iota(jnp.int32, (128, width), 0)
    col = lax.broadcasted_iota(jnp.int32, (128, width), 1)
    owner = ((col.astype(F32) + 0.5) * (1.0 / size)).astype(jnp.int32)
    pick = (col - owner * size == lane).astype(F32).astype(BF)
    dev = lax.broadcasted_iota(jnp.int32, (16, width), 0) * 2
    col = lax.broadcasted_iota(jnp.int32, (16, width), 1)
    owner = ((col.astype(F32) + 0.5) * (1.0 / size)).astype(jnp.int32)
    total = jnp.zeros((16, width), F32)
    for c, rows in enumerate(sides):
        total = total + jnp.where(owner == dev + c, nn(rows.astype(BF), pick), 0.0)
    return jnp.sum(total, 0, keepdims=True)


def swap_rows(me, ref, s, send, recv):
    width = 256

    def block(index):
        return ref.at[tile(index, width), :]

    def copy(index, way, n):
        return pltpu.make_async_remote_copy(
            block(index), block(index), send.at[n], recv.at[n], device_id=me.to(way), device_id_type=MESH)

    mine = me.y * 2 + me.c
    over = (1 - me.y) * 2 + me.c
    return (copy(mine, "core", 0), copy(mine, "y", 1), copy(over, "core", 2)), (
        copy(me.y * 2 + 1 - me.c, "core", 0), copy(over, "y", 1), copy((1 - me.y) * 2 + 1 - me.c, "core", 2))


def head_rows(array, axis):
    lane = lax.broadcasted_iota(jnp.int32, array.shape, 1)
    zero = jnp.zeros_like(array)
    return jnp.concatenate([jnp.where(lane < HD, array, zero), jnp.where(lane >= HD, array, zero)], axis)


def forward_kernel(
    fq, fo, fu, fd, fs, x, cot, seg, pad, keep,
    to_out, to_a, to_u, to_d, to_xt, to_v, to_kt, to_e, to_q8, to_ot, to_r, to_actt, to_gp, to_nlt, to_n1, to_r1, to_gs, to_sm,
    flats, wide, wa, wu, wd, smf, xall, kk, vv, kt, vt, st, ee, mask, vec, vecu, n2, xt, act, nl,
    out, hq8, hot, hr, hactt, hgp, hnlt, hn1, hr1, hgs, hsm,
    fsend, frecv, send, recv, csend, crecv, osem, xsend, xrecv,
):
    me = Place()
    s = me.y * 2 + me.c
    outs = []

    def put(held, to):
        outs.append(pltpu.make_async_copy(held, to, osem.at[len(outs)]))
        outs[-1].start()

    enter(me)
    refs = (wa, wu, wd)
    g = Gather(me, refs, send, recv, csend, crecv)
    swaps = [
        pltpu.make_async_remote_copy(
            src, flats.at[pl.ds(b, n), :], fsend.at[i], frecv.at[i], device_id=me.to("core"), device_id_type=MESH)
        for i, (src, b, n) in enumerate(zip((fq, fo, fu, fd), BASE, LINES))
    ]
    for c in swaps:
        c.start()
    chip = (me.z * 2 + me.x) * 2 + me.y
    wa[pl.ds(pl.multiple_of(chip * 48, 16), 48), pl.ds(pl.multiple_of(me.c * WIDE + 1536, 128), 128)] = jnp.concatenate(
        [fs[...], jnp.zeros((32, 128), BF)], 0)
    xall[tile(s, 256), :] = x[...]
    xs, xr = swap_rows(me, xall, s, xsend, xrecv)
    xs[0].start()
    xs[1].start()
    slot = iter(GATHER_PLAN)
    count = {}

    def tick():
        for code in next(slot, ()):
            p, fx, fy, k = NAMES[code // 16], code // 8 % 2, code // 4 % 2, code % 4
            if fx + fy + k:
                g.serve(p, fx, fy, k)
            else:
                unpack(p)
                g.own(p)
            count[p] = count.get(p, 0) + 1
            if count[p] == 16:
                g.across(p, me.c).start()

    unpacked = []

    def unpack(p):
        name = p.rstrip("01")
        if name in unpacked:
            return
        unpacked.append(name)
        for i in {"attn": (0, 1), "up": (2,), "down": (3,)}[name]:
            src, b, n = (fq, fo, fu, fd)[i], BASE[i], LINES[i]
            wide[me.c, pl.ds(b, n), :] = src[...].astype(F32)
            swaps[i].wait_recv()
            wide[1 - me.c, pl.ds(b, n), :] = flats[pl.ds(b, n), :].astype(F32)
        relayout(me, wide, refs, name)

    codes = jnp.where(pad[...] > 0, seg[...], -1).astype(F32)
    mine = seg[:, tile(s, 256)].astype(F32)
    for j in range(8):
        column = jnp.broadcast_to(codes[:, j * 128:(j + 1) * 128], (128, 128)).T
        for i in range(2):
            row = jnp.broadcast_to(mine[:, i * 128:(i + 1) * 128], (128, 128))
            mask[pl.ds(j * 128, 128), pl.ds(i * 128, 128)] = jnp.where(column == row, 0.0, -1e9)

    tick()
    xr[1].wait_recv()
    xs[2].start()
    g.arrived("attn0")
    g.arrived("attn1")
    xr[0].wait_recv()
    xr[2].wait_recv()
    put(wa, to_a)
    for j in range(4):
        xt[:, pl.ds(j * 256, 256)] = xall[pl.ds(j * 256, 256), :].T

    for c in range(2):
        smf[c] = wa[:, pl.ds(c * WIDE + 1536, 128)].astype(F32)
    vec[...] = jnp.zeros_like(vec)
    for i in range(8):
        vec[pl.ds(i, 1), :] = spread([smf[c, pl.ds(i, 16, stride=48), :] for c in range(2)], 24, 768)
    vecu[...] = spread([smf[c, pl.ds(8, 16, stride=48), :] for c in range(2)], 96, 3072)

    tick()
    for j in range(3):
        w = pl.ds(j * 256, 256)
        hq8[:, w] = ((nn(x[...], wa[:, w]) + vec[0:1, w]).astype(BF).astype(F32) * 0.125).astype(BF)
    for j in range(3):
        w = pl.ds(j * 256, 256)
        for r in range(2):
            rows = pl.ds(r * 512, 512)
            tick()
            k = nn(xall[rows, :], wa[:, pl.ds(768 + j * 256, 256)]).astype(BF)
            kk[rows, w] = k
            kt[w, rows] = k.T
            v = (nn(xall[rows, :], wa[:, pl.ds(WIDE + j * 256, 256)]) + vec[1:2, w]).astype(BF)
            vv[rows, w] = v
            vt[w, rows] = v.T
    put(hq8, to_q8)
    put(xt, to_xt)
    put(vv, to_v)
    put(kt, to_kt)

    for p in range(PAIRS):
        w = pl.ds(p * 128, 128)
        qm = head_rows(hq8[:, w], 0)
        tick()
        top = jnp.full((8, 512), -3e38, F32)
        for c in range(4):
            rows = pl.ds(c * 256, 256)
            one = mask[rows, :]
            v = nt(kk[rows, w], qm) + jnp.concatenate([one, one], 1)
            st[rows, :] = v
            top = jnp.maximum(top, jnp.max(v.reshape(32, 8, 512), 0))
        top = jnp.max(top, 0, keepdims=True)
        tick()
        total = jnp.zeros((8, 512), F32)
        for c in range(8):
            rows = pl.ds(c * 128, 128)
            v = jnp.exp(st[rows, :] - top)
            ee[p, rows, :] = v.astype(BF)
            total = total + jnp.sum(v.reshape(16, 8, 512), 0)
        inverse = 1.0 / jnp.sum(total, 0, keepdims=True)
        hr[pl.ds(p, 1), :] = inverse
        tick()
        for h in range(2):
            o = nn(vt[pl.ds(p * 128 + h * 64, 64), :], ee[p, :, pl.ds(h * 256, 256)])
            hot[pl.ds(p * 128 + h * 64, 64), :] = (o * inverse[:, h * 256:(h + 1) * 256]).astype(BF)
        put(ee.at[p], to_e.at[p])

    tick()
    put(hot, to_ot)
    put(hr, to_r)
    n2[...] = tn(hot[...], wa[:, pl.ds(WIDE + 768, 768)])
    tick()
    for r in range(8):
        rows = pl.ds(r * 32, 32)
        value = x[rows, :].astype(F32) + n2[rows, :] + vec[2:3, :]
        centred = value - jnp.mean(value, -1, keepdims=True)
        r1 = lax.rsqrt(jnp.mean(centred * centred, -1, keepdims=True) + EPS)
        n1 = centred * r1
        hn1[rows, :] = n1
        hr1[rows, :] = jnp.broadcast_to(r1, (32, 128))
        normed = n1 * vec[3:4, :] + vec[4:5, :]
        n2[rows, :] = normed
        nl[rows, :] = normed.astype(BF)
    hnlt[...] = nl[...].T
    put(hnlt, to_nlt)
    put(hn1, to_n1)
    put(hr1, to_r1)
    for p in ("attn0", "attn1"):
        g.drain(p)
    tick()
    g.arrived("up0")
    g.arrived("up1")
    put(wu, to_u)

    for j in range(12):
        w = pl.ds(j * 256, 256)
        if j:
            tick()
        before = nn(nl[...], wu[:, w]) + vecu[:, w]
        phi = 0.5 * (1.0 + lax.erf(before * 0.7071067811865476))
        a = (before * phi).astype(BF)
        act[:, w] = a
        hactt[w, :] = a.T
        hgp[:, w] = (phi + before * 0.3989422804014327 * jnp.exp(-0.5 * before * before)).astype(BF)

    tick()
    g.drain("up0")
    g.drain("up1")
    g.arrived("down0")
    g.arrived("down1")
    put(hactt, to_actt)
    put(hgp, to_gp)
    put(wd, to_d)

    for j in range(3):
        w = pl.ds(j * 256, 256)
        n2[:, w] += nn(act[...], wd[:, :, w].reshape(3072, 256)) + vec[5:6, w]
    hsm[...] = jnp.zeros_like(hsm)
    hsm[2:3, :] = vec[3:4, :]
    kept = keep[...] > 0
    gain = jnp.zeros((8, 768), F32)
    shift = jnp.zeros((8, 768), F32)
    for r in range(8):
        rows = pl.ds(r * 32, 32)
        value = n2[rows, :]
        centred = value - jnp.mean(value, -1, keepdims=True)
        r2 = lax.rsqrt(jnp.mean(centred * centred, -1, keepdims=True) + EPS)
        n = centred * r2
        out[rows, :] = jnp.where(kept, n * vec[6:7, :] + vec[7:8, :], x[rows, :].astype(F32)).astype(BF)
        grad = jnp.where(kept, cot[rows, :].astype(F32), 0.0)
        gain = gain + jnp.sum((grad * n).reshape(4, 8, 768), 0)
        shift = shift + jnp.sum(grad.reshape(4, 8, 768), 0)
        c = grad * vec[6:7, :]
        hgs[rows, :] = r2 * (c - jnp.mean(c, -1, keepdims=True) - n * jnp.mean(c * n, -1, keepdims=True))
    hsm[0:1, :] = jnp.sum(gain, 0, keepdims=True)
    hsm[1:2, :] = jnp.sum(shift, 0, keepdims=True)
    put(out, to_out)
    put(hgs, to_gs)
    put(hsm, to_sm)

    g.drain("down0")
    g.drain("down1")
    for c in swaps:
        c.wait_send()
    for c in xs:
        c.wait_send()
    for o in outs:
        o.wait()


FORWARD_OUT = (
    ((256, 768), BF), ((768, 2 * WIDE), BF), ((768, 3072), BF), ((16, 192, 768), BF), ((768, 1024), BF),
    ((1024, 768), BF), ((768, 1024), BF), ((PAIRS, 1024, 512), BF), ((256, 768), BF), ((768, 256), BF),
    ((8, 512), F32), ((3072, 256), BF), ((256, 3072), BF), ((768, 256), BF), ((256, 768), F32), ((256, 128), F32),
    ((256, 768), F32), ((8, 768), F32),
)


def forward_call(fq, fo, fu, fd, fs, x, cot, seg, pad, keep):
    a = pl.BlockSpec(memory_space=pl.ANY)
    v = pl.BlockSpec(memory_space=pltpu.VMEM)
    n = len(PARTS)
    dma = pltpu.SemaphoreType.DMA
    return pl.pallas_call(
        forward_kernel,
        out_shape=[jax.ShapeDtypeStruct(s, d) for s, d in FORWARD_OUT],
        in_specs=[v] * 10,
        out_specs=[a] * len(FORWARD_OUT),
        scratch_shapes=[
            pltpu.VMEM((1728, 128), BF), pltpu.VMEM((2, 1728, 128), F32),
            pltpu.VMEM((768, 2 * WIDE), BF), pltpu.VMEM((768, 3072), BF),
            pltpu.VMEM((16, 192, 768), BF), pltpu.VMEM((2, 768, 128), F32),
            pltpu.VMEM((1024, 768), BF), pltpu.VMEM((1024, 768), BF), pltpu.VMEM((1024, 768), BF),
            pltpu.VMEM((768, 1024), BF), pltpu.VMEM((768, 1024), BF), pltpu.VMEM((1024, 512), F32),
            pltpu.VMEM((PAIRS, 1024, 512), BF), pltpu.VMEM((1024, 256), F32), pltpu.VMEM((8, 768), F32),
            pltpu.VMEM((1, 3072), F32), pltpu.VMEM((256, 768), F32), pltpu.VMEM((768, 1024), BF),
            pltpu.VMEM((256, 3072), BF), pltpu.VMEM((256, 768), BF),
            pltpu.VMEM((256, 768), BF), pltpu.VMEM((256, 768), BF), pltpu.VMEM((768, 256), BF),
            pltpu.VMEM((8, 512), F32), pltpu.VMEM((3072, 256), BF), pltpu.VMEM((256, 3072), BF),
            pltpu.VMEM((768, 256), BF), pltpu.VMEM((256, 768), F32), pltpu.VMEM((256, 128), F32),
            pltpu.VMEM((256, 768), F32), pltpu.VMEM((8, 768), F32),
            dma((4,)), dma((4,)), dma((n, 16, 4)), dma((n, 16)), dma((n,)), dma((n,)), dma((24,)), dma((3,)), dma((3,)),
        ],
        compiler_params=pltpu.CompilerParams(collective_id=1, has_side_effects=True, vmem_limit_bytes=62 << 20),
        name="forward",
    )(fq, fo, fu, fd, fs, x, cot, seg, pad, keep)


RPARTS = (
    ("down0", 3, "zyx", 96, 0, 0, 384),
    ("down1", 3, "xzy", 96, 96, 0, 384),
    ("up0", 2, "zxy", 48, 0, 0, 768),
    ("up1", 2, "yzx", 48, 0, 768, 768),
    ("out", 1, "yzx", 48, 0, 0, 384),
    ("qkv0", 0, "zxy", 48, 0, 0, 384),
    ("qkv1", 0, "yzx", 48, 0, 384, 384),
    ("qkv2", 0, "zxy", 48, 0, 768, 384),
)
HALF = (1152, 384, 1536, 384)
CHIPROWS = (48, 48, 48, 192)
ROWS = (768, 768, 768, 3072)
SIZES = {"x": 2, "y": 2, "z": 4}
LINKS = ("up", "down", "x", "y")


def slots(order, axis):
    n = 4 if axis == "z" else 1
    for a in order[: order.index(axis)]:
        n *= SIZES[a]
    return n


def landing_shapes():
    shapes = []
    for name, mat, order, rows, ro, co, cols in RPARTS:
        for way in LINKS:
            axis = "z" if way in ("up", "down") else way
            shapes.append(pltpu.VMEM((slots(order, axis), rows, cols), BF))
    return shapes


class Scatter:
    def __init__(self, me, grads, half, lands, finals, send, recv):
        self.me, self.grads, self.half, self.lands, self.finals = me, grads, half, lands, finals
        self.send, self.recv = send, recv

    def chip(self, x, y, z):
        return (z * 2 + x) * 2 + y

    def part(self, refs, i, dest):
        name, mat, order, rows, ro, co, cols = RPARTS[i]
        first = pl.multiple_of(self.chip(*dest) * CHIPROWS[mat] + ro, 16)
        return refs[mat].at[pl.ds(first, rows), pl.ds(co, cols)]

    def block(self, i, dest):
        return self.part(self.grads, i, dest)

    def slot(self, i, way, dest):
        order = RPARTS[i][2]
        axis = "z" if way in ("up", "down") else way
        coords = dict(zip("xyz", dest))
        index = coords["z"] if axis == "z" else 0
        for a in order[: order.index(axis)]:
            index = index * SIZES[a] + coords[a]
        return index

    def land(self, i, way, dest):
        return self.lands[i * 4 + LINKS.index(way)].at[self.slot(i, way, dest)]

    def copy(self, i, way, dest):
        chip = self.chip(*dest)
        return pltpu.make_async_remote_copy(
            self.block(i, dest), self.land(i, way, dest), self.send.at[i, chip],
            self.recv.at[i, LINKS.index(way), chip], device_id=self.me.to(way), device_id_type=MESH)

    def stage(self, i, fx, fy, k):
        moved = {"x": fx, "y": fy, "z": k}
        return max(s for s in range(3) if moved[RPARTS[i][2][s]])

    def take(self, i, way, dest):
        self.copy(i, way, dest).wait_recv()
        ref = self.block(i, dest)
        ref[...] = (ref[...].astype(F32) + self.land(i, way, dest)[...].astype(F32)).astype(BF)

    def total(self, i, dest, ways):
        value = self.block(i, dest)[...].astype(F32) + self.part(self.half, i, dest)[...].astype(F32)
        for way in ways:
            self.copy(i, way, dest).wait_recv()
            value = value + self.land(i, way, dest)[...].astype(F32)
        return value

    def serve(self, i, fx, fy, k):
        me = self.me
        order = RPARTS[i][2]
        stage = self.stage(i, fx, fy, k)
        axis = order[stage]

        def act(dest, sign):
            way = axis
            if axis == "z":
                way, more = ("down", me.z < 3) if sign < 0 else ("up", me.z > 0)
                pl.when(more)(lambda: self.take(i, way, dest))
            if "z" in order[stage + 1:]:
                pl.when(me.z < 3)(lambda: self.take(i, "down", dest))
                pl.when(me.z > 0)(lambda: self.take(i, "up", dest))
            value = self.total(i, dest, [a for a in order[stage + 1:] if a != "z"])
            self.block(i, dest)[...] = value.astype(BF)
            self.copy(i, way, dest).start()

        self.dests(fx, fy, k, act)

    def dests(self, fx, fy, k, act):
        me = self.me
        x = 1 - me.x if fx else me.x
        y = 1 - me.y if fy else me.y
        if k == 0:
            act((x, y, me.z), 0)
        else:
            pl.when(me.z >= k)(lambda: act((x, y, me.z - k), -1))
            pl.when(me.z + k <= 3)(lambda: act((x, y, me.z + k), 1))

    def own(self, i):
        dest = (self.me.x, self.me.y, self.me.z)
        name, mat, order, rows, ro, co, cols = RPARTS[i]
        self.finals[mat].at[pl.ds(ro, rows), pl.ds(co, cols)][...] = self.total(i, dest, ())

    def finish(self, i):
        name, mat, order, rows, ro, co, cols = RPARTS[i]
        me = self.me
        dest = (me.x, me.y, me.z)
        fin = self.finals[mat].at[pl.ds(ro, rows), pl.ds(co, cols)]

        def add(way):
            self.copy(i, way, dest).wait_recv()
            fin[...] += self.land(i, way, dest)[...].astype(F32)
        for axis in order:
            if axis == "z":
                pl.when(me.z < 3)(lambda: add("down"))
                pl.when(me.z > 0)(lambda: add("up"))
            else:
                add(axis)

    def drain(self, i):
        for fx in (0, 1):
            for fy in (0, 1):
                for k in range(4):
                    if fx + fy + k:
                        axis = RPARTS[i][2][self.stage(i, fx, fy, k)]
                        self.dests(fx, fy, k, lambda dest, sign: self.copy(
                            i, axis if axis != "z" else ("down" if sign < 0 else "up"), dest).wait_send())


SCATTER_PLAN = (
    (), (), (), (28, 12, 30, 31), (), (), (), (), (), (), (), (), (), (), (), (23, 22, 59, 13, 9, 15, 46, 11, 27, 36),
    (), (), (), (), (), (), (), (), (), (63, 47, 7, 79, 78, 19), (),
    (58, 44, 10, 55, 4, 14, 51, 5, 43, 75, 39, 8, 71), (), (), (), (), (), (), (),
    (42, 61, 26, 62, 45, 77, 3, 50, 74, 70), (), (), (), (), (), (), (), (29, 94, 21, 86, 95, 57, 6, 35), (), (), (),
    (), (), (), (), (), (), (), (), (18, 105, 92, 93, 41, 54, 87, 108, 91), (), (), (), (),
    (20, 69, 2, 107, 38, 111, 25), (), (), (), (),
    (117, 124, 67, 125, 119, 106, 40, 1, 127, 109, 17, 83, 99, 37, 103, 56, 85, 126), (), (), (),
    (24, 110, 116, 121, 34, 73, 123, 118, 53, 84, 49, 66, 98, 60), (), (), (115, 120, 122, 102, 90, 33), (),
    (114, 89, 101, 88, 76, 82, 65, 52), (97, 100, 72, 113, 104, 68, 81, 0, 48, 16, 32, 112, 96, 64, 80),
)

FLATROWS = ((24, 18, 432), (24, 6, 144), (24, 24, 576), (96, 6, 576))


def column(mat, c, j):
    if mat:
        return c * (FLATROWS[mat][1] // 2) + j
    group, t = j // 3, j % 3
    if c == 0:
        return 2 * group + t if t < 2 else 6 + 2 * group
    return 7 + 2 * group if t == 0 else 11 + 2 * group + t


def flatten(me, mat, finals, sides, out):
    rows, tiles, lines = FLATROWS[mat]
    half = tiles // 2
    for c in range(2):
        @pl.when(me.c == c)
        def _():
            for j in range(half):
                mine = finals[mat][pl.ds(pl.multiple_of(me.c * rows, 8), rows), pl.ds(j * 128, 128)]
                out[pl.ds(column(mat, c, j), rows, stride=tiles), :] = mine
                out[pl.ds(column(mat, 1 - c, j), rows, stride=tiles), :] = sides[mat][:, pl.ds(j * 128, 128)]


def colsum(array):
    return jnp.sum(array.astype(F32), 0, keepdims=True)


def backward_kernel(
    ha, hu, hd, hxt, hv, hkt, he, *rest,
):
    far, keep, rest = rest[:11], rest[11], rest[12:]
    (ingrad, oq, oo, ou, od, chosen), rest = rest[:6], rest[6:]
    near, rest = rest[:11], rest[11:]
    q8, ot, rr, actt, gp, nlt, n1, r1, gs, sm0, cot = near
    lands, rest = rest[:32], rest[32:]
    grads, rest = rest[:4], rest[4:]
    stage, rest = rest[:3], rest[3:]
    stage = (stage[1].at[:, pl.ds(0, HALF[0])],) + tuple(stage)
    half, rest = rest[:4], rest[4:]
    finals, rest = rest[:4], rest[4:]
    sides, rest = rest[:4], rest[4:]
    (wbig, wo, xt, vv, kt, ee, ds, gbr, gbef, first, gts, gsa, dq, dkv, dx, dxc, dxy, acc, sland, osm,
     nsem, wsem, isem, esem, csend, crecv, send, recv, fsend, frecv, dsend, drecv, asend, arecv) = rest
    me = Place()
    s = me.y * 2 + me.c
    wds = [pltpu.make_async_copy(hd.at[pl.ds(q * 768, 768), :], wbig.at[pl.ds(q * 768, 768), :], wsem.at[q]) for q in range(4)]
    wus = [pltpu.make_async_copy(hu.at[:, pl.ds(q * 768, 768)], wbig.at[pl.ds(q * 768, 768), :], wsem.at[4 + q]) for q in range(4)]
    wqs = [pltpu.make_async_copy(ha.at[:, pl.ds((0, 768, WIDE)[q], 768)], wbig.at[pl.ds(q * 768, 768), :], wsem.at[8 + q]) for q in range(3)]
    others = [pltpu.make_async_copy(a, b, isem.at[i]) for i, (a, b) in enumerate(((ha.at[:, pl.ds(WIDE + 768, 768)], wo), (hv, vv), (hkt, kt), (hxt, xt)))]
    ees = [pltpu.make_async_copy(he.at[p], ee.at[p % 2], esem.at[p]) for p in range(PAIRS)]
    nears = [pltpu.make_async_copy(a, b, nsem.at[i]) for i, (a, b) in enumerate(zip(far, near))]
    for i in (8, 9, 3):
        nears[i].start()
    for c in wds:
        c.start()
    for i in (4, 5, 6, 7, 1, 2, 0, 10):
        nears[i].start()
    for c in others:
        c.start()
    ees[0].start()
    ees[1].start()
    enter(me)

    sc = Scatter(me, grads, half, lands, finals, send, recv)

    def swap(mat, group=None):
        src, dst, n = stage[mat], half[mat], 3 + mat
        if mat == 0:
            src, dst, n = src.at[:, pl.ds(group * 384, 384)], dst.at[:, pl.ds(group * 384, 384)], group
        return pltpu.make_async_remote_copy(
            src, dst, csend.at[n], crecv.at[n], device_id=me.to("core"), device_id_type=MESH)

    slot = iter(SCATTER_PLAN)

    def tick():
        for code in next(slot, ()):
            i, fx, fy, k = code // 16, code // 8 % 2, code // 4 % 2, code % 4
            if fx + fy + k:
                sc.serve(i, fx, fy, k)
            else:
                sc.own(i)
                sc.finish(i)

    def arrange(value_ref, to):
        to[:, 0:384] = value_ref[:, pl.ds(pl.multiple_of(me.c * 384, 128), 384)]
        to[:, 384:768] = value_ref[:, pl.ds(pl.multiple_of((1 - me.c) * 384, 128), 384)]

    osm[...] = jnp.zeros_like(osm)
    for i in (8, 9):
        nears[i].wait()
    osm[6:8, :] = sm0[0:2, :]
    gsa[...] = gs[...].astype(BF)
    osm[5:6, :] = colsum(gsa[...])
    arrange(gsa, gbr)
    nears[3].wait()

    for j in range(12):
        w = pl.ds(j * 256, 256)
        v = nn(actt[w, :], gbr[...]).astype(BF)
        grads[3][w, :] = v[:, 0:384]
        stage[3][w, :] = v[:, 384:768]
    swap(3).start()

    nears[4].wait()
    for q in range(4):
        wds[q].wait()
        for j in range(3):
            w = pl.ds(q * 768 + j * 256, 256)
            ga = nt(gsa[...], wbig[w, :]).astype(BF).astype(F32)
            gb = (ga * gp[:, w].astype(F32)).astype(BF)
            gbef[:, w] = gb
            osm[8 + q:9 + q, pl.ds(j * 256, 256)] = colsum(gb)
        wus[q].start()
    swap(3).wait_recv()
    tick()

    for i in (5, 6, 7, 1, 2, 0, 10):
        nears[i].wait()
    for j in range(6):
        w = pl.ds(j * 256, 256)
        tick()
        stage[2][:, w] = nn(nlt[...], gbef[:, pl.ds(pl.multiple_of((1 - me.c) * 1536 + j * 256, 256), 256)]).astype(BF)
    swap(2).start()
    for j in range(6):
        w = pl.ds(j * 256, 256)
        tick()
        grads[2][:, w] = nn(nlt[...], gbef[:, pl.ds(pl.multiple_of(me.c * 1536 + j * 256, 256), 256)]).astype(BF)
    for c in wus:
        c.wait()
    tick()
    swap(2).wait_recv()

    for j in range(3):
        w = pl.ds(j * 256, 256)
        tick()
        total = gs[:, w]
        for q in range(4):
            total += nt(gbef[:, pl.ds(q * 768, 768)], wbig[pl.ds(q * 768 + j * 256, 256), :])
        first[:, w] = total
    for c in wqs:
        c.start()

    gain = jnp.zeros((8, 768), F32)
    shift = jnp.zeros((8, 768), F32)
    for r in range(8):
        rows = pl.ds(r * 32, 32)
        if r % 4 == 0:
            tick()
        gn = first[rows, :]
        n = n1[rows, :]
        gain = gain + jnp.sum((gn * n).reshape(4, 8, 768), 0)
        shift = shift + jnp.sum(gn.reshape(4, 8, 768), 0)
        c1 = gn * sm0[2:3, :]
        gf = r1[rows, 0:1] * (c1 - jnp.mean(c1, -1, keepdims=True) - n * jnp.mean(c1 * n, -1, keepdims=True))
        first[rows, :] = gf
        gsa[rows, :] = gf.astype(BF)
    osm[3:4, :] = jnp.sum(gain, 0, keepdims=True)
    osm[4:5, :] = jnp.sum(shift, 0, keepdims=True)
    osm[2:3, :] = colsum(gsa[...])
    arrange(gsa, gbr)
    tick()

    for j in range(3):
        w = pl.ds(j * 256, 256)
        v = nn(ot[w, :], gbr[...]).astype(BF)
        grads[1][w, :] = v[:, 0:384]
        stage[1][w, :] = v[:, 384:768]
    swap(1).start()
    for c in others:
        c.wait()
    for p in range(PAIRS):
        w = pl.ds(p * 128, 128)
        if p % 2 == 0:
            tick()
        g = nt(wo[w, :], gsa[...]).astype(BF).astype(F32)
        scale = jnp.concatenate(
            [jnp.broadcast_to(rr[p:p + 1, h * 256:(h + 1) * 256], (64, 256)) for h in range(2)], 0)
        gts[w, :] = (g * scale).astype(BF)
    swap(1).wait_recv()

    mine = xt.at[:, tile(s, 256)]

    def qkv_grads(group):
        q = pl.ds(group * 256, 256)
        v = pl.ds(768 + group * 256, 256)
        mid = pl.ds(group * 384, 384)

        def put(r, a, b):
            rows = pl.ds(r * 256, 256)
            vq = nn(mine[rows, :], dq[:, q]).astype(BF)
            vk = nn(xt[rows, :], dkv[:, q]).astype(BF)
            vv_ = nn(xt[rows, :], dkv[:, v]).astype(BF)
            a[rows, pl.ds(group * 384, 256)] = vq
            a[rows, pl.ds(group * 384 + 256, 128)] = vk[:, 0:128]
            b[rows, pl.ds(group * 384, 128)] = vk[:, 128:256]
            b[rows, pl.ds(group * 384 + 128, 256)] = vv_

        for r in range(3):
            tick()
            pl.when(me.c == 0)(lambda: put(r, grads[0], stage[0]))
            pl.when(me.c == 1)(lambda: put(r, stage[0], grads[0]))
        swap(0, group).start()

    for p in range(PAIRS):
        w = pl.ds(p * 128, 128)
        g = gts[w, :]
        both = ot[w, :].astype(F32) * g.astype(F32)
        delta = jnp.concatenate([jnp.sum(both[0:64], 0, keepdims=True), jnp.sum(both[64:128], 0, keepdims=True)], 1)
        gm = head_rows(g.T, 0)
        qm = head_rows(q8[:, w], 0)
        ees[p].wait()
        e = ee.at[p % 2]
        for c in range(4):
            rows = pl.ds(c * 256, 256)
            if c % 2 == 0:
                tick()
            dp = nt(vv[rows, w], gm)
            ds[rows, :] = (e[rows, :].astype(F32) * (dp - delta)).astype(BF)
        tick()
        dkv[:, w] = nn(ds[...], qm).astype(BF)
        tick()
        dkv[:, pl.ds(768 + p * 128, 128)] = nn(e[...], gm).astype(BF)
        tick()
        dqt = jnp.concatenate([
            nn(kt[pl.ds(p * 128 + h * 64, 64), :], ds[:, pl.ds(h * 256, 256)]) for h in range(2)], 0)
        dq[:, w] = (dqt * 0.125).astype(BF).T
        if p + 2 < PAIRS:
            ees[p + 2].start()
        if p == 1:
            swap(2).wait_send()
        if p % 2:
            qkv_grads(p // 2)
        if p in (2, 4):
            swap(0, p // 2 - 1).wait_recv()
            tick()

    osm[0:1, :] = colsum(dq[...])
    osm[1:2, :] = colsum(dkv[:, pl.ds(768, 768)])

    for c in wqs:
        c.wait()

    for j in range(3):
        w = pl.ds(j * 256, 256)
        for r in range(2):
            rows = pl.ds(r * 512, 512)
            if j == 0 and r == 1:
                swap(0, 2).wait_recv()
            tick()
            dx[rows, w] = (
                nt(dkv[rows, 0:768], wbig[pl.ds(768 + j * 256, 256), :])
                + nt(dkv[rows, 768:1536], wbig[pl.ds(1536 + j * 256, 256), :])).astype(BF)
        first[:, w] += nt(dq[...], wbig[w, :])

    def dx_copy(n):
        if n < 2:
            yy = me.y if n == 0 else 1 - me.y
            return pltpu.make_async_remote_copy(
                dx.at[tile(yy * 2 + 1 - me.c, 256), :], dxc.at[n], dsend.at[n], drecv.at[n],
                device_id=me.to("core"), device_id_type=MESH)
        return pltpu.make_async_remote_copy(
            dx.at[tile((1 - me.y) * 2 + me.c, 256), :], dxy, dsend.at[2], drecv.at[2],
            device_id=me.to("y"), device_id_type=MESH)
    dx_copy(1).start()
    dx_copy(0).start()
    dx_copy(1).wait_recv()
    over = tile((1 - me.y) * 2 + me.c, 256)
    dx[over, :] = (dx[over, :].astype(F32) + dxc[1].astype(F32)).astype(BF)
    dx_copy(2).start()

    acc[0] = osm[...]
    pairz = {"outer": (me.z + 1 - 2 * (me.z % 2)) * 2 + me.x}
    smalls = [
        pltpu.make_async_remote_copy(acc.at[i], sland.at[i], asend.at[i], arecv.at[i], device_id=to, device_id_type=MESH)
        for i, to in enumerate((me.to("core"), me.to("x"), me.to("y"), pairz, me.to("far")))
    ]
    smalls[0].start()

    def small_step(i):
        smalls[i].wait_recv()
        acc[i + 1] = acc[i] + sland[i]
        if i < 4:
            smalls[i + 1].start()

    for i in range(5):
        tick()
        small_step(i)
    tick()
    owner = ((me.z * 2 + me.x) * 4 + s).astype(F32)
    at = lax.broadcasted_iota(jnp.int32, (768, 128), 0).astype(F32)
    lane = lax.broadcasted_iota(jnp.int32, (768, 128), 1).astype(F32)

    def choose(rows, start, size):
        pick = jnp.where((at == start + lane) & (lane < size), 1.0, 0.0)
        return jnp.dot(rows, pick, precision=lax.Precision.HIGHEST, preferred_element_type=F32)
    up = jnp.zeros((8, 128), F32)
    for q in range(4):
        up = up + choose(acc[5, 8 + q:9 + q, :], owner * 96 - q * 768, 96)
    chosen[0:8, :] = choose(acc[5, 0:8, :], owner * 24, 24)
    chosen[8:16, :] = up
    lasts = []
    for mat in range(4):
        rows = FLATROWS[mat][0]
        src = finals[mat].at[pl.ds(pl.multiple_of((1 - me.c) * rows, 8), rows), :]
        lasts.append(pltpu.make_async_remote_copy(
            src, sides[mat], fsend.at[mat], frecv.at[mat], device_id=me.to("core"), device_id_type=MESH))
        lasts[-1].start()
    dx_copy(0).wait_recv()
    dx_copy(2).wait_recv()
    total = first[...] + dx[tile(s, 256), :].astype(F32) + dxc[0].astype(F32) + dxy[...].astype(F32)
    ingrad[...] = jnp.where(keep[...] > 0, total, cot[...].astype(F32)).astype(BF)
    for i in range(8):
        sc.drain(i)
    for mat in (3, 1):
        swap(mat).wait_send()
    for group in range(3):
        swap(0, group).wait_send()
    for n in range(3):
        dx_copy(n).wait_send()
    for c in smalls:
        c.wait_send()
    for mat, c in enumerate(lasts):
        c.wait()
        flatten(me, mat, finals, sides, (oq, oo, ou, od)[mat])


def backward_call(*args):
    a = pl.BlockSpec(memory_space=pl.ANY)
    v = pl.BlockSpec(memory_space=pltpu.VMEM)
    dma = pltpu.SemaphoreType.DMA
    outs = [((256, 768), BF)] + [((FLATROWS[m][2], 128), F32) for m in range(4)] + [((16, 128), F32)]
    halves = [(ROWS[m], HALF[m]) for m in range(4)]
    return pl.pallas_call(
        backward_kernel,
        out_shape=[jax.ShapeDtypeStruct(s, d) for s, d in outs],
        in_specs=[a] * 18 + [v],
        out_specs=[v] * 6,
        scratch_shapes=[pltpu.VMEM(s, d) for s, d in FORWARD_OUT[8:]] + [pltpu.VMEM((256, 768), BF)]
        + landing_shapes()
        + [pltpu.VMEM(h, BF) for h in halves + halves[1:] + halves]
        + [pltpu.VMEM((CHIPROWS[m], HALF[m]), F32) for m in range(4)]
        + [pltpu.VMEM((FLATROWS[m][0], HALF[m]), F32) for m in range(4)]
        + [
            pltpu.VMEM((3072, 768), BF), pltpu.VMEM((768, 768), BF), pltpu.VMEM((768, 1024), BF),
            pltpu.VMEM((1024, 768), BF), pltpu.VMEM((768, 1024), BF), pltpu.VMEM((2, 1024, 512), BF),
            pltpu.VMEM((1024, 512), BF), pltpu.VMEM((256, 768), BF), pltpu.VMEM((256, 3072), BF),
            pltpu.VMEM((256, 768), F32), pltpu.VMEM((768, 256), BF), pltpu.VMEM((256, 768), BF),
            pltpu.VMEM((256, 768), BF), pltpu.VMEM((1024, 1536), BF), pltpu.VMEM((1024, 768), BF),
            pltpu.VMEM((2, 256, 768), BF), pltpu.VMEM((256, 768), BF), pltpu.VMEM((6, 16, 768), F32),
            pltpu.VMEM((5, 16, 768), F32), pltpu.VMEM((16, 768), F32),
            dma((11,)), dma((11,)), dma((4,)), dma((PAIRS,)), dma((7,)), dma((7,)), dma((8, 16)), dma((8, 4, 16)),
            dma((4,)), dma((4,)), dma((3,)), dma((3,)), dma((5,)), dma((5,)),
        ],
        compiler_params=pltpu.CompilerParams(collective_id=2, has_side_effects=True, vmem_limit_bytes=63 << 20),
        name="backward",
    )(*args)


SMALL_SIZES = (24,) * 8 + (96,)


def finish_kernel(*refs):
    ins, small, outs, smalls = refs[:6], refs[6], refs[7:13], refs[13:22]
    for a, b in zip(ins, outs):
        b[...] = a[...]
    for i, (to, size) in enumerate(zip(smalls, SMALL_SIZES)):
        to[...] = small[i, 0:size]


def finish_call(*args):
    v = pl.BlockSpec(memory_space=pltpu.VMEM)
    return pl.pallas_call(
        finish_kernel,
        out_shape=[jax.ShapeDtypeStruct(x.shape, x.dtype) for x in args[:6]]
        + [jax.ShapeDtypeStruct((size,), F32) for size in SMALL_SIZES],
        in_specs=[v] * 7,
        out_specs=[v] * 15,
        name="finish",
    )(*args)


AXES = ("outer", "inner", "seq")
SMALLS = (1, 2, 4, 5, 6, 10, 11, 12, 8)


def to_part(flat):
    inner = lax.axis_size("inner")
    if inner == 1:
        return flat
    every = lax.all_gather(flat, ("inner", "seq"), axis=0, tiled=True)
    size = flat.shape[0] * inner
    return lax.dynamic_slice_in_dim(every, lax.axis_index("seq") * size, size, 0)


def whole_scatter(part):
    inner = lax.axis_size("inner")
    if inner == 1:
        return part
    every = lax.psum(lax.all_gather(part, "seq", axis=0, tiled=True), "inner")
    size = part.shape[0] // inner
    index = lax.axis_index("inner") * lax.axis_size("seq") + lax.axis_index("seq")
    return lax.dynamic_slice_in_dim(every, index * size, size, 0)


def shards(inputs, *rest):
    params, (cotangent, segment_ids, pad_mask, keep_flag) = rest[:13], rest[13:]
    parts = [to_part(p) for p in params]
    small = sum(
        jnp.pad(parts[i][None, :], ((row, 15 - row), (0, 128 - parts[i].shape[0])))
        for row, i in enumerate(SMALLS)
    )
    x, cot = inputs[0], cotangent[0]
    keep = keep_flag.reshape(1, 1)
    out, *held = forward_call(
        *(parts[i].reshape(-1, 128) for i in (0, 3, 7, 9)), small, x, cot, segment_ids, pad_mask, keep
    )
    held[2] = held[2].reshape(FF, D)
    grad, *big, small = backward_call(*held, cot, keep)
    out, grad, *rest = finish_call(out, grad, *big, small)
    big = [whole_scatter(part.reshape(-1)) for part in rest[:4]]
    q, v, ob, g1, b1, db, g2, b2, ub = (whole_scatter(part) for part in rest[4:])
    return (out[None], grad[None], big[0], q, v, big[1], ob, g1, b1, big[2], ub, big[3], db, g2, b2)


def solution(mesh):
    fsdp, seq = mesh.shape["fsdp"], mesh.shape["seq"]
    mesh = Mesh(mesh.devices.reshape(8, fsdp // 8, seq), AXES)
    tokens = P(("outer", "inner"), "seq", None)
    flat = P(AXES)
    rows = P(("outer", "inner"), None)
    return jax.shard_map(
        shards,
        mesh=mesh,
        in_specs=(tokens,) + (flat,) * 13 + (tokens, rows, rows, P(("outer", "inner"))),
        out_specs=(tokens, tokens) + (flat,) * 13,
        check_vma=False,
    )
```

```python
import functools
import jax
import jax.numpy as jnp
from jax import lax
from jax.experimental import pallas as pl
from jax.experimental.pallas import tpu as pltpu
from jax.sharding import Mesh, PartitionSpec as P

MESH = pl.DeviceIdType.MESH
D = 768
FF = 3072
BF = jnp.bfloat16
F32 = jnp.float32
LINES = (432, 144, 576, 576)
BASE = (0, 432, 576, 1152)
WIDE = 1664


class Place:
    def __init__(self):
        o = lax.axis_index("outer")
        s = lax.axis_index("seq")
        self.z, self.x, self.y, self.c = o // 2, o % 2, s // 2, s % 2

    def to(self, way):
        z, x, y, c = self.z, self.x, self.y, self.c
        return {
            "up": {"outer": (z + 1) * 2 + x},
            "down": {"outer": (z - 1) * 2 + x},
            "x": {"outer": z * 2 + 1 - x},
            "y": {"seq": (1 - y) * 2 + c},
            "core": {"seq": y * 2 + 1 - c},
            "far": {"outer": (3 - z) * 2 + x},
        }[way]


def enter(me):
    bar = pltpu.get_barrier_semaphore()

    def greet(to):
        pl.semaphore_signal(bar, 1, device_id=to, device_id_type=MESH)

    for way in ("x", "y", "core"):
        greet(me.to(way))
    pl.when(me.z < 3)(lambda: greet(me.to("up")))
    pl.when(me.z > 0)(lambda: greet(me.to("down")))
    pl.when((me.z == 0) | (me.z == 3))(lambda: greet(me.to("far")))
    pl.semaphore_wait(bar, 5)


WAYS = ("up", "down", "x", "y")

PARTS = (
    ("attn0", "yzx"),
    ("attn1", "zxy"),
    ("up0", "zyx"),
    ("up1", "xzy"),
    ("down0", "xzy"),
    ("down1", "yzx"),
)
LATE = ("down0", "down1")
NAMES = [p[0] for p in PARTS]
ORDER = dict(PARTS)


class Gather:
    def __init__(self, me, refs, send, recv, csend, crecv, lsend, lrecv):
        self.me = me
        self.refs = refs
        self.send, self.recv, self.csend, self.crecv = send, recv, csend, crecv
        self.lsend, self.lrecv = lsend, lrecv

    def block(self, part, chip, c):
        wa, wu, wd = self.refs
        m = pl.multiple_of
        if part == "down0":
            return wd.at[chip, pl.ds(0, 96), pl.ds(m(c * 384, 128), 384)]
        if part == "down1":
            return wd.at[chip, pl.ds(96, 96), pl.ds(m(c * 384, 128), 384)]
        rows = pl.ds(m(chip * 48, 16), 48)
        if part == "attn0":
            return wa.at[rows, pl.ds(m(c * WIDE, 128), 768)]
        if part == "attn1":
            return wa.at[rows, pl.ds(m(c * WIDE + 768, 128), 896)]
        if part == "up0":
            return wu.at[rows, pl.ds(m(c * 1536, 128), 768)]
        return wu.at[rows, pl.ds(m(c * 1536 + 768, 128), 768)]

    def half(self, part, c):
        wa, wu, wd = self.refs
        m = pl.multiple_of
        if part == "down0":
            return wd.at[:, pl.ds(0, 96), pl.ds(m(c * 384, 128), 384)]
        if part == "down1":
            return wd.at[:, pl.ds(96, 96), pl.ds(m(c * 384, 128), 384)]
        if part == "attn0":
            return wa.at[:, pl.ds(m(c * WIDE, 128), 768)]
        if part == "attn1":
            return wa.at[:, pl.ds(m(c * WIDE + 768, 128), 896)]
        if part == "up0":
            return wu.at[:, pl.ds(m(c * 1536, 128), 768)]
        return wu.at[:, pl.ds(m(c * 1536 + 768, 128), 768)]

    def chip(self, x, y, z):
        return (z * 2 + x) * 2 + y

    def copy(self, part, chip, way):
        i = NAMES.index(part)
        ref = self.block(part, chip, self.me.c)
        return pltpu.make_async_remote_copy(
            ref, ref, self.send.at[i, chip, WAYS.index(way)], self.recv.at[i, chip],
            device_id=self.me.to(way), device_id_type=MESH)

    def across(self, part, c):
        i = NAMES.index(part)
        ref = self.half(part, c)
        return pltpu.make_async_remote_copy(
            ref, ref, self.csend.at[i], self.crecv.at[i], device_id=self.me.to("core"), device_id_type=MESH)

    def onward(self, part, chip, axes):
        me = self.me
        for axis in axes:
            if axis == "z":
                pl.when(me.z < 3)(lambda: self.copy(part, chip, "up").start())
                pl.when(me.z > 0)(lambda: self.copy(part, chip, "down").start())
            else:
                self.copy(part, chip, axis).start()

    def own(self, part):
        me = self.me
        chip = self.chip(me.x, me.y, me.z)
        self.onward(part, chip, ORDER[part])
        if part in LATE:
            self.beside(part, chip, me.c).start()

    def origins(self, fx, fy, k, act):
        me = self.me
        x = 1 - me.x if fx else me.x
        y = 1 - me.y if fy else me.y
        if k == 0:
            act(self.chip(x, y, me.z), 0)
        else:
            pl.when(me.z >= k)(lambda: act(self.chip(x, y, me.z - k), -1))
            pl.when(me.z + k <= 3)(lambda: act(self.chip(x, y, me.z + k), 1))

    def arrival(self, part, fx, fy, k):
        moved = {"x": fx, "y": fy, "z": k}
        return max(i for i in range(3) if moved[ORDER[part][i]])

    def serve(self, part, fx, fy, k):
        me = self.me
        order = ORDER[part]
        stage = self.arrival(part, fx, fy, k)
        axis = order[stage]

        def act(chip, sign):
            if axis == "z":
                way, more = ("up", me.z < 3) if sign < 0 else ("down", me.z > 0)
                self.copy(part, chip, way).wait_recv()
                pl.when(more)(lambda: self.copy(part, chip, way).start())
            else:
                self.copy(part, chip, axis).wait_recv()
            self.onward(part, chip, order[stage + 1:])
            if part in LATE:
                self.beside(part, chip, me.c).start()

        self.origins(fx, fy, k, act)

    def beside(self, part, chip, c):
        i = LATE.index(part)
        ref = self.block(part, chip, c)
        return pltpu.make_async_remote_copy(
            ref, ref, self.lsend.at[i, chip], self.lrecv.at[i, chip], device_id=self.me.to("core"), device_id_type=MESH)

    def arrived(self, part):
        if part not in LATE:
            self.across(part, 1 - self.me.c).wait_recv()
            return

        def body(chip, _):
            self.beside(part, chip, 1 - self.me.c).wait_recv()
            return 0
        lax.fori_loop(0, 16, body, 0)

    def drain(self, part):
        me = self.me
        order = ORDER[part]

        if part in LATE:
            def body(chip, _):
                self.beside(part, chip, me.c).wait_send()
                return 0
            lax.fori_loop(0, 16, body, 0)
        else:
            self.across(part, me.c).wait_send()

        def sent(chip, axes, sign):
            for axis in axes:
                if axis == "z":
                    if sign <= 0:
                        pl.when(me.z < 3)(lambda: self.copy(part, chip, "up").wait_send())
                    if sign >= 0:
                        pl.when(me.z > 0)(lambda: self.copy(part, chip, "down").wait_send())
                else:
                    self.copy(part, chip, axis).wait_send()

        for fx in (0, 1):
            for fy in (0, 1):
                for k in range(4):
                    if fx + fy + k == 0:
                        sent(self.chip(me.x, me.y, me.z), order, 0)
                        continue
                    stage = self.arrival(part, fx, fy, k)
                    axes = order[stage:] if order[stage] == "z" else order[stage + 1:]
                    self.origins(fx, fy, k, lambda chip, sign: sent(
                        chip, axes, sign if order[stage] == "z" else 0))


def relayout(me, wide, refs, name):
    m = pl.multiple_of
    chip = (me.z * 2 + me.x) * 2 + me.y
    wa, wu, wd = refs

    def rows(base, count, stride):
        both = [wide[d, pl.ds(base, count, stride=stride), :] for d in range(2)]
        return jnp.concatenate(both, 0).astype(BF)

    if name == "up":
        for j in range(12):
            wu[pl.ds(m(chip * 48, 16), 48), pl.ds(m((me.c * 12 + j) * 128, 128), 128)] = rows(
                BASE[2] + me.c * 12 + j, 24, 24)
    elif name == "down":
        for j in range(3):
            wd[chip, :, pl.ds(m((me.c * 3 + j) * 128, 128), 128)] = rows(BASE[3] + me.c * 3 + j, 96, 6)
    else:
        for j in range(6):
            wa[pl.ds(m(chip * 48, 16), 48), pl.ds(m(me.c * WIDE + j * 128, 128), 128)] = rows(
                BASE[0] + me.c * 12 + j, 24, 18)
            to = wa.at[pl.ds(m(chip * 48, 16), 48), pl.ds(m(me.c * WIDE + 768 + j * 128, 128), 128)]

            @pl.when(me.c == 0)
            def _():
                to[...] = rows(BASE[0] + 6 + j, 24, 18)

            @pl.when(me.c == 1)
            def _():
                to[...] = rows(BASE[1] + j, 24, 6)


GATHER_PLAN = (

    (16, 0, 32, 17, 80, 48, 18, 4, 20, 1, 8, 24, 19, 5, 25, 2, 27, 26, 3, 6, 23, 21, 56, 7, 33, 9, 40, 36, 49, 88, 28, 64, 81, 29, 57, 10, 13, 22, 84, 52, 12, 34, 31, 30, 50, 14, 15, 11),
    (), (), (), (), (), (), (), (), (), (), (), (72, 37), (85, 35, 65, 58), (), (), (), (), (), (), (),
    (89, 44, 73, 82, 53, 61, 60, 38), (), (), (86, 51, 43, 92, 54, 39, 42, 41, 76, 59, 66, 45, 74, 68), (), (), (),
    (69, 90, 93, 83, 55, 62, 46, 63, 67, 87, 47), (), (75,), (), (), (), (), (), (), (), (), (),
    (70, 95, 91, 77, 94, 71, 78, 79),
)

GATHER_X = 0


HEADS = 12
HD = 64
EPS = 1e-05
PAIRS = HEADS // 2

def nt(left, right):
    return lax.dot_general(left, right, (((1,), (1,)), ((), ())), preferred_element_type=F32)


def nn(left, right):
    return jnp.dot(left, right, preferred_element_type=F32)


def tn(left, right):
    return lax.dot_general(left, right, (((0,), (0,)), ((), ())), preferred_element_type=F32)


def tile(i, size):
    return pl.ds(pl.multiple_of(i * size, size), size)


def spread(sides, size, width):
    lane = lax.broadcasted_iota(jnp.int32, (128, width), 0)
    col = lax.broadcasted_iota(jnp.int32, (128, width), 1)
    owner = ((col.astype(F32) + 0.5) * (1.0 / size)).astype(jnp.int32)
    pick = (col - owner * size == lane).astype(F32).astype(BF)
    dev = lax.broadcasted_iota(jnp.int32, (16, width), 0) * 2
    col = lax.broadcasted_iota(jnp.int32, (16, width), 1)
    owner = ((col.astype(F32) + 0.5) * (1.0 / size)).astype(jnp.int32)
    total = jnp.zeros((16, width), F32)
    for c, rows in enumerate(sides):
        total = total + jnp.where(owner == dev + c, nn(rows.astype(BF), pick), 0.0)
    return jnp.sum(total, 0, keepdims=True)


def swap_rows(me, ref, s, send, recv):
    width = 256

    def block(index):
        return ref.at[tile(index, width), :]

    def copy(index, way, n):
        return pltpu.make_async_remote_copy(
            block(index), block(index), send.at[n], recv.at[n], device_id=me.to(way), device_id_type=MESH)

    mine = me.y * 2 + me.c
    over = (1 - me.y) * 2 + me.c
    return (copy(mine, "core", 0), copy(mine, "y", 1), copy(over, "core", 2)), (
        copy(me.y * 2 + 1 - me.c, "core", 0), copy(over, "y", 1), copy((1 - me.y) * 2 + 1 - me.c, "core", 2))


def head_rows(array, axis):
    lane = lax.broadcasted_iota(jnp.int32, array.shape, 1)
    zero = jnp.zeros_like(array)
    return jnp.concatenate([jnp.where(lane < HD, array, zero), jnp.where(lane >= HD, array, zero)], axis)


def forward_kernel(
    fq, fo, fu, fd, s0, s1, s2, s3, s4, s5, s6, s7, s8, x, cot, seg, pad, keep,
    to_out, to_a, to_u, to_d, to_xt, to_v, to_kt, to_e, to_q8, to_ot, to_r, to_actt, to_gp, to_nlt, to_n1, to_r1, to_gs, to_sm,
    flats, wide, wa, wu, wd, smf, xall, kk, vv, kt, vt, st, ee, mask, vec, vecu, n2, xt, act, nl,
    out, hq8, hot, hr, hactt, hgp, hnlt, hn1, hr1, hgs, hsm,
    fsend, frecv, send, recv, csend, crecv, lsend, lrecv, osem, xsend, xrecv,
):
    me = Place()
    s = me.y * 2 + me.c
    outs = []

    def put(held, to):
        outs.append(pltpu.make_async_copy(held, to, osem.at[len(outs)]))
        outs[-1].start()

    enter(me)
    refs = (wa, wu, wd)
    g = Gather(me, refs, send, recv, csend, crecv, lsend, lrecv)
    swaps = [
        pltpu.make_async_remote_copy(
            src, flats.at[pl.ds(b, n), :], fsend.at[i], frecv.at[i], device_id=me.to("core"), device_id_type=MESH)
        for i, (src, b, n) in enumerate(zip((fq, fo, fu, fd), BASE, LINES))
    ]
    for c in swaps:
        c.start()
    chip = (me.z * 2 + me.x) * 2 + me.y
    smf[0, 0:48, :] = jnp.zeros((48, 128), F32)
    for i, vector in enumerate((s0, s1, s2, s3, s4, s5, s6, s7, s8)):
        smf[0, i:i + 1, 0:vector.shape[0]] = vector[...].astype(F32).reshape(1, vector.shape[0])
    wa[pl.ds(pl.multiple_of(chip * 48, 16), 48), pl.ds(pl.multiple_of(me.c * WIDE + 1536, 128), 128)] = (
        smf[0, 0:48, :].astype(BF))
    xall[tile(s, 256), :] = x[...]
    xs, xr = swap_rows(me, xall, s, xsend, xrecv)
    xs[0].start()
    slot = iter(GATHER_PLAN)
    count = {}

    def tick():
        for code in next(slot, ()):
            if sum(count.values()) == GATHER_X:
                xs[1].start()
            p, fx, fy, k = NAMES[code // 16], code // 8 % 2, code // 4 % 2, code % 4
            if fx + fy + k:
                g.serve(p, fx, fy, k)
            else:
                unpack(p)
                g.own(p)
            count[p] = count.get(p, 0) + 1
            if count[p] == 16 and p not in LATE:
                g.across(p, me.c).start()

    unpacked = []

    def unpack(p):
        name = p.rstrip("01")
        if name in unpacked:
            return
        unpacked.append(name)
        for i in {"attn": (0, 1), "up": (2,), "down": (3,)}[name]:
            src, b, n = (fq, fo, fu, fd)[i], BASE[i], LINES[i]
            wide[me.c, pl.ds(b, n), :] = src[...].astype(F32)
            swaps[i].wait_recv()
            wide[1 - me.c, pl.ds(b, n), :] = flats[pl.ds(b, n), :].astype(F32)
        relayout(me, wide, refs, name)

    codes = jnp.where(pad[...] > 0, seg[...], -1).astype(F32)
    mine = seg[:, tile(s, 256)].astype(F32)
    for j in range(8):
        column = jnp.broadcast_to(codes[:, j * 128:(j + 1) * 128], (128, 128)).T
        for i in range(2):
            row = jnp.broadcast_to(mine[:, i * 128:(i + 1) * 128], (128, 128))
            mask[pl.ds(j * 128, 128), pl.ds(i * 128, 128)] = jnp.where(column == row, 0.0, -1e9)

    tick()
    xr[1].wait_recv()
    xs[2].start()
    g.arrived("attn0")
    g.arrived("attn1")
    xr[0].wait_recv()
    xr[2].wait_recv()
    put(wa, to_a)
    for j in range(4):
        xt[:, pl.ds(j * 256, 256)] = xall[pl.ds(j * 256, 256), :].T

    for c in range(2):
        smf[c] = wa[:, pl.ds(c * WIDE + 1536, 128)].astype(F32)
    vec[...] = jnp.zeros_like(vec)
    for i in range(8):
        vec[pl.ds(i, 1), :] = spread([smf[c, pl.ds(i, 16, stride=48), :] for c in range(2)], 24, 768)
    vecu[...] = spread([smf[c, pl.ds(8, 16, stride=48), :] for c in range(2)], 96, 3072)

    tick()
    for j in range(3):
        w = pl.ds(j * 256, 256)
        hq8[:, w] = ((nn(x[...], wa[:, w]) + vec[0:1, w]).astype(BF).astype(F32) * 0.125).astype(BF)
    for j in range(3):
        w = pl.ds(j * 256, 256)
        for r in range(2):
            rows = pl.ds(r * 512, 512)
            tick()
            k = nn(xall[rows, :], wa[:, pl.ds(768 + j * 256, 256)]).astype(BF)
            kk[rows, w] = k
            kt[w, rows] = k.T
            v = (nn(xall[rows, :], wa[:, pl.ds(WIDE + j * 256, 256)]) + vec[1:2, w]).astype(BF)
            vv[rows, w] = v
            vt[w, rows] = v.T
    put(hq8, to_q8)
    put(xt, to_xt)
    put(vv, to_v)
    put(kt, to_kt)

    for p in range(PAIRS):
        w = pl.ds(p * 128, 128)
        qm = head_rows(hq8[:, w], 0)
        tick()
        top = jnp.full((8, 512), -3e38, F32)
        for c in range(4):
            rows = pl.ds(c * 256, 256)
            one = mask[rows, :]
            v = nt(kk[rows, w], qm) + jnp.concatenate([one, one], 1)
            st[rows, :] = v
            top = jnp.maximum(top, jnp.max(v.reshape(32, 8, 512), 0))
        top = jnp.max(top, 0, keepdims=True)
        tick()
        total = jnp.zeros((8, 512), F32)
        for c in range(8):
            rows = pl.ds(c * 128, 128)
            v = jnp.exp(st[rows, :] - top)
            ee[p, rows, :] = v.astype(BF)
            total = total + jnp.sum(v.reshape(16, 8, 512), 0)
        inverse = 1.0 / jnp.sum(total, 0, keepdims=True)
        hr[pl.ds(p, 1), :] = inverse
        tick()
        for h in range(2):
            o = nn(vt[pl.ds(p * 128 + h * 64, 64), :], ee[p, :, pl.ds(h * 256, 256)])
            hot[pl.ds(p * 128 + h * 64, 64), :] = (o * inverse[:, h * 256:(h + 1) * 256]).astype(BF)
        put(ee.at[p], to_e.at[p])

    tick()
    put(hot, to_ot)
    put(hr, to_r)
    n2[...] = tn(hot[...], wa[:, pl.ds(WIDE + 768, 768)])
    tick()
    for r in range(8):
        rows = pl.ds(r * 32, 32)
        value = x[rows, :].astype(F32) + n2[rows, :] + vec[2:3, :]
        centred = value - jnp.mean(value, -1, keepdims=True)
        r1 = lax.rsqrt(jnp.mean(centred * centred, -1, keepdims=True) + EPS)
        n1 = centred * r1
        hn1[rows, :] = n1
        hr1[rows, :] = jnp.broadcast_to(r1, (32, 128))
        normed = n1 * vec[3:4, :] + vec[4:5, :]
        n2[rows, :] = normed
        nl[rows, :] = normed.astype(BF)
    hnlt[...] = nl[...].T
    put(hnlt, to_nlt)
    put(hn1, to_n1)
    put(hr1, to_r1)
    for p in ("attn0", "attn1"):
        g.drain(p)
    tick()
    g.arrived("up0")
    g.arrived("up1")
    put(wu, to_u)

    for j in range(12):
        w = pl.ds(j * 256, 256)
        if j:
            tick()
        before = nn(nl[...], wu[:, w]) + vecu[:, w]
        phi = 0.5 * (1.0 + lax.erf(before * 0.7071067811865476))
        a = (before * phi).astype(BF)
        act[:, w] = a
        hactt[w, :] = a.T
        hgp[:, w] = (phi + before * 0.3989422804014327 * jnp.exp(-0.5 * before * before)).astype(BF)

    tick()
    g.drain("up0")
    g.drain("up1")
    g.arrived("down0")
    g.arrived("down1")
    put(hactt, to_actt)
    put(hgp, to_gp)
    put(wd, to_d)

    for j in range(3):
        w = pl.ds(j * 256, 256)
        n2[:, w] += nn(act[...], wd[:, :, w].reshape(3072, 256)) + vec[5:6, w]
    hsm[...] = jnp.zeros_like(hsm)
    hsm[2:3, :] = vec[3:4, :]
    kept = keep[...] > 0
    gain = jnp.zeros((8, 768), F32)
    shift = jnp.zeros((8, 768), F32)
    for r in range(8):
        rows = pl.ds(r * 32, 32)
        value = n2[rows, :]
        centred = value - jnp.mean(value, -1, keepdims=True)
        r2 = lax.rsqrt(jnp.mean(centred * centred, -1, keepdims=True) + EPS)
        n = centred * r2
        out[rows, :] = jnp.where(kept, n * vec[6:7, :] + vec[7:8, :], x[rows, :].astype(F32)).astype(BF)
        grad = jnp.where(kept, cot[rows, :].astype(F32), 0.0)
        gain = gain + jnp.sum((grad * n).reshape(4, 8, 768), 0)
        shift = shift + jnp.sum(grad.reshape(4, 8, 768), 0)
        c = grad * vec[6:7, :]
        hgs[rows, :] = r2 * (c - jnp.mean(c, -1, keepdims=True) - n * jnp.mean(c * n, -1, keepdims=True))
    hsm[0:1, :] = jnp.sum(gain, 0, keepdims=True)
    hsm[1:2, :] = jnp.sum(shift, 0, keepdims=True)
    put(out, to_out)
    put(hgs, to_gs)
    put(hsm, to_sm)

    g.drain("down0")
    g.drain("down1")
    for c in swaps:
        c.wait_send()
    for c in xs:
        c.wait_send()
    for o in outs:
        o.wait()


FORWARD_OUT = (
    ((256, 768), BF), ((768, 2 * WIDE), BF), ((768, 3072), BF), ((16, 192, 768), BF), ((768, 1024), BF),
    ((1024, 768), BF), ((768, 1024), BF), ((PAIRS, 1024, 512), BF), ((256, 768), BF), ((768, 256), BF),
    ((8, 512), F32), ((3072, 256), BF), ((256, 3072), BF), ((768, 256), BF), ((256, 768), F32), ((256, 128), F32),
    ((256, 768), F32), ((8, 768), F32),
)


def forward_call(*args):
    a = pl.BlockSpec(memory_space=pl.ANY)
    v = pl.BlockSpec(memory_space=pltpu.VMEM)
    n = len(PARTS)
    dma = pltpu.SemaphoreType.DMA
    return pl.pallas_call(
        forward_kernel,
        out_shape=[jax.ShapeDtypeStruct(s, d) for s, d in FORWARD_OUT],
        in_specs=[v] * 18,
        out_specs=[a] * len(FORWARD_OUT),
        scratch_shapes=[
            pltpu.VMEM((1728, 128), BF), pltpu.VMEM((2, 1728, 128), F32),
            pltpu.VMEM((768, 2 * WIDE), BF), pltpu.VMEM((768, 3072), BF),
            pltpu.VMEM((16, 192, 768), BF), pltpu.VMEM((2, 768, 128), F32),
            pltpu.VMEM((1024, 768), BF), pltpu.VMEM((1024, 768), BF), pltpu.VMEM((1024, 768), BF),
            pltpu.VMEM((768, 1024), BF), pltpu.VMEM((768, 1024), BF), pltpu.VMEM((1024, 512), F32),
            pltpu.VMEM((PAIRS, 1024, 512), BF), pltpu.VMEM((1024, 256), F32), pltpu.VMEM((8, 768), F32),
            pltpu.VMEM((1, 3072), F32), pltpu.VMEM((256, 768), F32), pltpu.VMEM((768, 1024), BF),
            pltpu.VMEM((256, 3072), BF), pltpu.VMEM((256, 768), BF),
            pltpu.VMEM((256, 768), BF), pltpu.VMEM((256, 768), BF), pltpu.VMEM((768, 256), BF),
            pltpu.VMEM((8, 512), F32), pltpu.VMEM((3072, 256), BF), pltpu.VMEM((256, 3072), BF),
            pltpu.VMEM((768, 256), BF), pltpu.VMEM((256, 768), F32), pltpu.VMEM((256, 128), F32),
            pltpu.VMEM((256, 768), F32), pltpu.VMEM((8, 768), F32),
            dma((4,)), dma((4,)), dma((n, 16, 4)), dma((n, 16)), dma((n,)), dma((n,)), dma((2, 16)), dma((2, 16)), dma((24,)), dma((3,)), dma((3,)),
        ],
        compiler_params=pltpu.CompilerParams(collective_id=1, has_side_effects=True, vmem_limit_bytes=62 << 20),
        name="forward",
    )(*args)


RPARTS = (
    ("down0", 3, "yzx", 96, 0, 0, 384),
    ("down1", 3, "xzy", 96, 96, 0, 384),
    ("up0", 2, "zxy", 48, 0, 0, 768),
    ("up1", 2, "yzx", 48, 0, 768, 768),
    ("out", 1, "yzx", 48, 0, 0, 384),
    ("qkv0", 0, "zxy", 48, 0, 0, 384),
    ("qkv1", 0, "zxy", 48, 0, 384, 384),
    ("qkv2", 0, "zxy", 48, 0, 768, 384),
)
HALF = (1152, 384, 1536, 384)
CHIPROWS = (48, 48, 48, 192)
ROWS = (768, 768, 768, 3072)
SIZES = {"x": 2, "y": 2, "z": 4}
LINKS = ("up", "down", "x", "y")


def slots(order, axis):
    n = 4 if axis == "z" else 1
    for a in order[: order.index(axis)]:
        n *= SIZES[a]
    return n


def landing_shapes():
    shapes = []
    for name, mat, order, rows, ro, co, cols in RPARTS:
        for way in LINKS:
            axis = "z" if way in ("up", "down") else way
            shapes.append(pltpu.VMEM((slots(order, axis), rows, cols), BF))
    return shapes


class Scatter:
    def __init__(self, me, grads, half, lands, finals, send, recv):
        self.me, self.grads, self.half, self.lands, self.finals = me, grads, half, lands, finals
        self.send, self.recv = send, recv

    def chip(self, x, y, z):
        return (z * 2 + x) * 2 + y

    def part(self, refs, i, dest):
        name, mat, order, rows, ro, co, cols = RPARTS[i]
        first = pl.multiple_of(self.chip(*dest) * CHIPROWS[mat] + ro, 16)
        return refs[mat].at[pl.ds(first, rows), pl.ds(co, cols)]

    def block(self, i, dest):
        return self.part(self.grads, i, dest)

    def slot(self, i, way, dest):
        order = RPARTS[i][2]
        axis = "z" if way in ("up", "down") else way
        coords = dict(zip("xyz", dest))
        index = coords["z"] if axis == "z" else 0
        for a in order[: order.index(axis)]:
            index = index * SIZES[a] + coords[a]
        return index

    def land(self, i, way, dest):
        return self.lands[i * 4 + LINKS.index(way)].at[self.slot(i, way, dest)]

    def copy(self, i, way, dest):
        chip = self.chip(*dest)
        return pltpu.make_async_remote_copy(
            self.block(i, dest), self.land(i, way, dest), self.send.at[i, chip],
            self.recv.at[i, LINKS.index(way), chip], device_id=self.me.to(way), device_id_type=MESH)

    def stage(self, i, fx, fy, k):
        moved = {"x": fx, "y": fy, "z": k}
        return max(s for s in range(3) if moved[RPARTS[i][2][s]])

    def take(self, i, way, dest):
        self.copy(i, way, dest).wait_recv()
        ref = self.block(i, dest)
        ref[...] = (ref[...].astype(F32) + self.land(i, way, dest)[...].astype(F32)).astype(BF)

    def total(self, i, dest, ways):
        value = self.block(i, dest)[...].astype(F32) + self.part(self.half, i, dest)[...].astype(F32)
        for way in ways:
            self.copy(i, way, dest).wait_recv()
            value = value + self.land(i, way, dest)[...].astype(F32)
        return value

    def serve(self, i, fx, fy, k):
        me = self.me
        order = RPARTS[i][2]
        stage = self.stage(i, fx, fy, k)
        axis = order[stage]

        def act(dest, sign):
            way = axis
            if axis == "z":
                way, more = ("down", me.z < 3) if sign < 0 else ("up", me.z > 0)
                pl.when(more)(lambda: self.take(i, way, dest))
            if "z" in order[stage + 1:]:
                pl.when(me.z < 3)(lambda: self.take(i, "down", dest))
                pl.when(me.z > 0)(lambda: self.take(i, "up", dest))
            value = self.total(i, dest, [a for a in order[stage + 1:] if a != "z"])
            self.block(i, dest)[...] = value.astype(BF)
            self.copy(i, way, dest).start()

        self.dests(fx, fy, k, act)

    def dests(self, fx, fy, k, act):
        me = self.me
        x = 1 - me.x if fx else me.x
        y = 1 - me.y if fy else me.y
        if k == 0:
            act((x, y, me.z), 0)
        else:
            pl.when(me.z >= k)(lambda: act((x, y, me.z - k), -1))
            pl.when(me.z + k <= 3)(lambda: act((x, y, me.z + k), 1))

    def own(self, i):
        dest = (self.me.x, self.me.y, self.me.z)
        name, mat, order, rows, ro, co, cols = RPARTS[i]
        self.finals[mat].at[pl.ds(ro, rows), pl.ds(co, cols)][...] = self.total(i, dest, ())

    def finish(self, i):
        name, mat, order, rows, ro, co, cols = RPARTS[i]
        me = self.me
        dest = (me.x, me.y, me.z)
        fin = self.finals[mat].at[pl.ds(ro, rows), pl.ds(co, cols)]

        def add(way):
            self.copy(i, way, dest).wait_recv()
            fin[...] += self.land(i, way, dest)[...].astype(F32)
        for axis in order:
            if axis == "z":
                pl.when(me.z < 3)(lambda: add("down"))
                pl.when(me.z > 0)(lambda: add("up"))
            else:
                add(axis)

    def drain(self, i):
        for fx in (0, 1):
            for fy in (0, 1):
                for k in range(4):
                    if fx + fy + k:
                        axis = RPARTS[i][2][self.stage(i, fx, fy, k)]
                        self.dests(fx, fy, k, lambda dest, sign: self.copy(
                            i, axis if axis != "z" else ("down" if sign < 0 else "up"), dest).wait_send())


SCATTER_PLAN = (
    (), (), (), (), (), (), (11, 28, 15, 31, 14, 23), (), (), (), (), (), (), (), (), (), (), (),
    (20, 63, 62, 30, 27, 10, 59, 3, 9, 47, 19, 46), (), (), (), (), (7, 26, 29, 61, 55, 58), (), (), (), (), (), (),
    (), (74, 51, 43, 6, 37, 57, 39, 21, 25, 22, 54, 2, 44, 13, 73), (), (), (), (), (), (), (), (), (), (), (), (),
    (), (93, 18, 1, 38, 12, 50, 79, 45, 94, 75, 24, 42, 36, 35, 95, 5, 77, 78, 60, 87, 86), (), (), (), (), (), (),
    (), (), (), (), (), (), (),
    (8, 67, 56, 103, 71, 40, 85, 101, 41, 17, 111, 109, 102, 92, 49, 34, 53, 91, 110, 108), (), (), (), (), (), (),
    (), (), (127, 107, 70, 90, 126, 125, 106, 66, 83, 33, 16, 119, 4, 123, 76), (),
    (99, 122, 118, 89, 105, 115, 124, 121, 88, 117, 82, 104, 72, 116, 52, 69, 32, 98), (100, 114), (),
    (65, 81, 68, 97, 120, 84, 0, 113), (), (), (), (), (48, 64, 80, 96, 112),
)

FLATROWS = ((24, 18, 432), (24, 6, 144), (24, 24, 576), (96, 6, 576))


def column(mat, c, j):
    if mat:
        return c * (FLATROWS[mat][1] // 2) + j
    group, t = j // 3, j % 3
    if c == 0:
        return 2 * group + t if t < 2 else 6 + 2 * group
    return 7 + 2 * group if t == 0 else 11 + 2 * group + t


def flatten(me, mat, finals, sides, out):
    rows, tiles, lines = FLATROWS[mat]
    half = tiles // 2
    for c in range(2):
        @pl.when(me.c == c)
        def _():
            for j in range(half):
                mine = finals[mat][pl.ds(pl.multiple_of(me.c * rows, 8), rows), pl.ds(j * 128, 128)]
                out[pl.ds(column(mat, c, j), rows, stride=tiles), :] = mine
                out[pl.ds(column(mat, 1 - c, j), rows, stride=tiles), :] = sides[mat][:, pl.ds(j * 128, 128)]


def colsum(array):
    return jnp.sum(array.astype(F32), 0, keepdims=True)


def backward_kernel(
    ha, hu, hd, hxt, hv, hkt, he, *rest,
):
    far, keep, rest = rest[:11], rest[11], rest[12:]
    (ingrad, oq, oo, ou, od, chosen), rest = rest[:6], rest[6:]
    near, rest = rest[:11], rest[11:]
    q8, ot, rr, actt, gp, nlt, n1, r1, gs, sm0, cot = near
    lands, rest = rest[:32], rest[32:]
    grads, rest = rest[:4], rest[4:]
    stage, rest = rest[:3], rest[3:]
    stage = (stage[1].at[:, pl.ds(0, HALF[0])],) + tuple(stage)
    half, rest = rest[:4], rest[4:]
    finals, rest = rest[:4], rest[4:]
    sides, rest = rest[:4], rest[4:]
    (wbig, wo, xt, vv, kt, ee, ds, gbr, gbef, first, gts, gsa, dq, dkv, dx, dxc, dxy, acc, sland, osm,
     nsem, wsem, isem, esem, csend, crecv, send, recv, fsend, frecv, dsend, drecv, asend, arecv) = rest
    me = Place()
    s = me.y * 2 + me.c
    wds = [pltpu.make_async_copy(hd.at[pl.ds(q * 768, 768), :], wbig.at[pl.ds(q * 768, 768), :], wsem.at[q]) for q in range(4)]
    wus = [pltpu.make_async_copy(hu.at[:, pl.ds(q * 768, 768)], wbig.at[pl.ds(q * 768, 768), :], wsem.at[4 + q]) for q in range(4)]
    wqs = [pltpu.make_async_copy(ha.at[:, pl.ds((0, 768, WIDE)[q], 768)], wbig.at[pl.ds(q * 768, 768), :], wsem.at[8 + q]) for q in range(3)]
    others = [pltpu.make_async_copy(a, b, isem.at[i]) for i, (a, b) in enumerate(((ha.at[:, pl.ds(WIDE + 768, 768)], wo), (hv, vv), (hkt, kt), (hxt, xt)))]
    ees = [pltpu.make_async_copy(he.at[p], ee.at[p % 2], esem.at[p]) for p in range(PAIRS)]
    nears = [pltpu.make_async_copy(a, b, nsem.at[i]) for i, (a, b) in enumerate(zip(far, near))]
    for i in (8, 9, 3):
        nears[i].start()
    for c in wds:
        c.start()
    for i in (4, 5, 6, 7, 1, 2, 0, 10):
        nears[i].start()
    for c in others:
        c.start()
    ees[0].start()
    ees[1].start()
    enter(me)

    sc = Scatter(me, grads, half, lands, finals, send, recv)

    def swap(mat, piece=0):
        cut = {
            0: (slice(None), pl.ds(piece * 384, 384)), 1: (slice(None), slice(None)),
            2: (slice(None), pl.ds(piece * 512, 512)), 3: (pl.ds(piece * 768, 768), slice(None)),
        }[mat]
        n = (0, 3, 4, 7)[mat] + piece
        return pltpu.make_async_remote_copy(
            stage[mat].at[cut], half[mat].at[cut], csend.at[n], crecv.at[n], device_id=me.to("core"), device_id_type=MESH)

    def last(mat):
        rows = FLATROWS[mat][0]
        src = finals[mat].at[pl.ds(pl.multiple_of((1 - me.c) * rows, 8), rows), :]
        return pltpu.make_async_remote_copy(
            src, sides[mat], fsend.at[mat], frecv.at[mat], device_id=me.to("core"), device_id_type=MESH)

    def swapped(mat):
        for piece in range((3, 1, 3, 4)[mat]):
            swap(mat, piece).wait_recv()

    def unstaged(mat):
        for piece in range((3, 1, 3, 4)[mat]):
            swap(mat, piece).wait_send()

    slot = iter(SCATTER_PLAN)
    count = {}

    def tick():
        for code in next(slot, ()):
            i, fx, fy, k = code // 16, code // 8 % 2, code // 4 % 2, code % 4
            if fx + fy + k:
                sc.serve(i, fx, fy, k)
            else:
                sc.own(i)
                sc.finish(i)
                mat = RPARTS[i][1]
                count[mat] = count.get(mat, 0) + 1
                if count[mat] == (3, 1, 2, 2)[mat]:
                    last(mat).start()

    def arrange(value_ref, to):
        to[:, 0:384] = value_ref[:, pl.ds(pl.multiple_of(me.c * 384, 128), 384)]
        to[:, 384:768] = value_ref[:, pl.ds(pl.multiple_of((1 - me.c) * 384, 128), 384)]

    osm[...] = jnp.zeros_like(osm)
    for i in (8, 9):
        nears[i].wait()
    osm[6:8, :] = sm0[0:2, :]
    gsa[...] = gs[...].astype(BF)
    osm[5:6, :] = colsum(gsa[...])
    arrange(gsa, gbr)
    nears[3].wait()

    for j in range(12):
        w = pl.ds(j * 256, 256)
        v = nn(actt[w, :], gbr[...]).astype(BF)
        grads[3][w, :] = v[:, 0:384]
        stage[3][w, :] = v[:, 384:768]
        if j % 3 == 2:
            swap(3, j // 3).start()

    nears[4].wait()
    for q in range(4):
        wds[q].wait()
        for j in range(3):
            w = pl.ds(q * 768 + j * 256, 256)
            ga = nt(gsa[...], wbig[w, :]).astype(BF).astype(F32)
            gb = (ga * gp[:, w].astype(F32)).astype(BF)
            gbef[:, w] = gb
            osm[8 + q:9 + q, pl.ds(j * 256, 256)] = colsum(gb)
        wus[q].start()
        if q == 0:
            swapped(3)
        tick()

    for i in (5, 6, 7, 1, 2, 0, 10):
        nears[i].wait()
    for j in range(6):
        w = pl.ds(j * 256, 256)
        tick()
        stage[2][:, w] = nn(nlt[...], gbef[:, pl.ds(pl.multiple_of((1 - me.c) * 1536 + j * 256, 256), 256)]).astype(BF)
        if j % 2:
            swap(2, j // 2).start()
    for j in range(6):
        w = pl.ds(j * 256, 256)
        tick()
        grads[2][:, w] = nn(nlt[...], gbef[:, pl.ds(pl.multiple_of(me.c * 1536 + j * 256, 256), 256)]).astype(BF)
    for c in wus:
        c.wait()
    tick()
    swapped(2)

    for j in range(3):
        w = pl.ds(j * 256, 256)
        tick()
        total = gs[:, w]
        for q in range(4):
            total += nt(gbef[:, pl.ds(q * 768, 768)], wbig[pl.ds(q * 768 + j * 256, 256), :])
        first[:, w] = total
    for c in wqs:
        c.start()

    gain = jnp.zeros((8, 768), F32)
    shift = jnp.zeros((8, 768), F32)
    for r in range(8):
        rows = pl.ds(r * 32, 32)
        if r % 4 == 0:
            tick()
        gn = first[rows, :]
        n = n1[rows, :]
        gain = gain + jnp.sum((gn * n).reshape(4, 8, 768), 0)
        shift = shift + jnp.sum(gn.reshape(4, 8, 768), 0)
        c1 = gn * sm0[2:3, :]
        gf = r1[rows, 0:1] * (c1 - jnp.mean(c1, -1, keepdims=True) - n * jnp.mean(c1 * n, -1, keepdims=True))
        first[rows, :] = gf
        gsa[rows, :] = gf.astype(BF)
    osm[3:4, :] = jnp.sum(gain, 0, keepdims=True)
    osm[4:5, :] = jnp.sum(shift, 0, keepdims=True)
    osm[2:3, :] = colsum(gsa[...])
    arrange(gsa, gbr)
    tick()

    for j in range(3):
        w = pl.ds(j * 256, 256)
        v = nn(ot[w, :], gbr[...]).astype(BF)
        grads[1][w, :] = v[:, 0:384]
        stage[1][w, :] = v[:, 384:768]
    swap(1).start()
    for c in others:
        c.wait()
    for p in range(PAIRS):
        w = pl.ds(p * 128, 128)
        if p % 2 == 0:
            tick()
        g = nt(wo[w, :], gsa[...]).astype(BF).astype(F32)
        scale = jnp.concatenate(
            [jnp.broadcast_to(rr[p:p + 1, h * 256:(h + 1) * 256], (64, 256)) for h in range(2)], 0)
        gts[w, :] = (g * scale).astype(BF)
    swapped(1)

    mine = xt.at[:, tile(s, 256)]

    def qkv_grads(group):
        q = pl.ds(group * 256, 256)
        v = pl.ds(768 + group * 256, 256)
        mid = pl.ds(group * 384, 384)

        def put(r, a, b):
            rows = pl.ds(r * 256, 256)
            vq = nn(mine[rows, :], dq[:, q]).astype(BF)
            vk = nn(xt[rows, :], dkv[:, q]).astype(BF)
            vv_ = nn(xt[rows, :], dkv[:, v]).astype(BF)
            a[rows, pl.ds(group * 384, 256)] = vq
            a[rows, pl.ds(group * 384 + 256, 128)] = vk[:, 0:128]
            b[rows, pl.ds(group * 384, 128)] = vk[:, 128:256]
            b[rows, pl.ds(group * 384 + 128, 256)] = vv_

        for r in range(3):
            tick()
            pl.when(me.c == 0)(lambda: put(r, grads[0], stage[0]))
            pl.when(me.c == 1)(lambda: put(r, stage[0], grads[0]))
        swap(0, group).start()

    for p in range(PAIRS):
        w = pl.ds(p * 128, 128)
        g = gts[w, :]
        both = ot[w, :].astype(F32) * g.astype(F32)
        delta = jnp.concatenate([jnp.sum(both[0:64], 0, keepdims=True), jnp.sum(both[64:128], 0, keepdims=True)], 1)
        gm = head_rows(g.T, 0)
        qm = head_rows(q8[:, w], 0)
        ees[p].wait()
        e = ee.at[p % 2]
        for c in range(4):
            rows = pl.ds(c * 256, 256)
            if c % 2 == 0:
                tick()
            dp = nt(vv[rows, w], gm)
            ds[rows, :] = (e[rows, :].astype(F32) * (dp - delta)).astype(BF)
        tick()
        dkv[:, w] = nn(ds[...], qm).astype(BF)
        tick()
        dkv[:, pl.ds(768 + p * 128, 128)] = nn(e[...], gm).astype(BF)
        tick()
        dqt = jnp.concatenate([
            nn(kt[pl.ds(p * 128 + h * 64, 64), :], ds[:, pl.ds(h * 256, 256)]) for h in range(2)], 0)
        dq[:, w] = (dqt * 0.125).astype(BF).T
        if p + 2 < PAIRS:
            ees[p + 2].start()
        if p == 1:
            unstaged(2)
        if p % 2:
            qkv_grads(p // 2)
        if p in (2, 4):
            swap(0, p // 2 - 1).wait_recv()
            tick()

    osm[0:1, :] = colsum(dq[...])
    osm[1:2, :] = colsum(dkv[:, pl.ds(768, 768)])

    acc[0] = osm[...]
    pairz = {"outer": (me.z + 1 - 2 * (me.z % 2)) * 2 + me.x}
    smalls = [
        pltpu.make_async_remote_copy(acc.at[i], sland.at[i], asend.at[i], arecv.at[i], device_id=to, device_id_type=MESH)
        for i, to in enumerate((me.to("core"), me.to("x"), me.to("y"), pairz, me.to("far")))
    ]
    smalls[0].start()

    def small_step(i):
        smalls[i].wait_recv()
        acc[i + 1] = acc[i] + sland[i]
        if i < 4:
            smalls[i + 1].start()

    for c in wqs:
        c.wait()

    for j in range(3):
        w = pl.ds(j * 256, 256)
        for r in range(2):
            rows = pl.ds(r * 512, 512)
            if j == 0 and r == 1:
                swap(0, 2).wait_recv()
            tick()
            dx[rows, w] = (
                nt(dkv[rows, 0:768], wbig[pl.ds(768 + j * 256, 256), :])
                + nt(dkv[rows, 768:1536], wbig[pl.ds(1536 + j * 256, 256), :])).astype(BF)
            if r:
                small_step(j)
        first[:, w] += nt(dq[...], wbig[w, :])

    def dx_copy(n):
        if n < 2:
            yy = me.y if n == 0 else 1 - me.y
            return pltpu.make_async_remote_copy(
                dx.at[tile(yy * 2 + 1 - me.c, 256), :], dxc.at[n], dsend.at[n], drecv.at[n],
                device_id=me.to("core"), device_id_type=MESH)
        return pltpu.make_async_remote_copy(
            dx.at[tile((1 - me.y) * 2 + me.c, 256), :], dxy, dsend.at[2], drecv.at[2],
            device_id=me.to("y"), device_id_type=MESH)
    dx_copy(1).start()
    dx_copy(0).start()
    dx_copy(1).wait_recv()
    over = tile((1 - me.y) * 2 + me.c, 256)
    dx[over, :] = (dx[over, :].astype(F32) + dxc[1].astype(F32)).astype(BF)
    dx_copy(2).start()

    for i in range(5):
        tick()
        if i < 2:
            small_step(3 + i)
    tick()
    owner = ((me.z * 2 + me.x) * 4 + s).astype(F32)
    at = lax.broadcasted_iota(jnp.int32, (768, 128), 0).astype(F32)
    lane = lax.broadcasted_iota(jnp.int32, (768, 128), 1).astype(F32)

    def choose(rows, start, size):
        pick = jnp.where((at == start + lane) & (lane < size), 1.0, 0.0)
        return jnp.dot(rows, pick, precision=lax.Precision.HIGHEST, preferred_element_type=F32)
    up = jnp.zeros((8, 128), F32)
    for q in range(4):
        up = up + choose(acc[5, 8 + q:9 + q, :], owner * 96 - q * 768, 96)
    chosen[0:8, :] = choose(acc[5, 0:8, :], owner * 24, 24)
    chosen[8:16, :] = up
    dx_copy(0).wait_recv()
    dx_copy(2).wait_recv()
    total = first[...] + dx[tile(s, 256), :].astype(F32) + dxc[0].astype(F32) + dxy[...].astype(F32)
    ingrad[...] = jnp.where(keep[...] > 0, total, cot[...].astype(F32)).astype(BF)
    for i in range(8):
        sc.drain(i)
    for mat in (3, 1, 0):
        unstaged(mat)
    for n in range(3):
        dx_copy(n).wait_send()
    for c in smalls:
        c.wait_send()
    for mat in (3, 2, 1, 0):
        last(mat).wait()
        flatten(me, mat, finals, sides, (oq, oo, ou, od)[mat])


def backward_call(*args):
    a = pl.BlockSpec(memory_space=pl.ANY)
    v = pl.BlockSpec(memory_space=pltpu.VMEM)
    dma = pltpu.SemaphoreType.DMA
    outs = [((256, 768), BF)] + [((FLATROWS[m][2], 128), F32) for m in range(4)] + [((16, 128), F32)]
    halves = [(ROWS[m], HALF[m]) for m in range(4)]
    return pl.pallas_call(
        backward_kernel,
        out_shape=[jax.ShapeDtypeStruct(s, d) for s, d in outs],
        in_specs=[a] * 18 + [v],
        out_specs=[v] * 6,
        scratch_shapes=[pltpu.VMEM(s, d) for s, d in FORWARD_OUT[8:]] + [pltpu.VMEM((256, 768), BF)]
        + landing_shapes()
        + [pltpu.VMEM(h, BF) for h in halves + halves[1:] + halves]
        + [pltpu.VMEM((CHIPROWS[m], HALF[m]), F32) for m in range(4)]
        + [pltpu.VMEM((FLATROWS[m][0], HALF[m]), F32) for m in range(4)]
        + [
            pltpu.VMEM((3072, 768), BF), pltpu.VMEM((768, 768), BF), pltpu.VMEM((768, 1024), BF),
            pltpu.VMEM((1024, 768), BF), pltpu.VMEM((768, 1024), BF), pltpu.VMEM((2, 1024, 512), BF),
            pltpu.VMEM((1024, 512), BF), pltpu.VMEM((256, 768), BF), pltpu.VMEM((256, 3072), BF),
            pltpu.VMEM((256, 768), F32), pltpu.VMEM((768, 256), BF), pltpu.VMEM((256, 768), BF),
            pltpu.VMEM((256, 768), BF), pltpu.VMEM((1024, 1536), BF), pltpu.VMEM((1024, 768), BF),
            pltpu.VMEM((2, 256, 768), BF), pltpu.VMEM((256, 768), BF), pltpu.VMEM((6, 16, 768), F32),
            pltpu.VMEM((5, 16, 768), F32), pltpu.VMEM((16, 768), F32),
            dma((11,)), dma((11,)), dma((4,)), dma((PAIRS,)), dma((11,)), dma((11,)), dma((8, 16)), dma((8, 4, 16)),
            dma((4,)), dma((4,)), dma((3,)), dma((3,)), dma((5,)), dma((5,)),
        ],
        compiler_params=pltpu.CompilerParams(collective_id=2, has_side_effects=True, vmem_limit_bytes=63 << 20),
        name="backward",
    )(*args)


SMALL_SIZES = (24,) * 8 + (96,)


def finish_kernel(*refs):
    ins, small, outs, smalls = refs[:6], refs[6], refs[7:13], refs[13:22]
    for a, b in zip(ins, outs):
        b[...] = a[...]
    for i, (to, size) in enumerate(zip(smalls, SMALL_SIZES)):
        to[...] = small[i, 0:size]


def finish_call(*args):
    v = pl.BlockSpec(memory_space=pltpu.VMEM)
    return pl.pallas_call(
        finish_kernel,
        out_shape=[jax.ShapeDtypeStruct(x.shape, x.dtype) for x in args[:6]]
        + [jax.ShapeDtypeStruct((size,), F32) for size in SMALL_SIZES],
        in_specs=[v] * 7,
        out_specs=[v] * 15,
        name="finish",
    )(*args)


AXES = ("outer", "inner", "seq")
SMALLS = (1, 2, 4, 5, 6, 10, 11, 12, 8)


def to_part(flat):
    inner = lax.axis_size("inner")
    if inner == 1:
        return flat
    every = lax.all_gather(flat, ("inner", "seq"), axis=0, tiled=True)
    size = flat.shape[0] * inner
    return lax.dynamic_slice_in_dim(every, lax.axis_index("seq") * size, size, 0)


def whole_scatter(part):
    inner = lax.axis_size("inner")
    if inner == 1:
        return part
    every = lax.psum(lax.all_gather(part, "seq", axis=0, tiled=True), "inner")
    size = part.shape[0] // inner
    index = lax.axis_index("inner") * lax.axis_size("seq") + lax.axis_index("seq")
    return lax.dynamic_slice_in_dim(every, index * size, size, 0)


def shards(inputs, *rest):
    params, (cotangent, segment_ids, pad_mask, keep_flag) = rest[:13], rest[13:]
    parts = [to_part(p) for p in params]
    x, cot = inputs[0], cotangent[0]
    keep = keep_flag.reshape(1, 1)
    out, *held = forward_call(
        *(parts[i].reshape(-1, 128) for i in (0, 3, 7, 9)), *(parts[i] for i in SMALLS), x, cot, segment_ids, pad_mask, keep
    )
    held[2] = held[2].reshape(FF, D)
    grad, *big, small = backward_call(*held, cot, keep)
    out, grad, *rest = finish_call(out, grad, *big, small)
    big = [whole_scatter(part.reshape(-1)) for part in rest[:4]]
    q, v, ob, g1, b1, db, g2, b2, ub = (whole_scatter(part) for part in rest[4:])
    return (out[None], grad[None], big[0], q, v, big[1], ob, g1, b1, big[2], ub, big[3], db, g2, b2)


def solution(mesh):
    fsdp, seq = mesh.shape["fsdp"], mesh.shape["seq"]
    mesh = Mesh(mesh.devices.reshape(8, fsdp // 8, seq), AXES)
    tokens = P(("outer", "inner"), "seq", None)
    flat = P(AXES)
    rows = P(("outer", "inner"), None)
    return jax.shard_map(
        shards,
        mesh=mesh,
        in_specs=(tokens,) + (flat,) * 13 + (tokens, rows, rows, P(("outer", "inner"))),
        out_specs=(tokens, tokens) + (flat,) * 13,
        check_vma=False,
    )
```

```python
import functools
import jax
import jax.numpy as jnp
from jax import lax
from jax.experimental import pallas as pl
from jax.experimental.pallas import tpu as pltpu
from jax.sharding import Mesh, PartitionSpec as P

MESH = pl.DeviceIdType.MESH
D = 768
FF = 3072
BF = jnp.bfloat16
F32 = jnp.float32
LINES = (432, 144, 576, 576)
BASE = (0, 432, 576, 1152)
WIDE = 1664


class Place:
    def __init__(self):
        o = lax.axis_index("outer")
        s = lax.axis_index("seq")
        self.z, self.x, self.y, self.c = o // 2, o % 2, s // 2, s % 2

    def to(self, way):
        z, x, y, c = self.z, self.x, self.y, self.c
        return {
            "up": {"outer": (z + 1) * 2 + x},
            "down": {"outer": (z - 1) * 2 + x},
            "x": {"outer": z * 2 + 1 - x},
            "y": {"seq": (1 - y) * 2 + c},
            "core": {"seq": y * 2 + 1 - c},
            "far": {"outer": (3 - z) * 2 + x},
        }[way]


def enter(me):
    bar = pltpu.get_barrier_semaphore()

    def greet(to):
        pl.semaphore_signal(bar, 1, device_id=to, device_id_type=MESH)

    for way in ("x", "y", "core"):
        greet(me.to(way))
    pl.when(me.z < 3)(lambda: greet(me.to("up")))
    pl.when(me.z > 0)(lambda: greet(me.to("down")))
    pl.when((me.z == 0) | (me.z == 3))(lambda: greet(me.to("far")))
    pl.semaphore_wait(bar, 5)


WAYS = ("up", "down", "x", "y")

PARTS = (
    ("attn0", "yzx"),
    ("attn1", "zxy"),
    ("up0", "yzx"),
    ("up1", "xzy"),
    ("down0", "zxy"),
    ("down1", "yzx"),
)
LATE = ("down0", "down1")
NAMES = [p[0] for p in PARTS]
ORDER = dict(PARTS)


class Gather:
    def __init__(self, me, refs, send, recv, csend, crecv, lsend, lrecv):
        self.me = me
        self.refs = refs
        self.send, self.recv, self.csend, self.crecv = send, recv, csend, crecv
        self.lsend, self.lrecv = lsend, lrecv

    def block(self, part, chip, c):
        wa, wu, wd = self.refs
        m = pl.multiple_of
        if part == "down0":
            return wd.at[chip, pl.ds(0, 96), pl.ds(m(c * 384, 128), 384)]
        if part == "down1":
            return wd.at[chip, pl.ds(96, 96), pl.ds(m(c * 384, 128), 384)]
        rows = pl.ds(m(chip * 48, 16), 48)
        if part == "attn0":
            return wa.at[rows, pl.ds(m(c * WIDE, 128), 768)]
        if part == "attn1":
            return wa.at[rows, pl.ds(m(c * WIDE + 768, 128), 896)]
        if part == "up0":
            return wu.at[rows, pl.ds(m(c * 1536, 128), 768)]
        return wu.at[rows, pl.ds(m(c * 1536 + 768, 128), 768)]

    def half(self, part, c):
        wa, wu, wd = self.refs
        m = pl.multiple_of
        if part == "down0":
            return wd.at[:, pl.ds(0, 96), pl.ds(m(c * 384, 128), 384)]
        if part == "down1":
            return wd.at[:, pl.ds(96, 96), pl.ds(m(c * 384, 128), 384)]
        if part == "attn0":
            return wa.at[:, pl.ds(m(c * WIDE, 128), 768)]
        if part == "attn1":
            return wa.at[:, pl.ds(m(c * WIDE + 768, 128), 896)]
        if part == "up0":
            return wu.at[:, pl.ds(m(c * 1536, 128), 768)]
        return wu.at[:, pl.ds(m(c * 1536 + 768, 128), 768)]

    def chip(self, x, y, z):
        return (z * 2 + x) * 2 + y

    def copy(self, part, chip, way):
        i = NAMES.index(part)
        ref = self.block(part, chip, self.me.c)
        return pltpu.make_async_remote_copy(
            ref, ref, self.send.at[i, chip, WAYS.index(way)], self.recv.at[i, chip],
            device_id=self.me.to(way), device_id_type=MESH)

    def across(self, part, c):
        i = NAMES.index(part)
        ref = self.half(part, c)
        return pltpu.make_async_remote_copy(
            ref, ref, self.csend.at[i], self.crecv.at[i], device_id=self.me.to("core"), device_id_type=MESH)

    def onward(self, part, chip, axes):
        me = self.me
        for axis in axes:
            if axis == "z":
                pl.when(me.z < 3)(lambda: self.copy(part, chip, "up").start())
                pl.when(me.z > 0)(lambda: self.copy(part, chip, "down").start())
            else:
                self.copy(part, chip, axis).start()

    def own(self, part):
        me = self.me
        chip = self.chip(me.x, me.y, me.z)
        self.onward(part, chip, ORDER[part])
        if part in LATE:
            self.beside(part, chip, me.c).start()

    def origins(self, fx, fy, k, act):
        me = self.me
        x = 1 - me.x if fx else me.x
        y = 1 - me.y if fy else me.y
        if k == 0:
            act(self.chip(x, y, me.z), 0)
        else:
            pl.when(me.z >= k)(lambda: act(self.chip(x, y, me.z - k), -1))
            pl.when(me.z + k <= 3)(lambda: act(self.chip(x, y, me.z + k), 1))

    def arrival(self, part, fx, fy, k):
        moved = {"x": fx, "y": fy, "z": k}
        return max(i for i in range(3) if moved[ORDER[part][i]])

    def serve(self, part, fx, fy, k):
        me = self.me
        order = ORDER[part]
        stage = self.arrival(part, fx, fy, k)
        axis = order[stage]

        def act(chip, sign):
            if axis == "z":
                way, more = ("up", me.z < 3) if sign < 0 else ("down", me.z > 0)
                self.copy(part, chip, way).wait_recv()
                pl.when(more)(lambda: self.copy(part, chip, way).start())
            else:
                self.copy(part, chip, axis).wait_recv()
            self.onward(part, chip, order[stage + 1:])
            if part in LATE:
                self.beside(part, chip, me.c).start()

        self.origins(fx, fy, k, act)

    def beside(self, part, chip, c):
        i = LATE.index(part)
        ref = self.block(part, chip, c)
        return pltpu.make_async_remote_copy(
            ref, ref, self.lsend.at[i, chip], self.lrecv.at[i, chip], device_id=self.me.to("core"), device_id_type=MESH)

    def arrived(self, part):
        if part not in LATE:
            self.across(part, 1 - self.me.c).wait_recv()
            return

        def body(chip, _):
            self.beside(part, chip, 1 - self.me.c).wait_recv()
            return 0
        lax.fori_loop(0, 16, body, 0)

    def drain(self, part):
        me = self.me
        order = ORDER[part]

        if part in LATE:
            def body(chip, _):
                self.beside(part, chip, me.c).wait_send()
                return 0
            lax.fori_loop(0, 16, body, 0)
        else:
            self.across(part, me.c).wait_send()

        def sent(chip, axes, sign):
            for axis in axes:
                if axis == "z":
                    if sign <= 0:
                        pl.when(me.z < 3)(lambda: self.copy(part, chip, "up").wait_send())
                    if sign >= 0:
                        pl.when(me.z > 0)(lambda: self.copy(part, chip, "down").wait_send())
                else:
                    self.copy(part, chip, axis).wait_send()

        for fx in (0, 1):
            for fy in (0, 1):
                for k in range(4):
                    if fx + fy + k == 0:
                        sent(self.chip(me.x, me.y, me.z), order, 0)
                        continue
                    stage = self.arrival(part, fx, fy, k)
                    axes = order[stage:] if order[stage] == "z" else order[stage + 1:]
                    self.origins(fx, fy, k, lambda chip, sign: sent(
                        chip, axes, sign if order[stage] == "z" else 0))


def relayout(me, wide, refs, name):
    m = pl.multiple_of
    chip = (me.z * 2 + me.x) * 2 + me.y
    wa, wu, wd = refs

    def rows(base, count, stride):
        both = [wide[d, pl.ds(base, count, stride=stride), :] for d in range(2)]
        return jnp.concatenate(both, 0).astype(BF)

    if name == "up":
        for j in range(12):
            wu[pl.ds(m(chip * 48, 16), 48), pl.ds(m((me.c * 12 + j) * 128, 128), 128)] = rows(
                BASE[2] + me.c * 12 + j, 24, 24)
    elif name == "down":
        for j in range(3):
            wd[chip, :, pl.ds(m((me.c * 3 + j) * 128, 128), 128)] = rows(BASE[3] + me.c * 3 + j, 96, 6)
    else:
        for j in range(6):
            wa[pl.ds(m(chip * 48, 16), 48), pl.ds(m(me.c * WIDE + j * 128, 128), 128)] = rows(
                BASE[0] + me.c * 12 + j, 24, 18)
            to = wa.at[pl.ds(m(chip * 48, 16), 48), pl.ds(m(me.c * WIDE + 768 + j * 128, 128), 128)]

            @pl.when(me.c == 0)
            def _():
                to[...] = rows(BASE[0] + 6 + j, 24, 18)

            @pl.when(me.c == 1)
            def _():
                to[...] = rows(BASE[1] + j, 24, 6)


GATHER_PLAN = (

    (16, 0, 48, 17, 1, 64, 18, 4, 32, 25, 8, 19, 2, 5, 21, 26, 27, 24, 3, 68, 6, 7, 49, 65, 12, 23, 22, 40, 20, 33, 80, 29, 72, 52, 30, 10, 9, 13, 11, 31, 50, 66, 36, 56, 28, 15, 14),
    (), (), (), (34,), (), (), (), (), (), (), (37, 51), (67, 84, 57), (), (), (), (), (), (), (), (38, 54),
    (88, 35, 74, 85, 73, 70, 75, 58, 41, 71, 42, 55, 53, 76, 44, 39, 81), (), (), (), (),
    (43, 60, 86, 61, 59, 78, 69), (79, 82, 45), (46, 87, 92, 77, 47, 62, 63, 93, 83), (), (), (), (), (), (), (), (),
    (), (), (), (94, 95, 89, 90, 91),
)

GATHER_X = 0


HEADS = 12
HD = 64
EPS = 1e-05
PAIRS = HEADS // 2

def nt(left, right):
    return lax.dot_general(left, right, (((1,), (1,)), ((), ())), preferred_element_type=F32)


def nn(left, right):
    return jnp.dot(left, right, preferred_element_type=F32)


def tn(left, right):
    return lax.dot_general(left, right, (((0,), (0,)), ((), ())), preferred_element_type=F32)


def tile(i, size):
    return pl.ds(pl.multiple_of(i * size, size), size)


def spread(sides, size, width):
    lane = lax.broadcasted_iota(jnp.int32, (128, width), 0)
    col = lax.broadcasted_iota(jnp.int32, (128, width), 1)
    owner = ((col.astype(F32) + 0.5) * (1.0 / size)).astype(jnp.int32)
    pick = (col - owner * size == lane).astype(F32).astype(BF)
    dev = lax.broadcasted_iota(jnp.int32, (16, width), 0) * 2
    col = lax.broadcasted_iota(jnp.int32, (16, width), 1)
    owner = ((col.astype(F32) + 0.5) * (1.0 / size)).astype(jnp.int32)
    total = jnp.zeros((16, width), F32)
    for c, rows in enumerate(sides):
        total = total + jnp.where(owner == dev + c, nn(rows.astype(BF), pick), 0.0)
    return jnp.sum(total, 0, keepdims=True)


def swap_rows(me, ref, s, send, recv):
    width = 256

    def block(index):
        return ref.at[tile(index, width), :]

    def copy(index, way, n):
        return pltpu.make_async_remote_copy(
            block(index), block(index), send.at[n], recv.at[n], device_id=me.to(way), device_id_type=MESH)

    mine = me.y * 2 + me.c
    over = (1 - me.y) * 2 + me.c
    return (copy(mine, "core", 0), copy(mine, "y", 1), copy(over, "core", 2)), (
        copy(me.y * 2 + 1 - me.c, "core", 0), copy(over, "y", 1), copy((1 - me.y) * 2 + 1 - me.c, "core", 2))


def head_rows(array, axis):
    lane = lax.broadcasted_iota(jnp.int32, array.shape, 1)
    zero = jnp.zeros_like(array)
    return jnp.concatenate([jnp.where(lane < HD, array, zero), jnp.where(lane >= HD, array, zero)], axis)


def forward_kernel(
    fq, fo, fu, fd, s0, s1, s2, s3, s4, s5, s6, s7, s8, x, cot, seg, pad, keep,
    to_out, to_a, to_u, to_d, to_xt, to_v, to_kt, to_e, to_q8, to_ot, to_r, to_actt, to_gp, to_nlt, to_n1, to_r1, to_gs, to_sm,
    flats, wide, wa, wu, wd, smf, xall, kk, vv, kt, vt, st, ee, mask, vec, vecu, n2, xt, act, nl,
    out, hq8, hot, hr, hactt, hgp, hnlt, hn1, hr1, hgs, hsm,
    fsend, frecv, send, recv, csend, crecv, lsend, lrecv, osem, xsend, xrecv,
):
    me = Place()
    s = me.y * 2 + me.c
    outs = []

    def put(held, to):
        outs.append(pltpu.make_async_copy(held, to, osem.at[len(outs)]))
        outs[-1].start()

    enter(me)
    refs = (wa, wu, wd)
    g = Gather(me, refs, send, recv, csend, crecv, lsend, lrecv)
    swaps = [
        pltpu.make_async_remote_copy(
            src, flats.at[pl.ds(b, n), :], fsend.at[i], frecv.at[i], device_id=me.to("core"), device_id_type=MESH)
        for i, (src, b, n) in enumerate(zip((fq, fo, fu, fd), BASE, LINES))
    ]
    for c in swaps:
        c.start()
    chip = (me.z * 2 + me.x) * 2 + me.y
    smf[0, 0:48, :] = jnp.zeros((48, 128), F32)
    for i, vector in enumerate((s0, s1, s2, s3, s4, s5, s6, s7, s8)):
        smf[0, i:i + 1, 0:vector.shape[0]] = vector[...].astype(F32).reshape(1, vector.shape[0])
    wa[pl.ds(pl.multiple_of(chip * 48, 16), 48), pl.ds(pl.multiple_of(me.c * WIDE + 1536, 128), 128)] = (
        smf[0, 0:48, :].astype(BF))
    xall[tile(s, 256), :] = x[...]
    xs, xr = swap_rows(me, xall, s, xsend, xrecv)
    xs[0].start()
    slot = iter(GATHER_PLAN)
    count = {}

    def tick():
        for code in next(slot, ()):
            if sum(count.values()) == GATHER_X:
                xs[1].start()
            p, fx, fy, k = NAMES[code // 16], code // 8 % 2, code // 4 % 2, code % 4
            if fx + fy + k:
                g.serve(p, fx, fy, k)
            else:
                unpack(p)
                g.own(p)
            count[p] = count.get(p, 0) + 1
            if count[p] == 16 and p not in LATE:
                g.across(p, me.c).start()

    unpacked = []

    def unpack(p):
        name = p.rstrip("01")
        if name in unpacked:
            return
        unpacked.append(name)
        for i in {"attn": (0, 1), "up": (2,), "down": (3,)}[name]:
            src, b, n = (fq, fo, fu, fd)[i], BASE[i], LINES[i]
            wide[me.c, pl.ds(b, n), :] = src[...].astype(F32)
            swaps[i].wait_recv()
            wide[1 - me.c, pl.ds(b, n), :] = flats[pl.ds(b, n), :].astype(F32)
        relayout(me, wide, refs, name)

    codes = jnp.where(pad[...] > 0, seg[...], -1).astype(F32)
    mine = seg[:, tile(s, 256)].astype(F32)
    for j in range(8):
        column = jnp.broadcast_to(codes[:, j * 128:(j + 1) * 128], (128, 128)).T
        for i in range(2):
            row = jnp.broadcast_to(mine[:, i * 128:(i + 1) * 128], (128, 128))
            mask[pl.ds(j * 128, 128), pl.ds(i * 128, 128)] = jnp.where(column == row, 0.0, -1e9)

    tick()
    xr[1].wait_recv()
    xs[2].start()
    g.arrived("attn0")
    g.arrived("attn1")
    xr[0].wait_recv()
    xr[2].wait_recv()
    put(wa, to_a)
    for j in range(4):
        xt[:, pl.ds(j * 256, 256)] = xall[pl.ds(j * 256, 256), :].T

    for c in range(2):
        smf[c] = wa[:, pl.ds(c * WIDE + 1536, 128)].astype(F32)
    vec[...] = jnp.zeros_like(vec)
    for i in range(8):
        vec[pl.ds(i, 1), :] = spread([smf[c, pl.ds(i, 16, stride=48), :] for c in range(2)], 24, 768)
    vecu[...] = spread([smf[c, pl.ds(8, 16, stride=48), :] for c in range(2)], 96, 3072)

    tick()
    for j in range(3):
        w = pl.ds(j * 256, 256)
        hq8[:, w] = ((nn(x[...], wa[:, w]) + vec[0:1, w]).astype(BF).astype(F32) * 0.125).astype(BF)
    for j in range(3):
        w = pl.ds(j * 256, 256)
        for r in range(2):
            rows = pl.ds(r * 512, 512)
            tick()
            k = nn(xall[rows, :], wa[:, pl.ds(768 + j * 256, 256)]).astype(BF)
            kk[rows, w] = k
            kt[w, rows] = k.T
            v = (nn(xall[rows, :], wa[:, pl.ds(WIDE + j * 256, 256)]) + vec[1:2, w]).astype(BF)
            vv[rows, w] = v
            vt[w, rows] = v.T
    put(hq8, to_q8)
    put(xt, to_xt)
    put(vv, to_v)
    put(kt, to_kt)

    for p in range(PAIRS):
        w = pl.ds(p * 128, 128)
        qm = head_rows(hq8[:, w], 0)
        tick()
        top = jnp.full((8, 512), -3e38, F32)
        for c in range(4):
            rows = pl.ds(c * 256, 256)
            one = mask[rows, :]
            v = nt(kk[rows, w], qm) + jnp.concatenate([one, one], 1)
            st[rows, :] = v
            top = jnp.maximum(top, jnp.max(v.reshape(32, 8, 512), 0))
        top = jnp.max(top, 0, keepdims=True)
        tick()
        total = jnp.zeros((8, 512), F32)
        for c in range(8):
            rows = pl.ds(c * 128, 128)
            v = jnp.exp(st[rows, :] - top)
            ee[p, rows, :] = v.astype(BF)
            total = total + jnp.sum(v.reshape(16, 8, 512), 0)
        inverse = 1.0 / jnp.sum(total, 0, keepdims=True)
        hr[pl.ds(p, 1), :] = inverse
        tick()
        for h in range(2):
            o = nn(vt[pl.ds(p * 128 + h * 64, 64), :], ee[p, :, pl.ds(h * 256, 256)])
            hot[pl.ds(p * 128 + h * 64, 64), :] = (o * inverse[:, h * 256:(h + 1) * 256]).astype(BF)
        put(ee.at[p], to_e.at[p])

    tick()
    put(hot, to_ot)
    put(hr, to_r)
    n2[...] = tn(hot[...], wa[:, pl.ds(WIDE + 768, 768)])
    tick()
    for r in range(8):
        rows = pl.ds(r * 32, 32)
        value = x[rows, :].astype(F32) + n2[rows, :] + vec[2:3, :]
        centred = value - jnp.mean(value, -1, keepdims=True)
        r1 = lax.rsqrt(jnp.mean(centred * centred, -1, keepdims=True) + EPS)
        n1 = centred * r1
        hn1[rows, :] = n1
        hr1[rows, :] = jnp.broadcast_to(r1, (32, 128))
        normed = n1 * vec[3:4, :] + vec[4:5, :]
        n2[rows, :] = normed
        nl[rows, :] = normed.astype(BF)
    hnlt[...] = nl[...].T
    put(hnlt, to_nlt)
    put(hn1, to_n1)
    put(hr1, to_r1)
    for p in ("attn0", "attn1"):
        g.drain(p)
    tick()
    g.arrived("up0")
    g.arrived("up1")
    put(wu, to_u)

    for j in range(12):
        w = pl.ds(j * 256, 256)
        if j:
            tick()
        before = nn(nl[...], wu[:, w]) + vecu[:, w]
        phi = 0.5 * (1.0 + lax.erf(before * 0.7071067811865476))
        a = (before * phi).astype(BF)
        act[:, w] = a
        hactt[w, :] = a.T
        hgp[:, w] = (phi + before * 0.3989422804014327 * jnp.exp(-0.5 * before * before)).astype(BF)

    tick()
    g.drain("up0")
    g.drain("up1")
    g.arrived("down0")
    g.arrived("down1")
    put(hactt, to_actt)
    put(hgp, to_gp)
    put(wd, to_d)

    for j in range(3):
        w = pl.ds(j * 256, 256)
        n2[:, w] += nn(act[...], wd[:, :, w].reshape(3072, 256)) + vec[5:6, w]
    hsm[...] = jnp.zeros_like(hsm)
    hsm[2:3, :] = vec[3:4, :]
    kept = keep[...] > 0
    gain = jnp.zeros((8, 768), F32)
    shift = jnp.zeros((8, 768), F32)
    for r in range(8):
        rows = pl.ds(r * 32, 32)
        value = n2[rows, :]
        centred = value - jnp.mean(value, -1, keepdims=True)
        r2 = lax.rsqrt(jnp.mean(centred * centred, -1, keepdims=True) + EPS)
        n = centred * r2
        out[rows, :] = jnp.where(kept, n * vec[6:7, :] + vec[7:8, :], x[rows, :].astype(F32)).astype(BF)
        grad = jnp.where(kept, cot[rows, :].astype(F32), 0.0)
        gain = gain + jnp.sum((grad * n).reshape(4, 8, 768), 0)
        shift = shift + jnp.sum(grad.reshape(4, 8, 768), 0)
        c = grad * vec[6:7, :]
        hgs[rows, :] = r2 * (c - jnp.mean(c, -1, keepdims=True) - n * jnp.mean(c * n, -1, keepdims=True))
    hsm[0:1, :] = jnp.sum(gain, 0, keepdims=True)
    hsm[1:2, :] = jnp.sum(shift, 0, keepdims=True)
    put(out, to_out)
    put(hgs, to_gs)
    put(hsm, to_sm)

    g.drain("down0")
    g.drain("down1")
    for c in swaps:
        c.wait_send()
    for c in xs:
        c.wait_send()
    for o in outs:
        o.wait()


FORWARD_OUT = (
    ((256, 768), BF), ((768, 2 * WIDE), BF), ((768, 3072), BF), ((16, 192, 768), BF), ((768, 1024), BF),
    ((1024, 768), BF), ((768, 1024), BF), ((PAIRS, 1024, 512), BF), ((256, 768), BF), ((768, 256), BF),
    ((8, 512), F32), ((3072, 256), BF), ((256, 3072), BF), ((768, 256), BF), ((256, 768), F32), ((256, 128), F32),
    ((256, 768), F32), ((8, 768), F32),
)


def forward_call(*args):
    a = pl.BlockSpec(memory_space=pl.ANY)
    v = pl.BlockSpec(memory_space=pltpu.VMEM)
    n = len(PARTS)
    dma = pltpu.SemaphoreType.DMA
    return pl.pallas_call(
        forward_kernel,
        out_shape=[jax.ShapeDtypeStruct(s, d) for s, d in FORWARD_OUT],
        in_specs=[v] * 18,
        out_specs=[a] * len(FORWARD_OUT),
        scratch_shapes=[
            pltpu.VMEM((1728, 128), BF), pltpu.VMEM((2, 1728, 128), F32),
            pltpu.VMEM((768, 2 * WIDE), BF), pltpu.VMEM((768, 3072), BF),
            pltpu.VMEM((16, 192, 768), BF), pltpu.VMEM((2, 768, 128), F32),
            pltpu.VMEM((1024, 768), BF), pltpu.VMEM((1024, 768), BF), pltpu.VMEM((1024, 768), BF),
            pltpu.VMEM((768, 1024), BF), pltpu.VMEM((768, 1024), BF), pltpu.VMEM((1024, 512), F32),
            pltpu.VMEM((PAIRS, 1024, 512), BF), pltpu.VMEM((1024, 256), F32), pltpu.VMEM((8, 768), F32),
            pltpu.VMEM((1, 3072), F32), pltpu.VMEM((256, 768), F32), pltpu.VMEM((768, 1024), BF),
            pltpu.VMEM((256, 3072), BF), pltpu.VMEM((256, 768), BF),
            pltpu.VMEM((256, 768), BF), pltpu.VMEM((256, 768), BF), pltpu.VMEM((768, 256), BF),
            pltpu.VMEM((8, 512), F32), pltpu.VMEM((3072, 256), BF), pltpu.VMEM((256, 3072), BF),
            pltpu.VMEM((768, 256), BF), pltpu.VMEM((256, 768), F32), pltpu.VMEM((256, 128), F32),
            pltpu.VMEM((256, 768), F32), pltpu.VMEM((8, 768), F32),
            dma((4,)), dma((4,)), dma((n, 16, 4)), dma((n, 16)), dma((n,)), dma((n,)), dma((2, 16)), dma((2, 16)), dma((24,)), dma((3,)), dma((3,)),
        ],
        compiler_params=pltpu.CompilerParams(collective_id=1, has_side_effects=True, vmem_limit_bytes=62 << 20),
        name="forward",
    )(*args)


RPARTS = (
    ("down", 3, "yzx", 192, 0, 0, 384),
    ("up", 2, "xzy", 48, 0, 0, 1536),
    ("out", 1, "zyx", 48, 0, 0, 384),
    ("qkv0", 0, "zyx", 48, 0, 0, 384),
    ("qkv1", 0, "zyx", 48, 0, 384, 384),
    ("qkv2", 0, "zxy", 48, 0, 768, 384),
)
HALF = (1152, 384, 1536, 384)
CHIPROWS = (48, 48, 48, 192)
ROWS = (768, 768, 768, 3072)
SIZES = {"x": 2, "y": 2, "z": 4}
LINKS = ("up", "down", "x", "y")


def slots(order, axis):
    n = 4 if axis == "z" else 1
    for a in order[: order.index(axis)]:
        n *= SIZES[a]
    return n


def landing_shapes():
    shapes = []
    for name, mat, order, rows, ro, co, cols in RPARTS:
        for way in LINKS:
            axis = "z" if way in ("up", "down") else way
            shapes.append(pltpu.VMEM((slots(order, axis), rows, cols), BF))
    return shapes


class Scatter:
    def __init__(self, me, grads, half, lands, finals, send, recv):
        self.me, self.grads, self.half, self.lands, self.finals = me, grads, half, lands, finals
        self.send, self.recv = send, recv

    def chip(self, x, y, z):
        return (z * 2 + x) * 2 + y

    def part(self, refs, i, dest):
        name, mat, order, rows, ro, co, cols = RPARTS[i]
        first = pl.multiple_of(self.chip(*dest) * CHIPROWS[mat] + ro, 16)
        return refs[mat].at[pl.ds(first, rows), pl.ds(co, cols)]

    def block(self, i, dest):
        return self.part(self.grads, i, dest)

    def slot(self, i, way, dest):
        order = RPARTS[i][2]
        axis = "z" if way in ("up", "down") else way
        coords = dict(zip("xyz", dest))
        index = coords["z"] if axis == "z" else 0
        for a in order[: order.index(axis)]:
            index = index * SIZES[a] + coords[a]
        return index

    def land(self, i, way, dest):
        return self.lands[i * 4 + LINKS.index(way)].at[self.slot(i, way, dest)]

    def copy(self, i, way, dest):
        chip = self.chip(*dest)
        return pltpu.make_async_remote_copy(
            self.block(i, dest), self.land(i, way, dest), self.send.at[i, chip],
            self.recv.at[i, LINKS.index(way), chip], device_id=self.me.to(way), device_id_type=MESH)

    def stage(self, i, fx, fy, k):
        moved = {"x": fx, "y": fy, "z": k}
        return max(s for s in range(3) if moved[RPARTS[i][2][s]])

    def take(self, i, way, dest):
        self.copy(i, way, dest).wait_recv()
        ref = self.block(i, dest)
        ref[...] = ref[...] + self.land(i, way, dest)[...]

    def total(self, i, dest, ways):
        value = self.block(i, dest)[...] + self.part(self.half, i, dest)[...]
        for way in ways:
            self.copy(i, way, dest).wait_recv()
            value = value + self.land(i, way, dest)[...]
        return value

    def serve(self, i, fx, fy, k):
        me = self.me
        order = RPARTS[i][2]
        stage = self.stage(i, fx, fy, k)
        axis = order[stage]

        def act(dest, sign):
            way = axis
            if axis == "z":
                way, more = ("down", me.z < 3) if sign < 0 else ("up", me.z > 0)
                pl.when(more)(lambda: self.take(i, way, dest))
            if "z" in order[stage + 1:]:
                pl.when(me.z < 3)(lambda: self.take(i, "down", dest))
                pl.when(me.z > 0)(lambda: self.take(i, "up", dest))
            value = self.total(i, dest, [a for a in order[stage + 1:] if a != "z"])
            self.block(i, dest)[...] = value
            self.copy(i, way, dest).start()

        self.dests(fx, fy, k, act)

    def dests(self, fx, fy, k, act):
        me = self.me
        x = 1 - me.x if fx else me.x
        y = 1 - me.y if fy else me.y
        if k == 0:
            act((x, y, me.z), 0)
        else:
            pl.when(me.z >= k)(lambda: act((x, y, me.z - k), -1))
            pl.when(me.z + k <= 3)(lambda: act((x, y, me.z + k), 1))

    def own(self, i):
        dest = (self.me.x, self.me.y, self.me.z)
        name, mat, order, rows, ro, co, cols = RPARTS[i]
        self.finals[mat].at[pl.ds(ro, rows), pl.ds(co, cols)][...] = (
            self.block(i, dest)[...].astype(F32) + self.part(self.half, i, dest)[...].astype(F32))

    def finish(self, i):
        name, mat, order, rows, ro, co, cols = RPARTS[i]
        me = self.me
        dest = (me.x, me.y, me.z)
        fin = self.finals[mat].at[pl.ds(ro, rows), pl.ds(co, cols)]

        def add(way):
            self.copy(i, way, dest).wait_recv()
            fin[...] += self.land(i, way, dest)[...].astype(F32)
        for axis in order:
            if axis == "z":
                pl.when(me.z < 3)(lambda: add("down"))
                pl.when(me.z > 0)(lambda: add("up"))
            else:
                add(axis)

    def drain(self, i):
        for fx in (0, 1):
            for fy in (0, 1):
                for k in range(4):
                    if fx + fy + k:
                        axis = RPARTS[i][2][self.stage(i, fx, fy, k)]
                        self.dests(fx, fy, k, lambda dest, sign: self.copy(
                            i, axis if axis != "z" else ("down" if sign < 0 else "up"), dest).wait_send())


SCATTER_PLAN = (
    (11, 15, 10, 14), (), (), (), (), (), (), (), (), (3,), (), (), (), (), (), (), (), (31, 7, 23, 9, 29), (), (),
    (), (8, 2), (), (), (), (), (27, 30, 22, 12), (), (), (), (), (6, 21, 46, 13, 19, 1), (), (), (), (), (), (), (),
    (), (), (), (), (), (), (), (), (), (20, 61, 47, 45, 60, 18, 26, 62, 63, 28, 56), (), (), (), (), (), (), (), (),
    (), (53, 5, 79, 77, 78, 37, 52, 17, 39, 38, 25, 57, 55, 76, 59), (), (), (), (),
    (41, 40, 54, 75, 43, 58, 71, 69, 74, 70), (), (), (), (), (95, 94, 42, 51, 93, 87, 92, 85, 72, 67),
    (86, 91, 35, 44, 73, 50, 90), (66, 89, 4, 68, 24, 83), (36, 34, 84, 49, 88), (82, 65), (33,), (81, 0), (16,), (),
    (32,), (64, 48, 80),
)

FLATROWS = ((24, 18, 432), (24, 6, 144), (24, 24, 576), (96, 6, 576))


def column(mat, c, j):
    if mat:
        return c * (FLATROWS[mat][1] // 2) + j
    group, t = j // 3, j % 3
    if c == 0:
        return 2 * group + t if t < 2 else 6 + 2 * group
    return 7 + 2 * group if t == 0 else 11 + 2 * group + t


def flatten(me, mat, finals, sides, out):
    rows, tiles, lines = FLATROWS[mat]
    half = tiles // 2
    for c in range(2):
        @pl.when(me.c == c)
        def _():
            for j in range(half):
                mine = finals[mat][pl.ds(pl.multiple_of(me.c * rows, 8), rows), pl.ds(j * 128, 128)]
                out[pl.ds(column(mat, c, j), rows, stride=tiles), :] = mine
                out[pl.ds(column(mat, 1 - c, j), rows, stride=tiles), :] = sides[mat][:, pl.ds(j * 128, 128)]


def colsum(array):
    return jnp.sum(array.astype(F32), 0, keepdims=True)


def backward_kernel(
    ha, hu, hd, hxt, hv, hkt, he, *rest,
):
    far, keep, rest = rest[:11], rest[11], rest[12:]
    (ingrad, oq, oo, ou, od, chosen), rest = rest[:6], rest[6:]
    near, rest = rest[:11], rest[11:]
    q8, ot, rr, actt, gp, nlt, n1, r1, gs, sm0, cot = near
    lands, rest = rest[:4 * len(RPARTS)], rest[4 * len(RPARTS):]
    grads, rest = rest[:4], rest[4:]
    stage, rest = rest[:3], rest[3:]
    stage = (stage[1].at[:, pl.ds(0, HALF[0])],) + tuple(stage)
    half, rest = rest[:4], rest[4:]
    finals, rest = rest[:4], rest[4:]
    sides, rest = rest[:4], rest[4:]
    (wbig, wo, xt, vv, kt, ee, ds, gbr, gbef, first, gts, gsa, dq, dkv, dx, dxc, dxy, acc, sland, osm,
     nsem, wsem, isem, esem, csend, crecv, send, recv, fsend, frecv, dsend, drecv, asend, arecv) = rest
    me = Place()
    s = me.y * 2 + me.c
    wds = [pltpu.make_async_copy(hd.at[pl.ds(q * 768, 768), :], wbig.at[pl.ds(q * 768, 768), :], wsem.at[q]) for q in range(4)]
    wus = [pltpu.make_async_copy(hu.at[:, pl.ds(q * 768, 768)], wbig.at[pl.ds(q * 768, 768), :], wsem.at[4 + q]) for q in range(4)]
    wqs = [pltpu.make_async_copy(ha.at[:, pl.ds((0, 768, WIDE)[q], 768)], wbig.at[pl.ds(q * 768, 768), :], wsem.at[8 + q]) for q in range(3)]
    others = [pltpu.make_async_copy(a, b, isem.at[i]) for i, (a, b) in enumerate(((ha.at[:, pl.ds(WIDE + 768, 768)], wo), (hv, vv), (hkt, kt), (hxt, xt)))]
    ees = [pltpu.make_async_copy(he.at[p], ee.at[p % 2], esem.at[p]) for p in range(PAIRS)]
    nears = [pltpu.make_async_copy(a, b, nsem.at[i]) for i, (a, b) in enumerate(zip(far, near))]
    for i in (8, 9, 3):
        nears[i].start()
    for c in wds:
        c.start()
    nears[4].start()
    enter(me)

    sc = Scatter(me, grads, half, lands, finals, send, recv)

    def swap(mat, piece=0):
        cut = {
            0: (slice(None), pl.ds(piece * 384, 384)), 1: (slice(None), slice(None)),
            2: (slice(None), pl.ds(piece * 512, 512)), 3: (pl.ds(piece * 768, 768), slice(None)),
        }[mat]
        n = (0, 3, 4, 7)[mat] + piece
        return pltpu.make_async_remote_copy(
            stage[mat].at[cut], half[mat].at[cut], csend.at[n], crecv.at[n], device_id=me.to("core"), device_id_type=MESH)

    def last(mat):
        rows = FLATROWS[mat][0]
        src = finals[mat].at[pl.ds(pl.multiple_of((1 - me.c) * rows, 8), rows), :]
        return pltpu.make_async_remote_copy(
            src, sides[mat], fsend.at[mat], frecv.at[mat], device_id=me.to("core"), device_id_type=MESH)

    def swapped(mat):
        for piece in range((3, 1, 3, 4)[mat]):
            swap(mat, piece).wait_recv()

    def unstaged(mat):
        for piece in range((3, 1, 3, 4)[mat]):
            swap(mat, piece).wait_send()

    slot = iter(SCATTER_PLAN)
    count = {}

    def tick():
        for code in next(slot, ()):
            i, fx, fy, k = code // 16, code // 8 % 2, code // 4 % 2, code % 4
            if fx + fy + k:
                sc.serve(i, fx, fy, k)
            else:
                sc.own(i)
                sc.finish(i)
                mat = RPARTS[i][1]
                count[mat] = count.get(mat, 0) + 1
                if count[mat] == (3, 1, 1, 1)[mat]:
                    last(mat).start()

    def arrange(value_ref, to):
        to[:, 0:384] = value_ref[:, pl.ds(pl.multiple_of(me.c * 384, 128), 384)]
        to[:, 384:768] = value_ref[:, pl.ds(pl.multiple_of((1 - me.c) * 384, 128), 384)]

    osm[...] = jnp.zeros_like(osm)
    for i in (8, 9):
        nears[i].wait()
    osm[6:8, :] = sm0[0:2, :]
    gsa[...] = gs[...].astype(BF)
    osm[5:6, :] = colsum(gsa[...])
    arrange(gsa, gbr)
    nears[3].wait()

    for j in range(12):
        w = pl.ds(j * 256, 256)
        v = nn(actt[w, :], gbr[...]).astype(BF)
        grads[3][w, :] = v[:, 0:384]
        stage[3][w, :] = v[:, 384:768]
        if j % 3 == 2:
            swap(3, j // 3).start()

    for i in (5, 6, 7, 1, 2):
        nears[i].start()
    nears[4].wait()
    for q in range(4):
        wds[q].wait()
        for j in range(3):
            w = pl.ds(q * 768 + j * 256, 256)
            gb = nt(gsa[...], wbig[w, :]).astype(BF) * gp[:, w]
            gbef[:, w] = gb
            osm[8 + q:9 + q, pl.ds(j * 256, 256)] = colsum(gb)
        wus[q].start()
        if q == 0:
            swapped(3)
        tick()

    for i in (0, 10):
        nears[i].start()
    for c in others:
        c.start()
    ees[0].start()
    ees[1].start()
    for i in (5, 6, 7, 1, 2):
        nears[i].wait()
    for j in range(6):
        w = pl.ds(j * 256, 256)
        tick()
        stage[2][:, w] = nn(nlt[...], gbef[:, pl.ds(pl.multiple_of((1 - me.c) * 1536 + j * 256, 256), 256)]).astype(BF)
        if j % 2:
            swap(2, j // 2).start()
    for j in range(6):
        w = pl.ds(j * 256, 256)
        tick()
        grads[2][:, w] = nn(nlt[...], gbef[:, pl.ds(pl.multiple_of(me.c * 1536 + j * 256, 256), 256)]).astype(BF)
    for c in wus:
        c.wait()
    tick()
    swapped(2)

    for j in range(3):
        w = pl.ds(j * 256, 256)
        tick()
        total = gs[:, w]
        for q in range(4):
            total += nt(gbef[:, pl.ds(q * 768, 768)], wbig[pl.ds(q * 768 + j * 256, 256), :])
        first[:, w] = total
    for c in wqs:
        c.start()

    gain = jnp.zeros((8, 768), F32)
    shift = jnp.zeros((8, 768), F32)
    for r in range(8):
        rows = pl.ds(r * 32, 32)
        if r % 4 == 0:
            tick()
        gn = first[rows, :]
        n = n1[rows, :]
        gain = gain + jnp.sum((gn * n).reshape(4, 8, 768), 0)
        shift = shift + jnp.sum(gn.reshape(4, 8, 768), 0)
        c1 = gn * sm0[2:3, :]
        gf = r1[rows, 0:1] * (c1 - jnp.mean(c1, -1, keepdims=True) - n * jnp.mean(c1 * n, -1, keepdims=True))
        first[rows, :] = gf
        gsa[rows, :] = gf.astype(BF)
    osm[3:4, :] = jnp.sum(gain, 0, keepdims=True)
    osm[4:5, :] = jnp.sum(shift, 0, keepdims=True)
    osm[2:3, :] = colsum(gsa[...])
    arrange(gsa, gbr)
    tick()

    for j in range(3):
        w = pl.ds(j * 256, 256)
        v = nn(ot[w, :], gbr[...]).astype(BF)
        grads[1][w, :] = v[:, 0:384]
        stage[1][w, :] = v[:, 384:768]
    swap(1).start()
    for c in others:
        c.wait()
    for i in (0, 10):
        nears[i].wait()
    for p in range(PAIRS):
        w = pl.ds(p * 128, 128)
        if p % 2 == 0:
            tick()
        g = nt(wo[w, :], gsa[...]).astype(BF).astype(F32)
        scale = jnp.concatenate(
            [jnp.broadcast_to(rr[p:p + 1, h * 256:(h + 1) * 256], (64, 256)) for h in range(2)], 0)
        gts[w, :] = (g * scale).astype(BF)
    swapped(1)

    mine = xt.at[:, tile(s, 256)]

    def qkv_grads(group):
        q = pl.ds(group * 256, 256)
        v = pl.ds(768 + group * 256, 256)
        mid = pl.ds(group * 384, 384)

        def put(r, a, b):
            rows = pl.ds(r * 256, 256)
            vq = nn(mine[rows, :], dq[:, q]).astype(BF)
            vk = nn(xt[rows, :], dkv[:, q]).astype(BF)
            vv_ = nn(xt[rows, :], dkv[:, v]).astype(BF)
            a[rows, pl.ds(group * 384, 256)] = vq
            a[rows, pl.ds(group * 384 + 256, 128)] = vk[:, 0:128]
            b[rows, pl.ds(group * 384, 128)] = vk[:, 128:256]
            b[rows, pl.ds(group * 384 + 128, 256)] = vv_

        for r in range(3):
            tick()
            pl.when(me.c == 0)(lambda: put(r, grads[0], stage[0]))
            pl.when(me.c == 1)(lambda: put(r, stage[0], grads[0]))
        swap(0, group).start()

    for p in range(PAIRS):
        w = pl.ds(p * 128, 128)
        g = gts[w, :]
        both = ot[w, :].astype(F32) * g.astype(F32)
        delta = jnp.concatenate([jnp.sum(both[0:64], 0, keepdims=True), jnp.sum(both[64:128], 0, keepdims=True)], 1)
        gm = head_rows(g.T, 0)
        qm = head_rows(q8[:, w], 0)
        ees[p].wait()
        e = ee.at[p % 2]
        for c in range(4):
            rows = pl.ds(c * 256, 256)
            if c % 2 == 0:
                tick()
            dp = nt(vv[rows, w], gm)
            ds[rows, :] = e[rows, :] * (dp - delta).astype(BF)
        tick()
        dkv[:, w] = nn(ds[...], qm).astype(BF)
        tick()
        dkv[:, pl.ds(768 + p * 128, 128)] = nn(e[...], gm).astype(BF)
        tick()
        dqt = jnp.concatenate([
            nn(kt[pl.ds(p * 128 + h * 64, 64), :], ds[:, pl.ds(h * 256, 256)]) for h in range(2)], 0)
        dq[:, w] = (dqt * 0.125).astype(BF).T
        if p + 2 < PAIRS:
            ees[p + 2].start()
        if p == 1:
            unstaged(2)
        if p % 2:
            qkv_grads(p // 2)
        if p in (2, 4):
            swap(0, p // 2 - 1).wait_recv()
            tick()

    osm[0:1, :] = colsum(dq[...])
    osm[1:2, :] = colsum(dkv[:, pl.ds(768, 768)])

    acc[0] = osm[...]
    pairz = {"outer": (me.z + 1 - 2 * (me.z % 2)) * 2 + me.x}
    smalls = [
        pltpu.make_async_remote_copy(acc.at[i], sland.at[i], asend.at[i], arecv.at[i], device_id=to, device_id_type=MESH)
        for i, to in enumerate((me.to("core"), me.to("x"), me.to("y"), pairz, me.to("far")))
    ]
    smalls[0].start()

    def small_step(i):
        smalls[i].wait_recv()
        acc[i + 1] = acc[i] + sland[i]
        if i < 4:
            smalls[i + 1].start()

    for c in wqs:
        c.wait()

    for j in range(3):
        w = pl.ds(j * 256, 256)
        for r in range(2):
            rows = pl.ds(r * 512, 512)
            if j == 0 and r == 1:
                swap(0, 2).wait_recv()
            tick()
            dx[rows, w] = (
                nt(dkv[rows, 0:768], wbig[pl.ds(768 + j * 256, 256), :])
                + nt(dkv[rows, 768:1536], wbig[pl.ds(1536 + j * 256, 256), :])).astype(BF)
            if r:
                small_step(j)
        first[:, w] += nt(dq[...], wbig[w, :])

    def dx_copy(n):
        if n < 2:
            yy = me.y if n == 0 else 1 - me.y
            return pltpu.make_async_remote_copy(
                dx.at[tile(yy * 2 + 1 - me.c, 256), :], dxc.at[n], dsend.at[n], drecv.at[n],
                device_id=me.to("core"), device_id_type=MESH)
        return pltpu.make_async_remote_copy(
            dx.at[tile((1 - me.y) * 2 + me.c, 256), :], dxy, dsend.at[2], drecv.at[2],
            device_id=me.to("y"), device_id_type=MESH)
    dx_copy(1).start()
    dx_copy(0).start()
    dx_copy(1).wait_recv()
    over = tile((1 - me.y) * 2 + me.c, 256)
    dx[over, :] = (dx[over, :].astype(F32) + dxc[1].astype(F32)).astype(BF)
    dx_copy(2).start()

    for i in range(5):
        tick()
        if i < 2:
            small_step(3 + i)
    tick()
    owner = ((me.z * 2 + me.x) * 4 + s).astype(F32)
    at = lax.broadcasted_iota(jnp.int32, (768, 128), 0).astype(F32)
    lane = lax.broadcasted_iota(jnp.int32, (768, 128), 1).astype(F32)

    def choose(rows, start, size):
        pick = jnp.where((at == start + lane) & (lane < size), 1.0, 0.0)
        return jnp.dot(rows, pick, precision=lax.Precision.HIGHEST, preferred_element_type=F32)
    up = jnp.zeros((8, 128), F32)
    for q in range(4):
        up = up + choose(acc[5, 8 + q:9 + q, :], owner * 96 - q * 768, 96)
    chosen[0:8, :] = choose(acc[5, 0:8, :], owner * 24, 24)
    chosen[8:16, :] = up
    dx_copy(0).wait_recv()
    dx_copy(2).wait_recv()
    total = first[...] + dx[tile(s, 256), :].astype(F32) + dxc[0].astype(F32) + dxy[...].astype(F32)
    ingrad[...] = jnp.where(keep[...] > 0, total, cot[...].astype(F32)).astype(BF)
    for i in range(len(RPARTS)):
        sc.drain(i)
    for mat in (3, 1, 0):
        unstaged(mat)
    for n in range(3):
        dx_copy(n).wait_send()
    for c in smalls:
        c.wait_send()
    for mat in (3, 2, 1, 0):
        last(mat).wait()
        flatten(me, mat, finals, sides, (oq, oo, ou, od)[mat])


def backward_call(*args):
    a = pl.BlockSpec(memory_space=pl.ANY)
    v = pl.BlockSpec(memory_space=pltpu.VMEM)
    dma = pltpu.SemaphoreType.DMA
    outs = [((256, 768), BF)] + [((FLATROWS[m][2], 128), F32) for m in range(4)] + [((16, 128), F32)]
    halves = [(ROWS[m], HALF[m]) for m in range(4)]
    return pl.pallas_call(
        backward_kernel,
        out_shape=[jax.ShapeDtypeStruct(s, d) for s, d in outs],
        in_specs=[a] * 18 + [v],
        out_specs=[v] * 6,
        scratch_shapes=[pltpu.VMEM(s, d) for s, d in FORWARD_OUT[8:]] + [pltpu.VMEM((256, 768), BF)]
        + landing_shapes()
        + [pltpu.VMEM(h, BF) for h in halves + halves[1:] + halves]
        + [pltpu.VMEM((CHIPROWS[m], HALF[m]), F32) for m in range(4)]
        + [pltpu.VMEM((FLATROWS[m][0], HALF[m]), F32) for m in range(4)]
        + [
            pltpu.VMEM((3072, 768), BF), pltpu.VMEM((768, 768), BF), pltpu.VMEM((768, 1024), BF),
            pltpu.VMEM((1024, 768), BF), pltpu.VMEM((768, 1024), BF), pltpu.VMEM((2, 1024, 512), BF),
            pltpu.VMEM((1024, 512), BF), pltpu.VMEM((256, 768), BF), pltpu.VMEM((256, 3072), BF),
            pltpu.VMEM((256, 768), F32), pltpu.VMEM((768, 256), BF), pltpu.VMEM((256, 768), BF),
            pltpu.VMEM((256, 768), BF), pltpu.VMEM((1024, 1536), BF), pltpu.VMEM((1024, 768), BF),
            pltpu.VMEM((2, 256, 768), BF), pltpu.VMEM((256, 768), BF), pltpu.VMEM((6, 16, 768), F32),
            pltpu.VMEM((5, 16, 768), F32), pltpu.VMEM((16, 768), F32),
            dma((11,)), dma((11,)), dma((4,)), dma((PAIRS,)), dma((11,)), dma((11,)), dma((len(RPARTS), 16)), dma((len(RPARTS), 4, 16)),
            dma((4,)), dma((4,)), dma((3,)), dma((3,)), dma((5,)), dma((5,)),
        ],
        compiler_params=pltpu.CompilerParams(collective_id=2, has_side_effects=True, vmem_limit_bytes=63 << 20),
        name="backward",
    )(*args)


SMALL_SIZES = (24,) * 8 + (96,)


def finish_kernel(*refs):
    ins, small, outs, smalls = refs[:6], refs[6], refs[7:13], refs[13:22]
    for a, b in zip(ins, outs):
        b[...] = a[...]
    for i, (to, size) in enumerate(zip(smalls, SMALL_SIZES)):
        to[...] = small[i, 0:size]


def finish_call(*args):
    v = pl.BlockSpec(memory_space=pltpu.VMEM)
    return pl.pallas_call(
        finish_kernel,
        out_shape=[jax.ShapeDtypeStruct(x.shape, x.dtype) for x in args[:6]]
        + [jax.ShapeDtypeStruct((size,), F32) for size in SMALL_SIZES],
        in_specs=[v] * 7,
        out_specs=[v] * 15,
        name="finish",
    )(*args)


AXES = ("outer", "inner", "seq")
SMALLS = (1, 2, 4, 5, 6, 10, 11, 12, 8)


def to_part(flat):
    inner = lax.axis_size("inner")
    if inner == 1:
        return flat
    every = lax.all_gather(flat, ("inner", "seq"), axis=0, tiled=True)
    size = flat.shape[0] * inner
    return lax.dynamic_slice_in_dim(every, lax.axis_index("seq") * size, size, 0)


def whole_scatter(part):
    inner = lax.axis_size("inner")
    if inner == 1:
        return part
    every = lax.psum(lax.all_gather(part, "seq", axis=0, tiled=True), "inner")
    size = part.shape[0] // inner
    index = lax.axis_index("inner") * lax.axis_size("seq") + lax.axis_index("seq")
    return lax.dynamic_slice_in_dim(every, index * size, size, 0)


def shards(inputs, *rest):
    params, (cotangent, segment_ids, pad_mask, keep_flag) = rest[:13], rest[13:]
    parts = [to_part(p) for p in params]
    x, cot = inputs[0], cotangent[0]
    keep = keep_flag.reshape(1, 1)
    out, *held = forward_call(
        *(parts[i].reshape(-1, 128) for i in (0, 3, 7, 9)), *(parts[i] for i in SMALLS), x, cot, segment_ids, pad_mask, keep
    )
    held[2] = held[2].reshape(FF, D)
    grad, *big, small = backward_call(*held, cot, keep)
    out, grad, *rest = finish_call(out, grad, *big, small)
    big = [whole_scatter(part.reshape(-1)) for part in rest[:4]]
    q, v, ob, g1, b1, db, g2, b2, ub = (whole_scatter(part) for part in rest[4:])
    return (out[None], grad[None], big[0], q, v, big[1], ob, g1, b1, big[2], ub, big[3], db, g2, b2)


def solution(mesh):
    fsdp, seq = mesh.shape["fsdp"], mesh.shape["seq"]
    mesh = Mesh(mesh.devices.reshape(8, fsdp // 8, seq), AXES)
    tokens = P(("outer", "inner"), "seq", None)
    flat = P(AXES)
    rows = P(("outer", "inner"), None)
    return jax.shard_map(
        shards,
        mesh=mesh,
        in_specs=(tokens,) + (flat,) * 13 + (tokens, rows, rows, P(("outer", "inner"))),
        out_specs=(tokens, tokens) + (flat,) * 13,
        check_vma=False,
    )
```

```python
import functools
import jax
import jax.numpy as jnp
from jax import lax
from jax.experimental import pallas as pl
from jax.experimental.pallas import tpu as pltpu
from jax.sharding import Mesh, PartitionSpec as P

MESH = pl.DeviceIdType.MESH
D = 768
FF = 3072
BF = jnp.bfloat16
F32 = jnp.float32
LINES = (432, 144, 576, 576)
BASE = (0, 432, 576, 1152)
WIDE = 1664


class Place:
    def __init__(self):
        o = lax.axis_index("outer")
        s = lax.axis_index("seq")
        self.z, self.x, self.y, self.c = o // 2, o % 2, s // 2, s % 2

    def to(self, way):
        z, x, y, c = self.z, self.x, self.y, self.c
        return {
            "up": {"outer": (z + 1) * 2 + x},
            "down": {"outer": (z - 1) * 2 + x},
            "x": {"outer": z * 2 + 1 - x},
            "y": {"seq": (1 - y) * 2 + c},
            "core": {"seq": y * 2 + 1 - c},
            "far": {"outer": (3 - z) * 2 + x},
        }[way]


def greet(me, semaphore):
    def say(to):
        pl.semaphore_signal(semaphore, 1, device_id=to, device_id_type=MESH)

    for way in ("x", "y", "core"):
        say(me.to(way))
    pl.when(me.z < 3)(lambda: say(me.to("up")))
    pl.when(me.z > 0)(lambda: say(me.to("down")))
    pl.when((me.z == 0) | (me.z == 3))(lambda: say(me.to("far")))


def enter(me):
    bar = pltpu.get_barrier_semaphore()
    greet(me, bar)
    pl.semaphore_wait(bar, 5)


WAYS = ("up", "down", "x", "y")

PARTS = (
    ("attn0", "yzx"),
    ("attn1", "zxy"),
    ("up0", "yzx"),
    ("up1", "xzy"),
    ("down0", "zxy"),
    ("down1", "yzx"),
)
LATE = ("down0", "down1")
NAMES = [p[0] for p in PARTS]
ORDER = dict(PARTS)


class Gather:
    def __init__(self, me, refs, send, recv, csend, crecv, lsend, lrecv):
        self.me = me
        self.refs = refs
        self.send, self.recv, self.csend, self.crecv = send, recv, csend, crecv
        self.lsend, self.lrecv = lsend, lrecv

    def block(self, part, chip, c):
        wa, wu, wd = self.refs
        m = pl.multiple_of
        if part in LATE:
            return wd.at[pl.ds(m(chip * 192 + 96 * LATE.index(part), 16), 96), pl.ds(m(c * 384, 128), 384)]
        rows = pl.ds(m(chip * 48, 16), 48)
        if part == "attn0":
            return wa.at[rows, pl.ds(m(c * WIDE, 128), 768)]
        if part == "attn1":
            return wa.at[rows, pl.ds(m(c * WIDE + 768, 128), 896)]
        if part == "up0":
            return wu.at[rows, pl.ds(m(c * 1536, 128), 768)]
        return wu.at[rows, pl.ds(m(c * 1536 + 768, 128), 768)]

    def half(self, part, c):
        wa, wu, wd = self.refs
        m = pl.multiple_of
        if part == "attn0":
            return wa.at[:, pl.ds(m(c * WIDE, 128), 768)]
        if part == "attn1":
            return wa.at[:, pl.ds(m(c * WIDE + 768, 128), 896)]
        if part == "up0":
            return wu.at[:, pl.ds(m(c * 1536, 128), 768)]
        return wu.at[:, pl.ds(m(c * 1536 + 768, 128), 768)]

    def chip(self, x, y, z):
        return (z * 2 + x) * 2 + y

    def copy(self, part, chip, way):
        i = NAMES.index(part)
        ref = self.block(part, chip, self.me.c)
        return pltpu.make_async_remote_copy(
            ref, ref, self.send.at[i, chip, WAYS.index(way)], self.recv.at[i, chip],
            device_id=self.me.to(way), device_id_type=MESH)

    def across(self, part, c):
        i = NAMES.index(part)
        ref = self.half(part, c)
        return pltpu.make_async_remote_copy(
            ref, ref, self.csend.at[i], self.crecv.at[i], device_id=self.me.to("core"), device_id_type=MESH)

    def onward(self, part, chip, axes):
        me = self.me
        for axis in axes:
            if axis == "z":
                pl.when(me.z < 3)(lambda: self.copy(part, chip, "up").start())
                pl.when(me.z > 0)(lambda: self.copy(part, chip, "down").start())
            else:
                self.copy(part, chip, axis).start()

    def own(self, part):
        me = self.me
        chip = self.chip(me.x, me.y, me.z)
        self.onward(part, chip, ORDER[part])
        if part in LATE:
            self.beside(part, chip, me.c).start()

    def origins(self, fx, fy, k, act):
        me = self.me
        x = 1 - me.x if fx else me.x
        y = 1 - me.y if fy else me.y
        if k == 0:
            act(self.chip(x, y, me.z), 0)
        else:
            pl.when(me.z >= k)(lambda: act(self.chip(x, y, me.z - k), -1))
            pl.when(me.z + k <= 3)(lambda: act(self.chip(x, y, me.z + k), 1))

    def arrival(self, part, fx, fy, k):
        moved = {"x": fx, "y": fy, "z": k}
        return max(i for i in range(3) if moved[ORDER[part][i]])

    def serve(self, part, fx, fy, k):
        me = self.me
        order = ORDER[part]
        stage = self.arrival(part, fx, fy, k)
        axis = order[stage]

        def act(chip, sign):
            if axis == "z":
                way, more = ("up", me.z < 3) if sign < 0 else ("down", me.z > 0)
                self.copy(part, chip, way).wait_recv()
                pl.when(more)(lambda: self.copy(part, chip, way).start())
            else:
                self.copy(part, chip, axis).wait_recv()
            self.onward(part, chip, order[stage + 1:])
            if part in LATE:
                self.beside(part, chip, me.c).start()

        self.origins(fx, fy, k, act)

    def beside(self, part, chip, c):
        i = LATE.index(part)
        ref = self.block(part, chip, c)
        return pltpu.make_async_remote_copy(
            ref, ref, self.lsend.at[i, chip], self.lrecv.at[i, chip], device_id=self.me.to("core"), device_id_type=MESH)

    def arrived(self, part):
        if part not in LATE:
            self.across(part, 1 - self.me.c).wait_recv()
            return

        def body(chip, _):
            self.beside(part, chip, 1 - self.me.c).wait_recv()
            return 0
        lax.fori_loop(0, 16, body, 0)

    def drain(self, part):
        me = self.me
        order = ORDER[part]

        if part in LATE:
            def body(chip, _):
                self.beside(part, chip, me.c).wait_send()
                return 0
            lax.fori_loop(0, 16, body, 0)
        else:
            self.across(part, me.c).wait_send()

        def sent(chip, axes, sign):
            for axis in axes:
                if axis == "z":
                    if sign <= 0:
                        pl.when(me.z < 3)(lambda: self.copy(part, chip, "up").wait_send())
                    if sign >= 0:
                        pl.when(me.z > 0)(lambda: self.copy(part, chip, "down").wait_send())
                else:
                    self.copy(part, chip, axis).wait_send()

        for fx in (0, 1):
            for fy in (0, 1):
                for k in range(4):
                    if fx + fy + k == 0:
                        sent(self.chip(me.x, me.y, me.z), order, 0)
                        continue
                    stage = self.arrival(part, fx, fy, k)
                    axes = order[stage:] if order[stage] == "z" else order[stage + 1:]
                    self.origins(fx, fy, k, lambda chip, sign: sent(
                        chip, axes, sign if order[stage] == "z" else 0))


def relayout(me, wide, refs, name):
    m = pl.multiple_of
    chip = (me.z * 2 + me.x) * 2 + me.y
    wa, wu, wd = refs

    def rows(base, count, stride):
        both = [wide[d, pl.ds(base, count, stride=stride), :] for d in range(2)]
        return jnp.concatenate(both, 0).astype(BF)

    if name == "up":
        for j in range(12):
            wu[pl.ds(m(chip * 48, 16), 48), pl.ds(m((me.c * 12 + j) * 128, 128), 128)] = rows(
                BASE[2] + me.c * 12 + j, 24, 24)
    elif name == "down":
        for j in range(3):
            wd[pl.ds(m(chip * 192, 16), 192), pl.ds(m((me.c * 3 + j) * 128, 128), 128)] = rows(BASE[3] + me.c * 3 + j, 96, 6)
    else:
        for j in range(6):
            wa[pl.ds(m(chip * 48, 16), 48), pl.ds(m(me.c * WIDE + j * 128, 128), 128)] = rows(
                BASE[0] + me.c * 12 + j, 24, 18)
            to = wa.at[pl.ds(m(chip * 48, 16), 48), pl.ds(m(me.c * WIDE + 768 + j * 128, 128), 128)]

            @pl.when(me.c == 0)
            def _():
                to[...] = rows(BASE[0] + 6 + j, 24, 18)

            @pl.when(me.c == 1)
            def _():
                to[...] = rows(BASE[1] + j, 24, 6)


GATHER_PLAN = (

    (16, 0, 48, 17, 1, 64, 18, 4, 32, 25, 8, 19, 2, 5, 21, 26, 27, 24, 3, 68, 6, 7, 49, 65, 12, 23, 22, 40, 20, 33, 80, 29, 72, 52, 30, 10, 9, 13, 11, 31, 50, 66, 36, 56, 28, 15, 14),
    (), (), (), (34,), (), (), (), (), (), (), (37, 51), (67, 84, 57), (), (), (), (), (), (), (), (38, 54),
    (88, 35, 74, 85, 73, 70, 75, 58, 41, 71, 42, 55, 53, 76, 44, 39, 81), (), (), (), (),
    (43, 60, 86, 61, 59, 78, 69), (79, 82, 45), (46, 87, 92, 77, 47, 62, 63, 93, 83), (), (), (), (), (), (), (), (),
    (), (), (), (94, 95, 89, 90, 91),
)

GATHER_X = 0


HEADS = 12
HD = 64
EPS = 1e-05
PAIRS = HEADS // 2

def nt(left, right):
    return lax.dot_general(left, right, (((1,), (1,)), ((), ())), preferred_element_type=F32)


def nn(left, right):
    return jnp.dot(left, right, preferred_element_type=F32)


def tn(left, right):
    return lax.dot_general(left, right, (((0,), (0,)), ((), ())), preferred_element_type=F32)


def tile(i, size):
    return pl.ds(pl.multiple_of(i * size, size), size)


def spread(sides, size, width):
    lane = lax.broadcasted_iota(jnp.int32, (128, width), 0)
    col = lax.broadcasted_iota(jnp.int32, (128, width), 1)
    owner = ((col.astype(F32) + 0.5) * (1.0 / size)).astype(jnp.int32)
    pick = (col - owner * size == lane).astype(F32).astype(BF)
    dev = lax.broadcasted_iota(jnp.int32, (16, width), 0) * 2
    col = lax.broadcasted_iota(jnp.int32, (16, width), 1)
    owner = ((col.astype(F32) + 0.5) * (1.0 / size)).astype(jnp.int32)
    total = jnp.zeros((16, width), F32)
    for c, rows in enumerate(sides):
        total = total + jnp.where(owner == dev + c, nn(rows.astype(BF), pick), 0.0)
    return jnp.sum(total, 0, keepdims=True)


def swap_rows(me, ref, s, send, recv):
    width = 256

    def block(index):
        return ref.at[tile(index, width), :]

    def copy(index, way, n):
        return pltpu.make_async_remote_copy(
            block(index), block(index), send.at[n], recv.at[n], device_id=me.to(way), device_id_type=MESH)

    mine = me.y * 2 + me.c
    over = (1 - me.y) * 2 + me.c
    return (copy(mine, "core", 0), copy(mine, "y", 1), copy(over, "core", 2)), (
        copy(me.y * 2 + 1 - me.c, "core", 0), copy(over, "y", 1), copy((1 - me.y) * 2 + 1 - me.c, "core", 2))


def head_rows(array, axis):
    lane = lax.broadcasted_iota(jnp.int32, array.shape, 1)
    zero = jnp.zeros_like(array)
    return jnp.concatenate([jnp.where(lane < HD, array, zero), jnp.where(lane >= HD, array, zero)], axis)


def forward_kernel(
    fq, fo, fu, fd, s0, s1, s2, s3, s4, s5, s6, s7, s8, x, cot, seg, pad, keep,
    to_out, to_a, to_u, to_xt, to_v, to_kt, to_e,
    hq8, hot, hr, hactt, hgp, hnlt, hn1, hr1, hgs, hsm, wd,
    flats, wide, wa, wu, smf, xall, kk, vv, kt, vt, st, ee, mask, vec, vecu, n2, xt, act, nl,
    out,
    fsend, frecv, send, recv, csend, crecv, lsend, lrecv, osem, xsend, xrecv,
):
    me = Place()
    s = me.y * 2 + me.c
    outs = []

    def put(held, to):
        outs.append(pltpu.make_async_copy(held, to, osem.at[len(outs)]))
        outs[-1].start()

    enter(me)
    refs = (wa, wu, wd)
    g = Gather(me, refs, send, recv, csend, crecv, lsend, lrecv)
    swaps = [
        pltpu.make_async_remote_copy(
            src, flats.at[pl.ds(b, n), :], fsend.at[i], frecv.at[i], device_id=me.to("core"), device_id_type=MESH)
        for i, (src, b, n) in enumerate(zip((fq, fo, fu, fd), BASE, LINES))
    ]
    for c in swaps:
        c.start()
    chip = (me.z * 2 + me.x) * 2 + me.y
    smf[0, 0:48, :] = jnp.zeros((48, 128), F32)
    for i, vector in enumerate((s0, s1, s2, s3, s4, s5, s6, s7, s8)):
        smf[0, i:i + 1, 0:vector.shape[0]] = vector[...].astype(F32).reshape(1, vector.shape[0])
    wa[pl.ds(pl.multiple_of(chip * 48, 16), 48), pl.ds(pl.multiple_of(me.c * WIDE + 1536, 128), 128)] = (
        smf[0, 0:48, :].astype(BF))
    xall[tile(s, 256), :] = x[...]
    xs, xr = swap_rows(me, xall, s, xsend, xrecv)
    xs[0].start()
    slot = iter(GATHER_PLAN)
    count = {}

    def tick():
        for code in next(slot, ()):
            if sum(count.values()) == GATHER_X:
                xs[1].start()
            p, fx, fy, k = NAMES[code // 16], code // 8 % 2, code // 4 % 2, code % 4
            if fx + fy + k:
                g.serve(p, fx, fy, k)
            else:
                unpack(p)
                g.own(p)
            count[p] = count.get(p, 0) + 1
            if count[p] == 16 and p not in LATE:
                g.across(p, me.c).start()

    unpacked = []

    def unpack(p):
        name = p.rstrip("01")
        if name in unpacked:
            return
        unpacked.append(name)
        for i in {"attn": (0, 1), "up": (2,), "down": (3,)}[name]:
            src, b, n = (fq, fo, fu, fd)[i], BASE[i], LINES[i]
            wide[me.c, pl.ds(b, n), :] = src[...].astype(F32)
            swaps[i].wait_recv()
            wide[1 - me.c, pl.ds(b, n), :] = flats[pl.ds(b, n), :].astype(F32)
        relayout(me, wide, refs, name)

    codes = jnp.where(pad[...] > 0, seg[...], -1).astype(F32)
    mine = seg[:, tile(s, 256)].astype(F32)
    for j in range(8):
        column = jnp.broadcast_to(codes[:, j * 128:(j + 1) * 128], (128, 128)).T
        for i in range(2):
            row = jnp.broadcast_to(mine[:, i * 128:(i + 1) * 128], (128, 128))
            mask[pl.ds(j * 128, 128), pl.ds(i * 128, 128)] = jnp.where(column == row, 0.0, -1e9)

    tick()
    xr[1].wait_recv()
    xs[2].start()
    g.arrived("attn0")
    g.arrived("attn1")
    xr[0].wait_recv()
    xr[2].wait_recv()
    put(wa, to_a)
    for j in range(4):
        xt[:, pl.ds(j * 256, 256)] = xall[pl.ds(j * 256, 256), :].T

    for c in range(2):
        smf[c] = wa[:, pl.ds(c * WIDE + 1536, 128)].astype(F32)
    vec[...] = jnp.zeros_like(vec)
    for i in range(8):
        vec[pl.ds(i, 1), :] = spread([smf[c, pl.ds(i, 16, stride=48), :] for c in range(2)], 24, 768)
    vecu[...] = spread([smf[c, pl.ds(8, 16, stride=48), :] for c in range(2)], 96, 3072)

    tick()
    for j in range(3):
        w = pl.ds(j * 256, 256)
        hq8[:, w] = ((nn(x[...], wa[:, w]) + vec[0:1, w]).astype(BF).astype(F32) * 0.125).astype(BF)
    for j in range(3):
        w = pl.ds(j * 256, 256)
        for r in range(2):
            rows = pl.ds(r * 512, 512)
            tick()
            k = nn(xall[rows, :], wa[:, pl.ds(768 + j * 256, 256)]).astype(BF)
            kk[rows, w] = k
            kt[w, rows] = k.T
            v = (nn(xall[rows, :], wa[:, pl.ds(WIDE + j * 256, 256)]) + vec[1:2, w]).astype(BF)
            vv[rows, w] = v
            vt[w, rows] = v.T
    put(xt, to_xt)
    put(vv, to_v)
    put(kt, to_kt)

    for p in range(PAIRS):
        w = pl.ds(p * 128, 128)
        qm = head_rows(hq8[:, w], 0)
        tick()
        top = jnp.full((8, 512), -3e38, F32)
        for c in range(4):
            rows = pl.ds(c * 256, 256)
            one = mask[rows, :]
            v = nt(kk[rows, w], qm) + jnp.concatenate([one, one], 1)
            st[rows, :] = v
            top = jnp.maximum(top, jnp.max(v.reshape(32, 8, 512), 0))
        top = jnp.max(top, 0, keepdims=True)
        tick()
        total = jnp.zeros((8, 512), F32)
        for c in range(8):
            rows = pl.ds(c * 128, 128)
            v = jnp.exp(st[rows, :] - top)
            ee[p, rows, :] = v.astype(BF)
            total = total + jnp.sum(v.reshape(16, 8, 512), 0)
        inverse = 1.0 / jnp.sum(total, 0, keepdims=True)
        hr[pl.ds(p, 1), :] = inverse
        tick()
        for h in range(2):
            o = nn(vt[pl.ds(p * 128 + h * 64, 64), :], ee[p, :, pl.ds(h * 256, 256)])
            hot[pl.ds(p * 128 + h * 64, 64), :] = (o * inverse[:, h * 256:(h + 1) * 256]).astype(BF)
        put(ee.at[p], to_e.at[p])

    tick()
    n2[...] = tn(hot[...], wa[:, pl.ds(WIDE + 768, 768)])
    tick()
    for r in range(8):
        rows = pl.ds(r * 32, 32)
        value = x[rows, :].astype(F32) + n2[rows, :] + vec[2:3, :]
        centred = value - jnp.mean(value, -1, keepdims=True)
        r1 = lax.rsqrt(jnp.mean(centred * centred, -1, keepdims=True) + EPS)
        n1 = centred * r1
        hn1[rows, :] = n1
        hr1[rows, :] = jnp.broadcast_to(r1, (32, 128))
        normed = n1 * vec[3:4, :] + vec[4:5, :]
        n2[rows, :] = normed
        nl[rows, :] = normed.astype(BF)
    hnlt[...] = nl[...].T
    for p in ("attn0", "attn1"):
        g.drain(p)
    tick()
    g.arrived("up0")
    g.arrived("up1")
    put(wu, to_u)

    for j in range(12):
        w = pl.ds(j * 256, 256)
        if j:
            tick()
        before = nn(nl[...], wu[:, w]) + vecu[:, w]
        phi = 0.5 * (1.0 + lax.erf(before * 0.7071067811865476))
        a = (before * phi).astype(BF)
        act[:, w] = a
        hactt[w, :] = a.T
        hgp[:, w] = (phi + before * 0.3989422804014327 * jnp.exp(-0.5 * before * before)).astype(BF)

    tick()
    for p in ("up0", "up1", "down0", "down1"):
        g.drain(p)
    g.arrived("down0")
    g.arrived("down1")

    for j in range(3):
        w = pl.ds(j * 256, 256)
        n2[:, w] += nn(act[...], wd[:, w]) + vec[5:6, w]
    hsm[...] = jnp.zeros_like(hsm)
    hsm[2:3, :] = vec[3:4, :]
    kept = keep[...] > 0
    gain = jnp.zeros((8, 768), F32)
    shift = jnp.zeros((8, 768), F32)
    for r in range(8):
        rows = pl.ds(r * 32, 32)
        value = n2[rows, :]
        centred = value - jnp.mean(value, -1, keepdims=True)
        r2 = lax.rsqrt(jnp.mean(centred * centred, -1, keepdims=True) + EPS)
        n = centred * r2
        out[rows, :] = jnp.where(kept, n * vec[6:7, :] + vec[7:8, :], x[rows, :].astype(F32)).astype(BF)
        grad = jnp.where(kept, cot[rows, :].astype(F32), 0.0)
        gain = gain + jnp.sum((grad * n).reshape(4, 8, 768), 0)
        shift = shift + jnp.sum(grad.reshape(4, 8, 768), 0)
        c = grad * vec[6:7, :]
        hgs[rows, :] = r2 * (c - jnp.mean(c, -1, keepdims=True) - n * jnp.mean(c * n, -1, keepdims=True))
    hsm[0:1, :] = jnp.sum(gain, 0, keepdims=True)
    hsm[1:2, :] = jnp.sum(shift, 0, keepdims=True)
    put(out, to_out)

    for c in swaps:
        c.wait_send()
    for c in xs:
        c.wait_send()
    for o in outs:
        o.wait()


def vmem(*shapes):
    return [pltpu.VMEM(s, d) for s, d in shapes]


HELD = vmem(
    ((256, 768), BF), ((768, 256), BF), ((8, 512), F32), ((3072, 256), BF), ((256, 3072), BF), ((768, 256), BF),
    ((256, 768), F32), ((256, 128), F32), ((256, 768), F32), ((8, 768), F32), ((3072, 768), BF),
)
SPOOLED = (
    ((768, 2 * WIDE), BF), ((768, 3072), BF), ((768, 1024), BF), ((1024, 768), BF), ((768, 1024), BF),
    ((PAIRS, 1024, 512), BF),
)
FORWARD_SCOPE = vmem(
    ((1728, 128), BF), ((2, 1728, 128), F32), ((768, 2 * WIDE), BF), ((768, 3072), BF), ((2, 768, 128), F32),
    ((1024, 768), BF), ((1024, 768), BF), ((1024, 768), BF), ((768, 1024), BF), ((768, 1024), BF), ((1024, 512), F32),
    ((PAIRS, 1024, 512), BF), ((1024, 256), F32), ((8, 768), F32), ((1, 3072), F32), ((256, 768), F32),
    ((768, 1024), BF), ((256, 3072), BF), ((256, 768), BF), ((256, 768), BF),
)


def forward_semaphores():
    n = len(PARTS)
    dma = pltpu.SemaphoreType.DMA
    return [dma(s) for s in (
        (4,), (4,), (n, 16, 4), (n, 16), (n,), (n,), (2, 16), (2, 16), (24,), (3,), (3,))]


RPARTS = (
    ("down", 3, "yzx", 192, 0, 0, 384),
    ("up", 2, "xzy", 48, 0, 0, 1536),
    ("out", 1, "zyx", 48, 0, 0, 384),
    ("qkv0", 0, "zxy", 48, 0, 0, 384),
    ("qkv1", 0, "zyx", 48, 0, 384, 384),
    ("qkv2", 0, "zyx", 48, 0, 768, 384),
)
HALF = (1152, 384, 1536, 384)
CHIPROWS = (48, 48, 48, 192)
ROWS = (768, 768, 768, 3072)
SIZES = {"x": 2, "y": 2, "z": 4}
LINKS = ("up", "down", "x", "y")


def slots(order, axis):
    n = 4 if axis == "z" else 1
    for a in order[: order.index(axis)]:
        n *= SIZES[a]
    return n


def landing_shapes():
    shapes = []
    for name, mat, order, rows, ro, co, cols in RPARTS:
        for way in LINKS:
            axis = "z" if way in ("up", "down") else way
            shapes.append(pltpu.VMEM((slots(order, axis), rows, cols), BF))
    return shapes


class Scatter:
    def __init__(self, me, grads, half, lands, finals, send, recv):
        self.me, self.grads, self.half, self.lands, self.finals = me, grads, half, lands, finals
        self.send, self.recv = send, recv

    def chip(self, x, y, z):
        return (z * 2 + x) * 2 + y

    def part(self, refs, i, dest):
        name, mat, order, rows, ro, co, cols = RPARTS[i]
        first = pl.multiple_of(self.chip(*dest) * CHIPROWS[mat] + ro, 16)
        return refs[mat].at[pl.ds(first, rows), pl.ds(co, cols)]

    def block(self, i, dest):
        return self.part(self.grads, i, dest)

    def slot(self, i, way, dest):
        order = RPARTS[i][2]
        axis = "z" if way in ("up", "down") else way
        coords = dict(zip("xyz", dest))
        index = coords["z"] if axis == "z" else 0
        for a in order[: order.index(axis)]:
            index = index * SIZES[a] + coords[a]
        return index

    def land(self, i, way, dest):
        return self.lands[i * 4 + LINKS.index(way)].at[self.slot(i, way, dest)]

    def copy(self, i, way, dest):
        chip = self.chip(*dest)
        return pltpu.make_async_remote_copy(
            self.block(i, dest), self.land(i, way, dest), self.send.at[i, chip],
            self.recv.at[i, LINKS.index(way), chip], device_id=self.me.to(way), device_id_type=MESH)

    def stage(self, i, fx, fy, k):
        moved = {"x": fx, "y": fy, "z": k}
        return max(s for s in range(3) if moved[RPARTS[i][2][s]])

    def take(self, i, way, dest):
        self.copy(i, way, dest).wait_recv()
        ref = self.block(i, dest)
        ref[...] = ref[...] + self.land(i, way, dest)[...]

    def total(self, i, dest, ways):
        value = self.block(i, dest)[...] + self.part(self.half, i, dest)[...]
        for way in ways:
            self.copy(i, way, dest).wait_recv()
            value = value + self.land(i, way, dest)[...]
        return value

    def serve(self, i, fx, fy, k):
        me = self.me
        order = RPARTS[i][2]
        stage = self.stage(i, fx, fy, k)
        axis = order[stage]

        def act(dest, sign):
            way = axis
            if axis == "z":
                way, more = ("down", me.z < 3) if sign < 0 else ("up", me.z > 0)
                pl.when(more)(lambda: self.take(i, way, dest))
            if "z" in order[stage + 1:]:
                pl.when(me.z < 3)(lambda: self.take(i, "down", dest))
                pl.when(me.z > 0)(lambda: self.take(i, "up", dest))
            value = self.total(i, dest, [a for a in order[stage + 1:] if a != "z"])
            self.block(i, dest)[...] = value
            self.copy(i, way, dest).start()

        self.dests(fx, fy, k, act)

    def dests(self, fx, fy, k, act):
        me = self.me
        x = 1 - me.x if fx else me.x
        y = 1 - me.y if fy else me.y
        if k == 0:
            act((x, y, me.z), 0)
        else:
            pl.when(me.z >= k)(lambda: act((x, y, me.z - k), -1))
            pl.when(me.z + k <= 3)(lambda: act((x, y, me.z + k), 1))

    def own(self, i):
        dest = (self.me.x, self.me.y, self.me.z)
        name, mat, order, rows, ro, co, cols = RPARTS[i]
        self.finals[mat].at[pl.ds(ro, rows), pl.ds(co, cols)][...] = (
            self.block(i, dest)[...].astype(F32) + self.part(self.half, i, dest)[...].astype(F32))

    def finish(self, i):
        name, mat, order, rows, ro, co, cols = RPARTS[i]
        me = self.me
        dest = (me.x, me.y, me.z)
        fin = self.finals[mat].at[pl.ds(ro, rows), pl.ds(co, cols)]

        def add(way):
            self.copy(i, way, dest).wait_recv()
            fin[...] += self.land(i, way, dest)[...].astype(F32)
        for axis in order:
            if axis == "z":
                pl.when(me.z < 3)(lambda: add("down"))
                pl.when(me.z > 0)(lambda: add("up"))
            else:
                add(axis)

    def drain(self, i):
        for fx in (0, 1):
            for fy in (0, 1):
                for k in range(4):
                    if fx + fy + k:
                        axis = RPARTS[i][2][self.stage(i, fx, fy, k)]
                        self.dests(fx, fy, k, lambda dest, sign: self.copy(
                            i, axis if axis != "z" else ("down" if sign < 0 else "up"), dest).wait_send())


SCATTER_PLAN = (
    (15, 14), (), (), (), (), (), (), (), (), (), (), (7, 11, 13), (), (), (), (), (), (31, 29), (6, 10, 23),
    (22, 12, 3), (), (), (), (9, 21, 5, 30, 27), (), (), (), (), (), (), (), (), (41, 42, 19, 2, 40), (), (), (), (),
    (), (), (), (), (), (), (), (47, 61, 18, 60, 62, 63, 20, 8, 45, 55, 43, 28), (), (), (), (), (), (),
    (46, 26, 57, 44, 56, 39, 1), (), (), (), (), (), (), (76, 77, 53, 75, 59, 4, 17, 79, 25, 58, 73, 38, 78, 74), (),
    (), (), (), (), (), (), (), (), (95, 71, 94, 54, 93, 35, 51, 37, 91), (),
    (87, 67, 90, 70, 86, 34, 92, 89, 69, 50), (83, 85, 72, 24, 52, 66, 33), (), (82, 36, 68, 84, 49, 65, 88), (81,),
    (), (), (), (16, 0, 48, 32, 64, 80),
)

FLATROWS = ((24, 18, 432), (24, 6, 144), (24, 24, 576), (96, 6, 576))


def column(mat, c, j):
    if mat:
        return c * (FLATROWS[mat][1] // 2) + j
    group, t = j // 3, j % 3
    if c == 0:
        return 2 * group + t if t < 2 else 6 + 2 * group
    return 7 + 2 * group if t == 0 else 11 + 2 * group + t


def flatten(me, mat, finals, sides, out):
    rows, tiles, lines = FLATROWS[mat]
    half = tiles // 2
    for c in range(2):
        @pl.when(me.c == c)
        def _():
            for j in range(half):
                mine = finals[mat][pl.ds(pl.multiple_of(me.c * rows, 8), rows), pl.ds(j * 128, 128)]
                out[pl.ds(column(mat, c, j), rows, stride=tiles), :] = mine
                out[pl.ds(column(mat, 1 - c, j), rows, stride=tiles), :] = sides[mat][:, pl.ds(j * 128, 128)]


def colsum(array):
    return jnp.sum(array.astype(F32), 0, keepdims=True)


def backward_kernel(ha, hu, hxt, hv, hkt, he, held, cot, keep, results, scope, semaphores, here):
    q8, ot, rr, actt, gp, nlt, n1, r1, gs, sm0, wbig = held
    ingrad, oq, oo, ou, od, chosen = results
    rest = list(scope)
    lands, rest = rest[:4 * len(RPARTS)], rest[4 * len(RPARTS):]
    grads, rest = rest[:4], rest[4:]
    stage, rest = rest[:3], rest[3:]
    stage = [stage[1].at[:, pl.ds(0, HALF[0])]] + stage
    half, rest = rest[:4], rest[4:]
    finals, rest = rest[:4], rest[4:]
    sides, rest = rest[:4], rest[4:]
    wo, xt, vv, kt, ee, ds, gbr, gbef, first, gts, gsa, dq, dkv, dx, dxc, dxy, acc, sland, osm = rest
    wsem, isem, esem, csend, crecv, send, recv, fsend, frecv, dsend, drecv, asend, arecv = semaphores
    me = Place()
    s = me.y * 2 + me.c
    wus = [pltpu.make_async_copy(hu.at[:, pl.ds(q * 768, 768)], wbig.at[pl.ds(q * 768, 768), :], wsem.at[4 + q]) for q in range(4)]
    wqs = [pltpu.make_async_copy(ha.at[:, pl.ds((0, 768, WIDE)[q], 768)], wbig.at[pl.ds(q * 768, 768), :], wsem.at[8 + q]) for q in range(3)]
    others = [pltpu.make_async_copy(a, b, isem.at[i]) for i, (a, b) in enumerate(((ha.at[:, pl.ds(WIDE + 768, 768)], wo), (hv, vv), (hkt, kt), (hxt, xt)))]
    ees = [pltpu.make_async_copy(he.at[p], ee.at[p % 2], esem.at[p]) for p in range(PAIRS)]
    greet(me, here)

    sc = Scatter(me, grads, half, lands, finals, send, recv)

    def swap(mat, piece=0):
        cut = {
            0: (slice(None), pl.ds(piece * 384, 384)), 1: (slice(None), slice(None)),
            2: (slice(None), pl.ds(piece * 512, 512)), 3: (pl.ds(piece * 768, 768), slice(None)),
        }[mat]
        n = (0, 3, 4, 7)[mat] + piece
        return pltpu.make_async_remote_copy(
            stage[mat].at[cut], half[mat].at[cut], csend.at[n], crecv.at[n], device_id=me.to("core"), device_id_type=MESH)

    def last(mat):
        rows = FLATROWS[mat][0]
        src = finals[mat].at[pl.ds(pl.multiple_of((1 - me.c) * rows, 8), rows), :]
        return pltpu.make_async_remote_copy(
            src, sides[mat], fsend.at[mat], frecv.at[mat], device_id=me.to("core"), device_id_type=MESH)

    def swapped(mat):
        for piece in range((3, 1, 3, 4)[mat]):
            swap(mat, piece).wait_recv()

    def unstaged(mat):
        for piece in range((3, 1, 3, 4)[mat]):
            swap(mat, piece).wait_send()

    slot = iter(SCATTER_PLAN)
    count = {}

    def tick():
        for code in next(slot, ()):
            i, fx, fy, k = code // 16, code // 8 % 2, code // 4 % 2, code % 4
            if fx + fy + k:
                sc.serve(i, fx, fy, k)
            else:
                sc.own(i)
                sc.finish(i)
                mat = RPARTS[i][1]
                count[mat] = count.get(mat, 0) + 1
                if count[mat] == (3, 1, 1, 1)[mat]:
                    last(mat).start()

    def arrange(value_ref, to):
        to[:, 0:384] = value_ref[:, pl.ds(pl.multiple_of(me.c * 384, 128), 384)]
        to[:, 384:768] = value_ref[:, pl.ds(pl.multiple_of((1 - me.c) * 384, 128), 384)]

    osm[...] = jnp.zeros_like(osm)
    osm[6:8, :] = sm0[0:2, :]
    gsa[...] = gs[...].astype(BF)
    osm[5:6, :] = colsum(gsa[...])
    arrange(gsa, gbr)

    for j in range(12):
        w = pl.ds(j * 256, 256)
        v = nn(actt[w, :], gbr[...]).astype(BF)
        grads[3][w, :] = v[:, 0:384]
        stage[3][w, :] = v[:, 384:768]
        if j == 2:
            pl.semaphore_wait(here, 5)
        if j % 3 == 2:
            swap(3, j // 3).start()

    for q in range(4):
        for j in range(3):
            w = pl.ds(q * 768 + j * 256, 256)
            gb = nt(gsa[...], wbig[w, :]).astype(BF) * gp[:, w]
            gbef[:, w] = gb
            osm[8 + q:9 + q, pl.ds(j * 256, 256)] = colsum(gb)
        wus[q].start()
        if q == 0:
            swapped(3)
        tick()

    for c in others:
        c.start()
    ees[0].start()
    ees[1].start()
    for j in range(6):
        w = pl.ds(j * 256, 256)
        tick()
        stage[2][:, w] = nn(nlt[...], gbef[:, pl.ds(pl.multiple_of((1 - me.c) * 1536 + j * 256, 256), 256)]).astype(BF)
        if j % 2:
            swap(2, j // 2).start()
    for j in range(6):
        w = pl.ds(j * 256, 256)
        tick()
        grads[2][:, w] = nn(nlt[...], gbef[:, pl.ds(pl.multiple_of(me.c * 1536 + j * 256, 256), 256)]).astype(BF)
    for c in wus:
        c.wait()
    tick()
    swapped(2)

    for j in range(3):
        w = pl.ds(j * 256, 256)
        tick()
        total = gs[:, w]
        for q in range(4):
            total += nt(gbef[:, pl.ds(q * 768, 768)], wbig[pl.ds(q * 768 + j * 256, 256), :])
        first[:, w] = total
    for c in wqs:
        c.start()

    gain = jnp.zeros((8, 768), F32)
    shift = jnp.zeros((8, 768), F32)
    for r in range(8):
        rows = pl.ds(r * 32, 32)
        if r % 4 == 0:
            tick()
        gn = first[rows, :]
        n = n1[rows, :]
        gain = gain + jnp.sum((gn * n).reshape(4, 8, 768), 0)
        shift = shift + jnp.sum(gn.reshape(4, 8, 768), 0)
        c1 = gn * sm0[2:3, :]
        gf = r1[rows, 0:1] * (c1 - jnp.mean(c1, -1, keepdims=True) - n * jnp.mean(c1 * n, -1, keepdims=True))
        first[rows, :] = gf
        gsa[rows, :] = gf.astype(BF)
    osm[3:4, :] = jnp.sum(gain, 0, keepdims=True)
    osm[4:5, :] = jnp.sum(shift, 0, keepdims=True)
    osm[2:3, :] = colsum(gsa[...])
    arrange(gsa, gbr)
    tick()

    for j in range(3):
        w = pl.ds(j * 256, 256)
        v = nn(ot[w, :], gbr[...]).astype(BF)
        grads[1][w, :] = v[:, 0:384]
        stage[1][w, :] = v[:, 384:768]
    swap(1).start()
    for c in others:
        c.wait()
    for p in range(PAIRS):
        w = pl.ds(p * 128, 128)
        if p % 2 == 0:
            tick()
        g = nt(wo[w, :], gsa[...]).astype(BF).astype(F32)
        scale = jnp.concatenate(
            [jnp.broadcast_to(rr[p:p + 1, h * 256:(h + 1) * 256], (64, 256)) for h in range(2)], 0)
        gts[w, :] = (g * scale).astype(BF)
    swapped(1)

    mine = xt.at[:, tile(s, 256)]

    def qkv_grads(group):
        q = pl.ds(group * 256, 256)
        v = pl.ds(768 + group * 256, 256)
        mid = pl.ds(group * 384, 384)

        def put(r, a, b):
            rows = pl.ds(r * 256, 256)
            vq = nn(mine[rows, :], dq[:, q]).astype(BF)
            vk = nn(xt[rows, :], dkv[:, q]).astype(BF)
            vv_ = nn(xt[rows, :], dkv[:, v]).astype(BF)
            a[rows, pl.ds(group * 384, 256)] = vq
            a[rows, pl.ds(group * 384 + 256, 128)] = vk[:, 0:128]
            b[rows, pl.ds(group * 384, 128)] = vk[:, 128:256]
            b[rows, pl.ds(group * 384 + 128, 256)] = vv_

        for r in range(3):
            tick()
            pl.when(me.c == 0)(lambda: put(r, grads[0], stage[0]))
            pl.when(me.c == 1)(lambda: put(r, stage[0], grads[0]))
        swap(0, group).start()

    for p in range(PAIRS):
        w = pl.ds(p * 128, 128)
        g = gts[w, :]
        both = ot[w, :].astype(F32) * g.astype(F32)
        delta = jnp.concatenate([jnp.sum(both[0:64], 0, keepdims=True), jnp.sum(both[64:128], 0, keepdims=True)], 1)
        gm = head_rows(g.T, 0)
        qm = head_rows(q8[:, w], 0)
        ees[p].wait()
        e = ee.at[p % 2]
        for c in range(4):
            rows = pl.ds(c * 256, 256)
            if c % 2 == 0:
                tick()
            dp = nt(vv[rows, w], gm)
            ds[rows, :] = e[rows, :] * (dp - delta).astype(BF)
        tick()
        dkv[:, w] = nn(ds[...], qm).astype(BF)
        tick()
        dkv[:, pl.ds(768 + p * 128, 128)] = nn(e[...], gm).astype(BF)
        tick()
        dqt = jnp.concatenate([
            nn(kt[pl.ds(p * 128 + h * 64, 64), :], ds[:, pl.ds(h * 256, 256)]) for h in range(2)], 0)
        dq[:, w] = (dqt * 0.125).astype(BF).T
        if p + 2 < PAIRS:
            ees[p + 2].start()
        if p == 1:
            unstaged(2)
        if p % 2:
            qkv_grads(p // 2)
        if p in (2, 4):
            swap(0, p // 2 - 1).wait_recv()
            tick()

    osm[0:1, :] = colsum(dq[...])
    osm[1:2, :] = colsum(dkv[:, pl.ds(768, 768)])

    acc[0] = osm[...]
    pairz = {"outer": (me.z + 1 - 2 * (me.z % 2)) * 2 + me.x}
    smalls = [
        pltpu.make_async_remote_copy(acc.at[i], sland.at[i], asend.at[i], arecv.at[i], device_id=to, device_id_type=MESH)
        for i, to in enumerate((me.to("core"), me.to("x"), me.to("y"), pairz, me.to("far")))
    ]
    smalls[0].start()

    def small_step(i):
        smalls[i].wait_recv()
        acc[i + 1] = acc[i] + sland[i]
        if i < 4:
            smalls[i + 1].start()

    for c in wqs:
        c.wait()

    for j in range(3):
        w = pl.ds(j * 256, 256)
        for r in range(2):
            rows = pl.ds(r * 512, 512)
            if j == 0 and r == 1:
                swap(0, 2).wait_recv()
            tick()
            dx[rows, w] = (
                nt(dkv[rows, 0:768], wbig[pl.ds(768 + j * 256, 256), :])
                + nt(dkv[rows, 768:1536], wbig[pl.ds(1536 + j * 256, 256), :])).astype(BF)
            if r:
                small_step(j)
        first[:, w] += nt(dq[...], wbig[w, :])

    def dx_copy(n):
        if n < 2:
            yy = me.y if n == 0 else 1 - me.y
            return pltpu.make_async_remote_copy(
                dx.at[tile(yy * 2 + 1 - me.c, 256), :], dxc.at[n], dsend.at[n], drecv.at[n],
                device_id=me.to("core"), device_id_type=MESH)
        return pltpu.make_async_remote_copy(
            dx.at[tile((1 - me.y) * 2 + me.c, 256), :], dxy, dsend.at[2], drecv.at[2],
            device_id=me.to("y"), device_id_type=MESH)
    dx_copy(1).start()
    dx_copy(0).start()
    dx_copy(1).wait_recv()
    over = tile((1 - me.y) * 2 + me.c, 256)
    dx[over, :] = (dx[over, :].astype(F32) + dxc[1].astype(F32)).astype(BF)
    dx_copy(2).start()

    for i in range(5):
        tick()
        if i < 2:
            small_step(3 + i)
    tick()
    owner = ((me.z * 2 + me.x) * 4 + s).astype(F32)
    at = lax.broadcasted_iota(jnp.int32, (768, 128), 0).astype(F32)
    lane = lax.broadcasted_iota(jnp.int32, (768, 128), 1).astype(F32)

    def choose(rows, start, size):
        pick = jnp.where((at == start + lane) & (lane < size), 1.0, 0.0)
        return jnp.dot(rows, pick, precision=lax.Precision.HIGHEST, preferred_element_type=F32)
    up = jnp.zeros((8, 128), F32)
    for q in range(4):
        up = up + choose(acc[5, 8 + q:9 + q, :], owner * 96 - q * 768, 96)
    chosen[0:8, :] = choose(acc[5, 0:8, :], owner * 24, 24)
    chosen[8:16, :] = up
    dx_copy(0).wait_recv()
    dx_copy(2).wait_recv()
    total = first[...] + dx[tile(s, 256), :].astype(F32) + dxc[0].astype(F32) + dxy[...].astype(F32)
    ingrad[...] = jnp.where(keep[...] > 0, total, cot[...].astype(F32)).astype(BF)
    for i in range(len(RPARTS)):
        sc.drain(i)
    for mat in (3, 1, 0):
        unstaged(mat)
    for n in range(3):
        dx_copy(n).wait_send()
    for c in smalls:
        c.wait_send()
    for mat in (3, 2, 1, 0):
        last(mat).wait()
        flatten(me, mat, finals, sides, (oq, oo, ou, od)[mat])


def backward_scope():
    halves = [((ROWS[m], HALF[m]), BF) for m in range(4)]
    return landing_shapes() + vmem(
        *halves, *halves[1:], *halves,
        *(((CHIPROWS[m], HALF[m]), F32) for m in range(4)),
        *(((FLATROWS[m][0], HALF[m]), F32) for m in range(4)),
        ((768, 768), BF), ((768, 1024), BF), ((1024, 768), BF), ((768, 1024), BF), ((2, 1024, 512), BF),
        ((1024, 512), BF), ((256, 768), BF), ((256, 3072), BF), ((256, 768), F32), ((768, 256), BF),
        ((256, 768), BF), ((256, 768), BF), ((1024, 1536), BF), ((1024, 768), BF), ((2, 256, 768), BF),
        ((256, 768), BF), ((6, 16, 768), F32), ((5, 16, 768), F32), ((16, 768), F32),
    )


def backward_semaphores():
    n = len(RPARTS)
    dma = pltpu.SemaphoreType.DMA
    return [dma(s) for s in (
        (11,), (4,), (PAIRS,), (11,), (11,), (n, 16), (n, 4, 16), (4,), (4,), (3,), (3,), (5,), (5,))]


RESULTS = [((256, 768), BF)] + [((FLATROWS[m][2], 128), F32) for m in range(4)] + [((16, 128), F32)]


def layer_kernel(*refs):
    def split(n):
        nonlocal refs
        head, refs = refs[:n], refs[n:]
        return head
    ins, out, spools, results = split(18), split(1), split(6), split(6)
    held, first_sems, second_sems, here = split(11), split(11), split(13), refs[0]
    cot, keep = ins[14], ins[17]
    pl.run_scoped(lambda *scope: forward_kernel(*ins, *out, *spools, *held, *scope, *first_sems), *FORWARD_SCOPE)
    pl.run_scoped(
        lambda *scope: backward_kernel(*spools, held, cot, keep, results, scope, second_sems, here), *backward_scope())


def layer_call(*args):
    a = pl.BlockSpec(memory_space=pl.ANY)
    v = pl.BlockSpec(memory_space=pltpu.VMEM)
    out = ((256, 768), BF)
    return pl.pallas_call(
        layer_kernel,
        out_shape=[jax.ShapeDtypeStruct(s, d) for s, d in (out,) + SPOOLED + tuple(RESULTS)],
        in_specs=[v] * 18,
        out_specs=[a] * 7 + [v] * 6,
        scratch_shapes=HELD + forward_semaphores() + backward_semaphores() + [pltpu.SemaphoreType.REGULAR],
        compiler_params=pltpu.CompilerParams(collective_id=1, has_side_effects=True, vmem_limit_bytes=(63 << 20) + (800 << 10)),
        name="layer",
    )(*args)


SMALL_SIZES = (24,) * 8 + (96,)


def finish_kernel(*refs):
    ins, small, outs, smalls = refs[:6], refs[6], refs[7:13], refs[13:22]
    for a, b in zip(ins, outs):
        b[...] = a[...]
    for i, (to, size) in enumerate(zip(smalls, SMALL_SIZES)):
        to[...] = small[i, 0:size]


def finish_call(*args):
    v = pl.BlockSpec(memory_space=pltpu.VMEM)
    return pl.pallas_call(
        finish_kernel,
        out_shape=[jax.ShapeDtypeStruct(x.shape, x.dtype) for x in args[:6]]
        + [jax.ShapeDtypeStruct((size,), F32) for size in SMALL_SIZES],
        in_specs=[v] * 7,
        out_specs=[v] * 15,
        name="finish",
    )(*args)


AXES = ("outer", "inner", "seq")
SMALLS = (1, 2, 4, 5, 6, 10, 11, 12, 8)


def to_part(flat):
    inner = lax.axis_size("inner")
    if inner == 1:
        return flat
    every = lax.all_gather(flat, ("inner", "seq"), axis=0, tiled=True)
    size = flat.shape[0] * inner
    return lax.dynamic_slice_in_dim(every, lax.axis_index("seq") * size, size, 0)


def whole_scatter(part):
    inner = lax.axis_size("inner")
    if inner == 1:
        return part
    every = lax.psum(lax.all_gather(part, "seq", axis=0, tiled=True), "inner")
    size = part.shape[0] // inner
    index = lax.axis_index("inner") * lax.axis_size("seq") + lax.axis_index("seq")
    return lax.dynamic_slice_in_dim(every, index * size, size, 0)


def shards(inputs, *rest):
    params, (cotangent, segment_ids, pad_mask, keep_flag) = rest[:13], rest[13:]
    parts = [to_part(p) for p in params]
    x, cot = inputs[0], cotangent[0]
    keep = keep_flag.reshape(1, 1)
    out, *rest = layer_call(
        *(parts[i].reshape(-1, 128) for i in (0, 3, 7, 9)), *(parts[i] for i in SMALLS), x, cot,
        segment_ids, pad_mask, keep
    )
    grad, *big, small = rest[6:]
    out, grad, *rest = finish_call(out, grad, *big, small)
    big = [whole_scatter(part.reshape(-1)) for part in rest[:4]]
    q, v, ob, g1, b1, db, g2, b2, ub = (whole_scatter(part) for part in rest[4:])
    return (out[None], grad[None], big[0], q, v, big[1], ob, g1, b1, big[2], ub, big[3], db, g2, b2)


def solution(mesh):
    fsdp, seq = mesh.shape["fsdp"], mesh.shape["seq"]
    mesh = Mesh(mesh.devices.reshape(8, fsdp // 8, seq), AXES)
    tokens = P(("outer", "inner"), "seq", None)
    flat = P(AXES)
    rows = P(("outer", "inner"), None)
    return jax.shard_map(
        shards,
        mesh=mesh,
        in_specs=(tokens,) + (flat,) * 13 + (tokens, rows, rows, P(("outer", "inner"))),
        out_specs=(tokens, tokens) + (flat,) * 13,
        check_vma=False,
    )
```

```python
import functools
import jax
import jax.numpy as jnp
from jax import lax
from jax.experimental import pallas as pl
from jax.experimental.pallas import tpu as pltpu
from jax.sharding import Mesh, PartitionSpec as P

MESH = pl.DeviceIdType.MESH
D = 768
FF = 3072
BF = jnp.bfloat16
F32 = jnp.float32
LINES = (432, 144, 576, 576)
BASE = (0, 432, 576, 1152)
WIDE = 1664


class Place:
    def __init__(self):
        o = lax.axis_index("outer")
        s = lax.axis_index("seq")
        self.z, self.x, self.y, self.c = o // 2, o % 2, s // 2, s % 2

    def to(self, way):
        z, x, y, c = self.z, self.x, self.y, self.c
        return {
            "up": {"outer": (z + 1) * 2 + x},
            "down": {"outer": (z - 1) * 2 + x},
            "x": {"outer": z * 2 + 1 - x},
            "y": {"seq": (1 - y) * 2 + c},
            "core": {"seq": y * 2 + 1 - c},
            "far": {"outer": (3 - z) * 2 + x},
        }[way]


def greet(me, semaphore):
    def say(to):
        pl.semaphore_signal(semaphore, 1, device_id=to, device_id_type=MESH)

    for way in ("x", "y", "core"):
        say(me.to(way))
    pl.when(me.z < 3)(lambda: say(me.to("up")))
    pl.when(me.z > 0)(lambda: say(me.to("down")))
    pl.when((me.z == 0) | (me.z == 3))(lambda: say(me.to("far")))


def enter(me):
    bar = pltpu.get_barrier_semaphore()
    greet(me, bar)
    pl.semaphore_wait(bar, 5)


WAYS = ("up", "down", "x", "y")

PARTS = (
    ("attn0", "yzx"),
    ("attn1", "zxy"),
    ("up0", "yzx"),
    ("up1", "xzy"),
    ("down0", "zxy"),
    ("down1", "yzx"),
)
LATE = ("down0", "down1")
NAMES = [p[0] for p in PARTS]
ORDER = dict(PARTS)


class Gather:
    def __init__(self, me, refs, send, recv, csend, crecv, lsend, lrecv):
        self.me = me
        self.refs = refs
        self.send, self.recv, self.csend, self.crecv = send, recv, csend, crecv
        self.lsend, self.lrecv = lsend, lrecv

    def block(self, part, chip, c):
        wa, wu, wd = self.refs
        m = pl.multiple_of
        if part in LATE:
            return wd.at[pl.ds(m(chip * 192 + 96 * LATE.index(part), 16), 96), pl.ds(m(c * 384, 128), 384)]
        rows = pl.ds(m(chip * 48, 16), 48)
        if part == "attn0":
            return wa.at[rows, pl.ds(m(c * WIDE, 128), 768)]
        if part == "attn1":
            return wa.at[rows, pl.ds(m(c * WIDE + 768, 128), 896)]
        if part == "up0":
            return wu.at[rows, pl.ds(m(c * 1536, 128), 768)]
        return wu.at[rows, pl.ds(m(c * 1536 + 768, 128), 768)]

    def half(self, part, c):
        wa, wu, wd = self.refs
        m = pl.multiple_of
        if part == "attn0":
            return wa.at[:, pl.ds(m(c * WIDE, 128), 768)]
        if part == "attn1":
            return wa.at[:, pl.ds(m(c * WIDE + 768, 128), 896)]
        if part == "up0":
            return wu.at[:, pl.ds(m(c * 1536, 128), 768)]
        return wu.at[:, pl.ds(m(c * 1536 + 768, 128), 768)]

    def chip(self, x, y, z):
        return (z * 2 + x) * 2 + y

    def copy(self, part, chip, way):
        i = NAMES.index(part)
        ref = self.block(part, chip, self.me.c)
        return pltpu.make_async_remote_copy(
            ref, ref, self.send.at[i, chip, WAYS.index(way)], self.recv.at[i, chip],
            device_id=self.me.to(way), device_id_type=MESH)

    def across(self, part, c):
        i = NAMES.index(part)
        ref = self.half(part, c)
        return pltpu.make_async_remote_copy(
            ref, ref, self.csend.at[i], self.crecv.at[i], device_id=self.me.to("core"), device_id_type=MESH)

    def onward(self, part, chip, axes):
        me = self.me
        for axis in axes:
            if axis == "z":
                pl.when(me.z < 3)(lambda: self.copy(part, chip, "up").start())
                pl.when(me.z > 0)(lambda: self.copy(part, chip, "down").start())
            else:
                self.copy(part, chip, axis).start()

    def own(self, part):
        me = self.me
        chip = self.chip(me.x, me.y, me.z)
        self.onward(part, chip, ORDER[part])
        if part in LATE:
            self.beside(part, chip, me.c).start()

    def origins(self, fx, fy, k, act):
        me = self.me
        x = 1 - me.x if fx else me.x
        y = 1 - me.y if fy else me.y
        if k == 0:
            act(self.chip(x, y, me.z), 0)
        else:
            pl.when(me.z >= k)(lambda: act(self.chip(x, y, me.z - k), -1))
            pl.when(me.z + k <= 3)(lambda: act(self.chip(x, y, me.z + k), 1))

    def arrival(self, part, fx, fy, k):
        moved = {"x": fx, "y": fy, "z": k}
        return max(i for i in range(3) if moved[ORDER[part][i]])

    def serve(self, part, fx, fy, k):
        me = self.me
        order = ORDER[part]
        stage = self.arrival(part, fx, fy, k)
        axis = order[stage]

        def act(chip, sign):
            if axis == "z":
                way, more = ("up", me.z < 3) if sign < 0 else ("down", me.z > 0)
                self.copy(part, chip, way).wait_recv()
                pl.when(more)(lambda: self.copy(part, chip, way).start())
            else:
                self.copy(part, chip, axis).wait_recv()
            self.onward(part, chip, order[stage + 1:])
            if part in LATE:
                self.beside(part, chip, me.c).start()

        self.origins(fx, fy, k, act)

    def beside(self, part, chip, c):
        i = LATE.index(part)
        ref = self.block(part, chip, c)
        return pltpu.make_async_remote_copy(
            ref, ref, self.lsend.at[i, chip], self.lrecv.at[i, chip], device_id=self.me.to("core"), device_id_type=MESH)

    def arrived(self, part):
        if part not in LATE:
            self.across(part, 1 - self.me.c).wait_recv()
            return

        def body(chip, _):
            self.beside(part, chip, 1 - self.me.c).wait_recv()
            return 0
        lax.fori_loop(0, 16, body, 0)

    def drain(self, part):
        me = self.me
        order = ORDER[part]

        if part in LATE:
            def body(chip, _):
                self.beside(part, chip, me.c).wait_send()
                return 0
            lax.fori_loop(0, 16, body, 0)
        else:
            self.across(part, me.c).wait_send()

        def sent(chip, axes, sign):
            for axis in axes:
                if axis == "z":
                    if sign <= 0:
                        pl.when(me.z < 3)(lambda: self.copy(part, chip, "up").wait_send())
                    if sign >= 0:
                        pl.when(me.z > 0)(lambda: self.copy(part, chip, "down").wait_send())
                else:
                    self.copy(part, chip, axis).wait_send()

        for fx in (0, 1):
            for fy in (0, 1):
                for k in range(4):
                    if fx + fy + k == 0:
                        sent(self.chip(me.x, me.y, me.z), order, 0)
                        continue
                    stage = self.arrival(part, fx, fy, k)
                    axes = order[stage:] if order[stage] == "z" else order[stage + 1:]
                    self.origins(fx, fy, k, lambda chip, sign: sent(
                        chip, axes, sign if order[stage] == "z" else 0))


def relayout(me, wide, refs, name):
    m = pl.multiple_of
    chip = (me.z * 2 + me.x) * 2 + me.y
    wa, wu, wd = refs

    def rows(base, count, stride):
        both = [wide[d, pl.ds(base, count, stride=stride), :] for d in range(2)]
        return jnp.concatenate(both, 0).astype(BF)

    if name == "up":
        for j in range(12):
            wu[pl.ds(m(chip * 48, 16), 48), pl.ds(m((me.c * 12 + j) * 128, 128), 128)] = rows(
                BASE[2] + me.c * 12 + j, 24, 24)
    elif name == "down":
        for j in range(3):
            wd[pl.ds(m(chip * 192, 16), 192), pl.ds(m((me.c * 3 + j) * 128, 128), 128)] = rows(BASE[3] + me.c * 3 + j, 96, 6)
    else:
        for j in range(6):
            wa[pl.ds(m(chip * 48, 16), 48), pl.ds(m(me.c * WIDE + j * 128, 128), 128)] = rows(
                BASE[0] + me.c * 12 + j, 24, 18)
            to = wa.at[pl.ds(m(chip * 48, 16), 48), pl.ds(m(me.c * WIDE + 768 + j * 128, 128), 128)]

            @pl.when(me.c == 0)
            def _():
                to[...] = rows(BASE[0] + 6 + j, 24, 18)

            @pl.when(me.c == 1)
            def _():
                to[...] = rows(BASE[1] + j, 24, 6)


GATHER_PLAN = (

    (16, 0, 48, 17, 1, 64, 18, 4, 32, 25, 8, 19, 2, 5, 21, 26, 27, 24, 3, 68, 6, 7, 49, 65, 12, 23, 22, 40, 20, 33, 80, 29, 72, 52, 30, 10, 9, 13, 11, 31, 50, 66, 36, 56, 28, 15, 14),
    (), (), (), (34,), (), (), (), (), (), (), (37, 51), (67, 84, 57), (), (), (), (), (), (), (), (38, 54),
    (88, 35, 74, 85, 73, 70, 75, 58, 41, 71, 42, 55, 53, 76, 44, 39, 81), (), (), (), (),
    (43, 60, 86, 61, 59, 78, 69), (79, 82, 45), (46, 87, 92, 77, 47, 62, 63, 93, 83), (), (), (), (), (), (), (), (),
    (), (), (), (94, 95, 89, 90, 91),
)

GATHER_X = 0


HEADS = 12
HD = 64
EPS = 1e-05
PAIRS = HEADS // 2

def nt(left, right):
    return lax.dot_general(left, right, (((1,), (1,)), ((), ())), preferred_element_type=F32)


def nn(left, right):
    return jnp.dot(left, right, preferred_element_type=F32)


def tn(left, right):
    return lax.dot_general(left, right, (((0,), (0,)), ((), ())), preferred_element_type=F32)


def tile(i, size):
    return pl.ds(pl.multiple_of(i * size, size), size)


def spread(sides, size, width):
    lane = lax.broadcasted_iota(jnp.int32, (128, width), 0)
    col = lax.broadcasted_iota(jnp.int32, (128, width), 1)
    owner = ((col.astype(F32) + 0.5) * (1.0 / size)).astype(jnp.int32)
    pick = (col - owner * size == lane).astype(F32).astype(BF)
    dev = lax.broadcasted_iota(jnp.int32, (16, width), 0) * 2
    col = lax.broadcasted_iota(jnp.int32, (16, width), 1)
    owner = ((col.astype(F32) + 0.5) * (1.0 / size)).astype(jnp.int32)
    total = jnp.zeros((16, width), F32)
    for c, rows in enumerate(sides):
        total = total + jnp.where(owner == dev + c, nn(rows.astype(BF), pick), 0.0)
    return jnp.sum(total, 0, keepdims=True)


def swap_rows(me, ref, s, send, recv):
    width = 256

    def block(index):
        return ref.at[tile(index, width), :]

    def copy(index, way, n):
        return pltpu.make_async_remote_copy(
            block(index), block(index), send.at[n], recv.at[n], device_id=me.to(way), device_id_type=MESH)

    mine = me.y * 2 + me.c
    over = (1 - me.y) * 2 + me.c
    return (copy(mine, "core", 0), copy(mine, "y", 1), copy(over, "core", 2)), (
        copy(me.y * 2 + 1 - me.c, "core", 0), copy(over, "y", 1), copy((1 - me.y) * 2 + 1 - me.c, "core", 2))


def head_rows(array, axis):
    lane = lax.broadcasted_iota(jnp.int32, array.shape, 1)
    zero = jnp.zeros_like(array)
    return jnp.concatenate([jnp.where(lane < HD, array, zero), jnp.where(lane >= HD, array, zero)], axis)


def forward_kernel(
    fq, fo, fu, fd, s0, s1, s2, s3, s4, s5, s6, s7, s8, x, cot, seg, pad, keep,
    to_out, to_a, to_u, to_xt, to_v, to_kt, to_e,
    hq8, hot, hr, hactt, hgp, hnlt, hn1, hr1, hgs, hsm, wd,
    flats, wide, wa, wu, smf, xall, kk, vv, kt, vt, st, ee, mask, vec, vecu, n2, xt, act, nl,
    out,
    fsend, frecv, send, recv, csend, crecv, lsend, lrecv, osem, xsend, xrecv,
):
    me = Place()
    s = me.y * 2 + me.c
    outs = []

    def put(held, to):
        outs.append(pltpu.make_async_copy(held, to, osem.at[len(outs)]))
        outs[-1].start()

    enter(me)
    refs = (wa, wu, wd)
    g = Gather(me, refs, send, recv, csend, crecv, lsend, lrecv)
    swaps = [
        pltpu.make_async_remote_copy(
            src, flats.at[pl.ds(b, n), :], fsend.at[i], frecv.at[i], device_id=me.to("core"), device_id_type=MESH)
        for i, (src, b, n) in enumerate(zip((fq, fo, fu, fd), BASE, LINES))
    ]
    for c in swaps:
        c.start()
    chip = (me.z * 2 + me.x) * 2 + me.y
    smf[0, 0:48, :] = jnp.zeros((48, 128), F32)
    for i, vector in enumerate((s0, s1, s2, s3, s4, s5, s6, s7, s8)):
        smf[0, i:i + 1, 0:vector.shape[0]] = vector[...].astype(F32).reshape(1, vector.shape[0])
    wa[pl.ds(pl.multiple_of(chip * 48, 16), 48), pl.ds(pl.multiple_of(me.c * WIDE + 1536, 128), 128)] = (
        smf[0, 0:48, :].astype(BF))
    xall[tile(s, 256), :] = x[...]
    xs, xr = swap_rows(me, xall, s, xsend, xrecv)
    xs[0].start()
    slot = iter(GATHER_PLAN)
    count = {}

    def tick():
        for code in next(slot, ()):
            if sum(count.values()) == GATHER_X:
                xs[1].start()
            p, fx, fy, k = NAMES[code // 16], code // 8 % 2, code // 4 % 2, code % 4
            if fx + fy + k:
                g.serve(p, fx, fy, k)
            else:
                unpack(p)
                g.own(p)
            count[p] = count.get(p, 0) + 1
            if count[p] == 16 and p not in LATE:
                g.across(p, me.c).start()

    unpacked = []

    def unpack(p):
        name = p.rstrip("01")
        if name in unpacked:
            return
        unpacked.append(name)
        for i in {"attn": (0, 1), "up": (2,), "down": (3,)}[name]:
            src, b, n = (fq, fo, fu, fd)[i], BASE[i], LINES[i]
            wide[me.c, pl.ds(b, n), :] = src[...].astype(F32)
            swaps[i].wait_recv()
            wide[1 - me.c, pl.ds(b, n), :] = flats[pl.ds(b, n), :].astype(F32)
        relayout(me, wide, refs, name)

    codes = jnp.where(pad[...] > 0, seg[...], -1).astype(F32)
    mine = seg[:, tile(s, 256)].astype(F32)
    for j in range(8):
        column = jnp.broadcast_to(codes[:, j * 128:(j + 1) * 128], (128, 128)).T
        for i in range(2):
            row = jnp.broadcast_to(mine[:, i * 128:(i + 1) * 128], (128, 128))
            mask[pl.ds(j * 128, 128), pl.ds(i * 128, 128)] = jnp.where(column == row, 0.0, -1e9)

    tick()
    xr[1].wait_recv()
    xs[2].start()
    g.arrived("attn0")
    g.arrived("attn1")
    xr[0].wait_recv()
    xr[2].wait_recv()
    put(wa, to_a)
    for j in range(4):
        xt[:, pl.ds(j * 256, 256)] = xall[pl.ds(j * 256, 256), :].T

    for c in range(2):
        smf[c] = wa[:, pl.ds(c * WIDE + 1536, 128)].astype(F32)
    vec[...] = jnp.zeros_like(vec)
    for i in range(8):
        vec[pl.ds(i, 1), :] = spread([smf[c, pl.ds(i, 16, stride=48), :] for c in range(2)], 24, 768)
    vecu[...] = spread([smf[c, pl.ds(8, 16, stride=48), :] for c in range(2)], 96, 3072)

    tick()
    for j in range(3):
        w = pl.ds(j * 256, 256)
        hq8[:, w] = ((nn(x[...], wa[:, w]) + vec[0:1, w]).astype(BF).astype(F32) * 0.125).astype(BF)
    for j in range(3):
        w = pl.ds(j * 256, 256)
        for r in range(2):
            rows = pl.ds(r * 512, 512)
            tick()
            k = nn(xall[rows, :], wa[:, pl.ds(768 + j * 256, 256)]).astype(BF)
            kk[rows, w] = k
            kt[w, rows] = k.T
            v = (nn(xall[rows, :], wa[:, pl.ds(WIDE + j * 256, 256)]) + vec[1:2, w]).astype(BF)
            vv[rows, w] = v
            vt[w, rows] = v.T
    put(xt, to_xt)
    put(vv, to_v)
    put(kt, to_kt)

    for p in range(PAIRS):
        w = pl.ds(p * 128, 128)
        qm = head_rows(hq8[:, w], 0)
        tick()
        top = jnp.full((8, 512), -3e38, F32)
        for c in range(4):
            rows = pl.ds(c * 256, 256)
            one = mask[rows, :]
            v = nt(kk[rows, w], qm) + jnp.concatenate([one, one], 1)
            st[rows, :] = v
            top = jnp.maximum(top, jnp.max(v.reshape(32, 8, 512), 0))
        top = jnp.max(top, 0, keepdims=True)
        tick()
        total = jnp.zeros((8, 512), F32)
        for c in range(8):
            rows = pl.ds(c * 128, 128)
            v = jnp.exp(st[rows, :] - top)
            ee[p, rows, :] = v.astype(BF)
            total = total + jnp.sum(v.reshape(16, 8, 512), 0)
        inverse = 1.0 / jnp.sum(total, 0, keepdims=True)
        hr[pl.ds(p, 1), :] = inverse
        tick()
        for h in range(2):
            o = nn(vt[pl.ds(p * 128 + h * 64, 64), :], ee[p, :, pl.ds(h * 256, 256)])
            hot[pl.ds(p * 128 + h * 64, 64), :] = (o * inverse[:, h * 256:(h + 1) * 256]).astype(BF)
        put(ee.at[p], to_e.at[p])

    tick()
    n2[...] = tn(hot[...], wa[:, pl.ds(WIDE + 768, 768)])
    tick()
    for r in range(8):
        rows = pl.ds(r * 32, 32)
        value = x[rows, :].astype(F32) + n2[rows, :] + vec[2:3, :]
        centred = value - jnp.mean(value, -1, keepdims=True)
        r1 = lax.rsqrt(jnp.mean(centred * centred, -1, keepdims=True) + EPS)
        n1 = centred * r1
        hn1[rows, :] = n1
        hr1[rows, :] = jnp.broadcast_to(r1, (32, 128))
        normed = n1 * vec[3:4, :] + vec[4:5, :]
        n2[rows, :] = normed
        nl[rows, :] = normed.astype(BF)
    hnlt[...] = nl[...].T
    for p in ("attn0", "attn1"):
        g.drain(p)
    tick()
    g.arrived("up0")
    g.arrived("up1")
    put(wu, to_u)

    for j in range(12):
        w = pl.ds(j * 256, 256)
        if j:
            tick()
        before = nn(nl[...], wu[:, w]) + vecu[:, w]
        phi = 0.5 * (1.0 + lax.erf(before * 0.7071067811865476))
        a = (before * phi).astype(BF)
        act[:, w] = a
        hactt[w, :] = a.T
        hgp[:, w] = (phi + before * 0.3989422804014327 * jnp.exp(-0.5 * before * before)).astype(BF)

    tick()
    for p in ("up0", "up1", "down0", "down1"):
        g.drain(p)
    g.arrived("down0")
    g.arrived("down1")

    for j in range(3):
        w = pl.ds(j * 256, 256)
        n2[:, w] += nn(act[...], wd[:, w]) + vec[5:6, w]
    hsm[...] = jnp.zeros_like(hsm)
    hsm[2:3, :] = vec[3:4, :]
    kept = keep[...] > 0
    gain = jnp.zeros((8, 768), F32)
    shift = jnp.zeros((8, 768), F32)
    for r in range(8):
        rows = pl.ds(r * 32, 32)
        value = n2[rows, :]
        centred = value - jnp.mean(value, -1, keepdims=True)
        r2 = lax.rsqrt(jnp.mean(centred * centred, -1, keepdims=True) + EPS)
        n = centred * r2
        out[rows, :] = jnp.where(kept, n * vec[6:7, :] + vec[7:8, :], x[rows, :].astype(F32)).astype(BF)
        grad = jnp.where(kept, cot[rows, :].astype(F32), 0.0)
        gain = gain + jnp.sum((grad * n).reshape(4, 8, 768), 0)
        shift = shift + jnp.sum(grad.reshape(4, 8, 768), 0)
        c = grad * vec[6:7, :]
        hgs[rows, :] = r2 * (c - jnp.mean(c, -1, keepdims=True) - n * jnp.mean(c * n, -1, keepdims=True))
    hsm[0:1, :] = jnp.sum(gain, 0, keepdims=True)
    hsm[1:2, :] = jnp.sum(shift, 0, keepdims=True)
    put(out, to_out)

    for c in swaps:
        c.wait_send()
    for c in xs:
        c.wait_send()
    for o in outs:
        o.wait()


def vmem(*shapes):
    return [pltpu.VMEM(s, d) for s, d in shapes]


HELD = vmem(
    ((256, 768), BF), ((768, 256), BF), ((8, 512), F32), ((3072, 256), BF), ((256, 3072), BF), ((768, 256), BF),
    ((256, 768), F32), ((256, 128), F32), ((256, 768), F32), ((8, 768), F32), ((3072, 768), BF),
)
SPOOLED = (
    ((768, 2 * WIDE), BF), ((768, 3072), BF), ((768, 1024), BF), ((1024, 768), BF), ((768, 1024), BF),
    ((PAIRS, 1024, 512), BF),
)
FORWARD_SCOPE = vmem(
    ((1728, 128), BF), ((2, 1728, 128), F32), ((768, 2 * WIDE), BF), ((768, 3072), BF), ((2, 768, 128), F32),
    ((1024, 768), BF), ((1024, 768), BF), ((1024, 768), BF), ((768, 1024), BF), ((768, 1024), BF), ((1024, 512), F32),
    ((PAIRS, 1024, 512), BF), ((1024, 256), F32), ((8, 768), F32), ((1, 3072), F32), ((256, 768), F32),
    ((768, 1024), BF), ((256, 3072), BF), ((256, 768), BF), ((256, 768), BF),
)


def forward_semaphores():
    n = len(PARTS)
    dma = pltpu.SemaphoreType.DMA
    return [dma(s) for s in (
        (4,), (4,), (n, 16, 4), (n, 16), (n,), (n,), (2, 16), (2, 16), (24,), (3,), (3,))]


RPARTS = (
    ("down", 3, "yzx", 192, 0, 0, 384),
    ("up", 2, "xzy", 48, 0, 0, 1536),
    ("out", 1, "zyx", 48, 0, 0, 384),
    ("qkv0", 0, "zxy", 48, 0, 0, 384),
    ("qkv1", 0, "zyx", 48, 0, 384, 384),
    ("qkv2", 0, "zyx", 48, 0, 768, 384),
)
HALF = (1152, 384, 1536, 384)
CHIPROWS = (48, 48, 48, 192)
ROWS = (768, 768, 768, 3072)
SIZES = {"x": 2, "y": 2, "z": 4}
LINKS = ("up", "down", "x", "y")


def slots(order, axis):
    n = 4 if axis == "z" else 1
    for a in order[: order.index(axis)]:
        n *= SIZES[a]
    return n


def landing_shapes():
    shapes = []
    for name, mat, order, rows, ro, co, cols in RPARTS:
        for way in LINKS:
            axis = "z" if way in ("up", "down") else way
            shapes.append(pltpu.VMEM((slots(order, axis), rows, cols), BF))
    return shapes


class Scatter:
    def __init__(self, me, grads, half, lands, finals, send, recv):
        self.me, self.grads, self.half, self.lands, self.finals = me, grads, half, lands, finals
        self.send, self.recv = send, recv

    def chip(self, x, y, z):
        return (z * 2 + x) * 2 + y

    def part(self, refs, i, dest):
        name, mat, order, rows, ro, co, cols = RPARTS[i]
        first = pl.multiple_of(self.chip(*dest) * CHIPROWS[mat] + ro, 16)
        return refs[mat].at[pl.ds(first, rows), pl.ds(co, cols)]

    def block(self, i, dest):
        return self.part(self.grads, i, dest)

    def slot(self, i, way, dest):
        order = RPARTS[i][2]
        axis = "z" if way in ("up", "down") else way
        coords = dict(zip("xyz", dest))
        index = coords["z"] if axis == "z" else 0
        for a in order[: order.index(axis)]:
            index = index * SIZES[a] + coords[a]
        return index

    def land(self, i, way, dest):
        return self.lands[i * 4 + LINKS.index(way)].at[self.slot(i, way, dest)]

    def copy(self, i, way, dest):
        chip = self.chip(*dest)
        return pltpu.make_async_remote_copy(
            self.block(i, dest), self.land(i, way, dest), self.send.at[i, chip],
            self.recv.at[i, LINKS.index(way), chip], device_id=self.me.to(way), device_id_type=MESH)

    def stage(self, i, fx, fy, k):
        moved = {"x": fx, "y": fy, "z": k}
        return max(s for s in range(3) if moved[RPARTS[i][2][s]])

    def take(self, i, way, dest):
        self.copy(i, way, dest).wait_recv()
        ref = self.block(i, dest)
        ref[...] = ref[...] + self.land(i, way, dest)[...]

    def total(self, i, dest, ways):
        value = self.block(i, dest)[...] + self.part(self.half, i, dest)[...]
        for way in ways:
            self.copy(i, way, dest).wait_recv()
            value = value + self.land(i, way, dest)[...]
        return value

    def serve(self, i, fx, fy, k):
        me = self.me
        order = RPARTS[i][2]
        stage = self.stage(i, fx, fy, k)
        axis = order[stage]

        def act(dest, sign):
            way = axis
            if axis == "z":
                way, more = ("down", me.z < 3) if sign < 0 else ("up", me.z > 0)
                pl.when(more)(lambda: self.take(i, way, dest))
            if "z" in order[stage + 1:]:
                pl.when(me.z < 3)(lambda: self.take(i, "down", dest))
                pl.when(me.z > 0)(lambda: self.take(i, "up", dest))
            value = self.total(i, dest, [a for a in order[stage + 1:] if a != "z"])
            self.block(i, dest)[...] = value
            self.copy(i, way, dest).start()

        self.dests(fx, fy, k, act)

    def dests(self, fx, fy, k, act):
        me = self.me
        x = 1 - me.x if fx else me.x
        y = 1 - me.y if fy else me.y
        if k == 0:
            act((x, y, me.z), 0)
        else:
            pl.when(me.z >= k)(lambda: act((x, y, me.z - k), -1))
            pl.when(me.z + k <= 3)(lambda: act((x, y, me.z + k), 1))

    def own(self, i):
        dest = (self.me.x, self.me.y, self.me.z)
        name, mat, order, rows, ro, co, cols = RPARTS[i]
        self.finals[mat].at[pl.ds(ro, rows), pl.ds(co, cols)][...] = (
            self.block(i, dest)[...].astype(F32) + self.part(self.half, i, dest)[...].astype(F32))

    def finish(self, i):
        name, mat, order, rows, ro, co, cols = RPARTS[i]
        me = self.me
        dest = (me.x, me.y, me.z)
        fin = self.finals[mat].at[pl.ds(ro, rows), pl.ds(co, cols)]

        def add(way):
            self.copy(i, way, dest).wait_recv()
            fin[...] += self.land(i, way, dest)[...].astype(F32)
        for axis in order:
            if axis == "z":
                pl.when(me.z < 3)(lambda: add("down"))
                pl.when(me.z > 0)(lambda: add("up"))
            else:
                add(axis)

    def drain(self, i):
        for fx in (0, 1):
            for fy in (0, 1):
                for k in range(4):
                    if fx + fy + k:
                        axis = RPARTS[i][2][self.stage(i, fx, fy, k)]
                        self.dests(fx, fy, k, lambda dest, sign: self.copy(
                            i, axis if axis != "z" else ("down" if sign < 0 else "up"), dest).wait_send())


SCATTER_PLAN = (
    (15, 14), (), (), (), (), (), (), (), (), (), (), (7, 11, 13), (), (), (), (), (), (31, 29), (6, 10, 23),
    (22, 12, 3), (), (), (), (9, 21, 5, 30, 27), (), (), (), (), (), (), (), (), (41, 42, 19, 2, 40), (), (), (), (),
    (), (), (), (), (), (), (), (47, 61, 18, 60, 62, 63, 20, 8, 45, 55, 43, 28), (), (), (), (), (), (),
    (46, 26, 57, 44, 56, 39, 1), (), (), (), (), (), (), (76, 77, 53, 75, 59, 4, 17, 79, 25, 58, 73, 38, 78, 74), (),
    (), (), (), (), (), (), (), (), (95, 71, 94, 54, 93, 35, 51, 37, 91), (),
    (87, 67, 90, 70, 86, 34, 92, 89, 69, 50), (83, 85, 72, 24, 52, 66, 33), (), (82, 36, 68, 84, 49, 65, 88), (81,),
    (), (), (), (16, 0, 48, 32, 64, 80),
)

FLATROWS = ((24, 18, 432), (24, 6, 144), (24, 24, 576), (96, 6, 576))


def column(mat, c, j):
    if mat:
        return c * (FLATROWS[mat][1] // 2) + j
    group, t = j // 3, j % 3
    if c == 0:
        return 2 * group + t if t < 2 else 6 + 2 * group
    return 7 + 2 * group if t == 0 else 11 + 2 * group + t


def flatten(me, mat, finals, sides, out):
    rows, tiles, lines = FLATROWS[mat]
    half = tiles // 2
    for c in range(2):
        @pl.when(me.c == c)
        def _():
            for j in range(half):
                mine = finals[mat][pl.ds(pl.multiple_of(me.c * rows, 8), rows), pl.ds(j * 128, 128)]
                out[pl.ds(column(mat, c, j), rows, stride=tiles), :] = mine
                out[pl.ds(column(mat, 1 - c, j), rows, stride=tiles), :] = sides[mat][:, pl.ds(j * 128, 128)]


def colsum(array):
    return jnp.sum(array.astype(F32), 0, keepdims=True)


def backward_kernel(ha, hu, hxt, hv, hkt, he, held, cot, keep, results, scope, semaphores, here):
    q8, ot, rr, actt, gp, nlt, n1, r1, gs, sm0, wbig = held
    ingrad, oq, oo, ou, od, chosen = results
    rest = list(scope)
    lands, rest = rest[:4 * len(RPARTS)], rest[4 * len(RPARTS):]
    grads, rest = rest[:4], rest[4:]
    stage, rest = rest[:3], rest[3:]
    stage = [stage[1].at[:, pl.ds(0, HALF[0])]] + stage
    half, rest = rest[:4], rest[4:]
    finals, rest = rest[:4], rest[4:]
    sides, rest = rest[:4], rest[4:]
    wo, xt, vv, kt, ee, ds, gbr, gbef, first, gts, gsa, dq, dkv, dx, dxc, dxy, acc, sland, osm = rest
    wsem, isem, esem, csend, crecv, send, recv, fsend, frecv, dsend, drecv, asend, arecv = semaphores
    me = Place()
    s = me.y * 2 + me.c
    wus = [pltpu.make_async_copy(hu.at[:, pl.ds(q * 768, 768)], wbig.at[pl.ds(q * 768, 768), :], wsem.at[4 + q]) for q in range(4)]
    wqs = [pltpu.make_async_copy(ha.at[:, pl.ds((0, 768, WIDE)[q], 768)], wbig.at[pl.ds(q * 768, 768), :], wsem.at[8 + q]) for q in range(3)]
    others = [pltpu.make_async_copy(a, b, isem.at[i]) for i, (a, b) in enumerate(((ha.at[:, pl.ds(WIDE + 768, 768)], wo), (hv, vv), (hkt, kt), (hxt, xt)))]
    ees = [pltpu.make_async_copy(he.at[p], ee.at[p % 2], esem.at[p]) for p in range(PAIRS)]
    greet(me, here)

    sc = Scatter(me, grads, half, lands, finals, send, recv)

    def swap(mat, piece=0):
        cut = {
            0: (slice(None), pl.ds(piece * 384, 384)), 1: (slice(None), slice(None)),
            2: (slice(None), pl.ds(piece * 512, 512)), 3: (pl.ds(piece * 768, 768), slice(None)),
        }[mat]
        n = (0, 3, 4, 7)[mat] + piece
        return pltpu.make_async_remote_copy(
            stage[mat].at[cut], half[mat].at[cut], csend.at[n], crecv.at[n], device_id=me.to("core"), device_id_type=MESH)

    def last(mat):
        rows = FLATROWS[mat][0]
        src = finals[mat].at[pl.ds(pl.multiple_of((1 - me.c) * rows, 8), rows), :]
        return pltpu.make_async_remote_copy(
            src, sides[mat], fsend.at[mat], frecv.at[mat], device_id=me.to("core"), device_id_type=MESH)

    def swapped(mat):
        for piece in range((3, 1, 3, 4)[mat]):
            swap(mat, piece).wait_recv()

    def unstaged(mat):
        for piece in range((3, 1, 3, 4)[mat]):
            swap(mat, piece).wait_send()

    slot = iter(SCATTER_PLAN)
    count = {}

    def tick():
        for code in next(slot, ()):
            i, fx, fy, k = code // 16, code // 8 % 2, code // 4 % 2, code % 4
            if fx + fy + k:
                sc.serve(i, fx, fy, k)
            else:
                sc.own(i)
                sc.finish(i)
                mat = RPARTS[i][1]
                count[mat] = count.get(mat, 0) + 1
                if count[mat] == (3, 1, 1, 1)[mat]:
                    last(mat).start()

    def arrange(value_ref, to):
        to[:, 0:384] = value_ref[:, pl.ds(pl.multiple_of(me.c * 384, 128), 384)]
        to[:, 384:768] = value_ref[:, pl.ds(pl.multiple_of((1 - me.c) * 384, 128), 384)]

    osm[...] = jnp.zeros_like(osm)
    osm[6:8, :] = sm0[0:2, :]
    gsa[...] = gs[...].astype(BF)
    osm[5:6, :] = colsum(gsa[...])
    arrange(gsa, gbr)

    for j in range(12):
        w = pl.ds(j * 256, 256)
        v = nn(actt[w, :], gbr[...]).astype(BF)
        grads[3][w, :] = v[:, 0:384]
        stage[3][w, :] = v[:, 384:768]
        if j == 2:
            pl.semaphore_wait(here, 5)
        if j % 3 == 2:
            swap(3, j // 3).start()

    for q in range(4):
        for j in range(3):
            w = pl.ds(q * 768 + j * 256, 256)
            gb = nt(gsa[...], wbig[w, :]).astype(BF) * gp[:, w]
            gbef[:, w] = gb
            osm[8 + q:9 + q, pl.ds(j * 256, 256)] = colsum(gb)
        wus[q].start()
        if q == 0:
            swapped(3)
        tick()

    for c in others:
        c.start()
    ees[0].start()
    ees[1].start()
    for j in range(6):
        w = pl.ds(j * 256, 256)
        tick()
        stage[2][:, w] = nn(nlt[...], gbef[:, pl.ds(pl.multiple_of((1 - me.c) * 1536 + j * 256, 256), 256)]).astype(BF)
        if j % 2:
            swap(2, j // 2).start()
    for j in range(6):
        w = pl.ds(j * 256, 256)
        tick()
        grads[2][:, w] = nn(nlt[...], gbef[:, pl.ds(pl.multiple_of(me.c * 1536 + j * 256, 256), 256)]).astype(BF)
    for c in wus:
        c.wait()
    tick()
    swapped(2)

    for j in range(3):
        w = pl.ds(j * 256, 256)
        tick()
        total = gs[:, w]
        for q in range(4):
            total += nt(gbef[:, pl.ds(q * 768, 768)], wbig[pl.ds(q * 768 + j * 256, 256), :])
        first[:, w] = total
    for c in wqs:
        c.start()

    gain = jnp.zeros((8, 768), F32)
    shift = jnp.zeros((8, 768), F32)
    for r in range(8):
        rows = pl.ds(r * 32, 32)
        if r % 4 == 0:
            tick()
        gn = first[rows, :]
        n = n1[rows, :]
        gain = gain + jnp.sum((gn * n).reshape(4, 8, 768), 0)
        shift = shift + jnp.sum(gn.reshape(4, 8, 768), 0)
        c1 = gn * sm0[2:3, :]
        gf = r1[rows, 0:1] * (c1 - jnp.mean(c1, -1, keepdims=True) - n * jnp.mean(c1 * n, -1, keepdims=True))
        first[rows, :] = gf
        gsa[rows, :] = gf.astype(BF)
    osm[3:4, :] = jnp.sum(gain, 0, keepdims=True)
    osm[4:5, :] = jnp.sum(shift, 0, keepdims=True)
    osm[2:3, :] = colsum(gsa[...])
    arrange(gsa, gbr)
    tick()

    for j in range(3):
        w = pl.ds(j * 256, 256)
        v = nn(ot[w, :], gbr[...]).astype(BF)
        grads[1][w, :] = v[:, 0:384]
        stage[1][w, :] = v[:, 384:768]
    swap(1).start()
    for c in others:
        c.wait()
    for p in range(PAIRS):
        w = pl.ds(p * 128, 128)
        if p % 2 == 0:
            tick()
        g = nt(wo[w, :], gsa[...]).astype(BF).astype(F32)
        scale = jnp.concatenate(
            [jnp.broadcast_to(rr[p:p + 1, h * 256:(h + 1) * 256], (64, 256)) for h in range(2)], 0)
        gts[w, :] = (g * scale).astype(BF)
    swapped(1)

    mine = xt.at[:, tile(s, 256)]

    def qkv_grads(group):
        q = pl.ds(group * 256, 256)
        v = pl.ds(768 + group * 256, 256)
        mid = pl.ds(group * 384, 384)

        def put(r, a, b):
            rows = pl.ds(r * 256, 256)
            vq = nn(mine[rows, :], dq[:, q]).astype(BF)
            vk = nn(xt[rows, :], dkv[:, q]).astype(BF)
            vv_ = nn(xt[rows, :], dkv[:, v]).astype(BF)
            a[rows, pl.ds(group * 384, 256)] = vq
            a[rows, pl.ds(group * 384 + 256, 128)] = vk[:, 0:128]
            b[rows, pl.ds(group * 384, 128)] = vk[:, 128:256]
            b[rows, pl.ds(group * 384 + 128, 256)] = vv_

        for r in range(3):
            tick()
            pl.when(me.c == 0)(lambda: put(r, grads[0], stage[0]))
            pl.when(me.c == 1)(lambda: put(r, stage[0], grads[0]))
        swap(0, group).start()

    for p in range(PAIRS):
        w = pl.ds(p * 128, 128)
        g = gts[w, :]
        both = ot[w, :].astype(F32) * g.astype(F32)
        delta = jnp.concatenate([jnp.sum(both[0:64], 0, keepdims=True), jnp.sum(both[64:128], 0, keepdims=True)], 1)
        gm = head_rows(g.T, 0)
        qm = head_rows(q8[:, w], 0)
        ees[p].wait()
        e = ee.at[p % 2]
        for c in range(4):
            rows = pl.ds(c * 256, 256)
            if c % 2 == 0:
                tick()
            dp = nt(vv[rows, w], gm)
            ds[rows, :] = e[rows, :] * (dp - delta).astype(BF)
        tick()
        dkv[:, w] = nn(ds[...], qm).astype(BF)
        tick()
        dkv[:, pl.ds(768 + p * 128, 128)] = nn(e[...], gm).astype(BF)
        tick()
        dqt = jnp.concatenate([
            nn(kt[pl.ds(p * 128 + h * 64, 64), :], ds[:, pl.ds(h * 256, 256)]) for h in range(2)], 0)
        dq[:, w] = (dqt * 0.125).astype(BF).T
        if p + 2 < PAIRS:
            ees[p + 2].start()
        if p == 1:
            unstaged(2)
        if p % 2:
            qkv_grads(p // 2)
        if p in (2, 4):
            swap(0, p // 2 - 1).wait_recv()
            tick()

    osm[0:1, :] = colsum(dq[...])
    osm[1:2, :] = colsum(dkv[:, pl.ds(768, 768)])

    acc[0] = osm[...]
    pairz = {"outer": (me.z + 1 - 2 * (me.z % 2)) * 2 + me.x}
    smalls = [
        pltpu.make_async_remote_copy(acc.at[i], sland.at[i], asend.at[i], arecv.at[i], device_id=to, device_id_type=MESH)
        for i, to in enumerate((me.to("core"), me.to("x"), me.to("y"), pairz, me.to("far")))
    ]
    smalls[0].start()

    def small_step(i):
        smalls[i].wait_recv()
        acc[i + 1] = acc[i] + sland[i]
        if i < 4:
            smalls[i + 1].start()

    for c in wqs:
        c.wait()

    for j in range(3):
        w = pl.ds(j * 256, 256)
        for r in range(2):
            rows = pl.ds(r * 512, 512)
            if j == 0 and r == 1:
                swap(0, 2).wait_recv()
            tick()
            dx[rows, w] = (
                nt(dkv[rows, 0:768], wbig[pl.ds(768 + j * 256, 256), :])
                + nt(dkv[rows, 768:1536], wbig[pl.ds(1536 + j * 256, 256), :])).astype(BF)
            if r:
                small_step(j)
        first[:, w] += nt(dq[...], wbig[w, :])

    def dx_copy(n):
        if n < 2:
            yy = me.y if n == 0 else 1 - me.y
            return pltpu.make_async_remote_copy(
                dx.at[tile(yy * 2 + 1 - me.c, 256), :], dxc.at[n], dsend.at[n], drecv.at[n],
                device_id=me.to("core"), device_id_type=MESH)
        return pltpu.make_async_remote_copy(
            dx.at[tile((1 - me.y) * 2 + me.c, 256), :], dxy, dsend.at[2], drecv.at[2],
            device_id=me.to("y"), device_id_type=MESH)
    dx_copy(1).start()
    dx_copy(0).start()
    dx_copy(1).wait_recv()
    over = tile((1 - me.y) * 2 + me.c, 256)
    dx[over, :] = (dx[over, :].astype(F32) + dxc[1].astype(F32)).astype(BF)
    dx_copy(2).start()

    for i in range(5):
        tick()
        if i < 2:
            small_step(3 + i)
    tick()
    owner = ((me.z * 2 + me.x) * 4 + s).astype(F32)
    at = lax.broadcasted_iota(jnp.int32, (768, 128), 0).astype(F32)
    lane = lax.broadcasted_iota(jnp.int32, (768, 128), 1).astype(F32)

    def choose(rows, start, size):
        pick = jnp.where((at == start + lane) & (lane < size), 1.0, 0.0)
        return jnp.dot(rows, pick, precision=lax.Precision.HIGHEST, preferred_element_type=F32)
    up = jnp.zeros((8, 128), F32)
    for q in range(4):
        up = up + choose(acc[5, 8 + q:9 + q, :], owner * 96 - q * 768, 96)
    chosen[0:8, :] = choose(acc[5, 0:8, :], owner * 24, 24)
    chosen[8:16, :] = up
    for i in range(len(RPARTS)):
        sc.drain(i)
    for mat in (3, 2, 1):
        last(mat).wait()
        flatten(me, mat, finals, sides, (oq, oo, ou, od)[mat])
    dx_copy(0).wait_recv()
    dx_copy(2).wait_recv()
    total = first[...] + dx[tile(s, 256), :].astype(F32) + dxc[0].astype(F32) + dxy[...].astype(F32)
    ingrad[...] = jnp.where(keep[...] > 0, total, cot[...].astype(F32)).astype(BF)
    for mat in (3, 1, 0):
        unstaged(mat)
    for n in range(3):
        dx_copy(n).wait_send()
    for c in smalls:
        c.wait_send()
    last(0).wait()
    flatten(me, 0, finals, sides, oq)


def backward_scope():
    halves = [((ROWS[m], HALF[m]), BF) for m in range(4)]
    return landing_shapes() + vmem(
        *halves, *halves[1:], *halves,
        *(((CHIPROWS[m], HALF[m]), F32) for m in range(4)),
        *(((FLATROWS[m][0], HALF[m]), F32) for m in range(4)),
        ((768, 768), BF), ((768, 1024), BF), ((1024, 768), BF), ((768, 1024), BF), ((2, 1024, 512), BF),
        ((1024, 512), BF), ((256, 768), BF), ((256, 3072), BF), ((256, 768), F32), ((768, 256), BF),
        ((256, 768), BF), ((256, 768), BF), ((1024, 1536), BF), ((1024, 768), BF), ((2, 256, 768), BF),
        ((256, 768), BF), ((6, 16, 768), F32), ((5, 16, 768), F32), ((16, 768), F32),
    )


def backward_semaphores():
    n = len(RPARTS)
    dma = pltpu.SemaphoreType.DMA
    return [dma(s) for s in (
        (11,), (4,), (PAIRS,), (11,), (11,), (n, 16), (n, 4, 16), (4,), (4,), (3,), (3,), (5,), (5,))]


RESULTS = [((256, 768), BF)] + [((FLATROWS[m][2], 128), F32) for m in range(4)] + [((16, 128), F32)]


def layer_kernel(*refs):
    def split(n):
        nonlocal refs
        head, refs = refs[:n], refs[n:]
        return head
    ins, out, spools, results = split(18), split(1), split(6), split(6)
    held, first_sems, second_sems, here = split(11), split(11), split(13), refs[0]
    cot, keep = ins[14], ins[17]
    pl.run_scoped(lambda *scope: forward_kernel(*ins, *out, *spools, *held, *scope, *first_sems), *FORWARD_SCOPE)
    pl.run_scoped(
        lambda *scope: backward_kernel(*spools, held, cot, keep, results, scope, second_sems, here), *backward_scope())


def layer_call(*args):
    a = pl.BlockSpec(memory_space=pl.ANY)
    v = pl.BlockSpec(memory_space=pltpu.VMEM)
    out = ((256, 768), BF)
    return pl.pallas_call(
        layer_kernel,
        out_shape=[jax.ShapeDtypeStruct(s, d) for s, d in (out,) + SPOOLED + tuple(RESULTS)],
        in_specs=[v] * 18,
        out_specs=[a] * 7 + [v] * 6,
        scratch_shapes=HELD + forward_semaphores() + backward_semaphores() + [pltpu.SemaphoreType.REGULAR],
        compiler_params=pltpu.CompilerParams(collective_id=1, has_side_effects=True, vmem_limit_bytes=(63 << 20) + (800 << 10)),
        name="layer",
    )(*args)


SMALL_SIZES = (24,) * 8 + (96,)


def finish_kernel(*refs):
    ins, small, outs, smalls = refs[:6], refs[6], refs[7:13], refs[13:22]
    for a, b in zip(ins, outs):
        b[...] = a[...]
    for i, (to, size) in enumerate(zip(smalls, SMALL_SIZES)):
        to[...] = small[i, 0:size]


def finish_call(*args):
    v = pl.BlockSpec(memory_space=pltpu.VMEM)
    return pl.pallas_call(
        finish_kernel,
        out_shape=[jax.ShapeDtypeStruct(x.shape, x.dtype) for x in args[:6]]
        + [jax.ShapeDtypeStruct((size,), F32) for size in SMALL_SIZES],
        in_specs=[v] * 7,
        out_specs=[v] * 15,
        name="finish",
    )(*args)


AXES = ("outer", "inner", "seq")
SMALLS = (1, 2, 4, 5, 6, 10, 11, 12, 8)


def to_part(flat):
    inner = lax.axis_size("inner")
    if inner == 1:
        return flat
    every = lax.all_gather(flat, ("inner", "seq"), axis=0, tiled=True)
    size = flat.shape[0] * inner
    return lax.dynamic_slice_in_dim(every, lax.axis_index("seq") * size, size, 0)


def whole_scatter(part):
    inner = lax.axis_size("inner")
    if inner == 1:
        return part
    every = lax.psum(lax.all_gather(part, "seq", axis=0, tiled=True), "inner")
    size = part.shape[0] // inner
    index = lax.axis_index("inner") * lax.axis_size("seq") + lax.axis_index("seq")
    return lax.dynamic_slice_in_dim(every, index * size, size, 0)


def shards(inputs, *rest):
    params, (cotangent, segment_ids, pad_mask, keep_flag) = rest[:13], rest[13:]
    parts = [to_part(p) for p in params]
    x, cot = inputs[0], cotangent[0]
    keep = keep_flag.reshape(1, 1)
    out, *rest = layer_call(
        *(parts[i].reshape(-1, 128) for i in (0, 3, 7, 9)), *(parts[i] for i in SMALLS), x, cot,
        segment_ids, pad_mask, keep
    )
    grad, *big, small = rest[6:]
    out, grad, *rest = finish_call(out, grad, *big, small)
    big = [whole_scatter(part.reshape(-1)) for part in rest[:4]]
    q, v, ob, g1, b1, db, g2, b2, ub = (whole_scatter(part) for part in rest[4:])
    return (out[None], grad[None], big[0], q, v, big[1], ob, g1, b1, big[2], ub, big[3], db, g2, b2)


def solution(mesh):
    fsdp, seq = mesh.shape["fsdp"], mesh.shape["seq"]
    mesh = Mesh(mesh.devices.reshape(8, fsdp // 8, seq), AXES)
    tokens = P(("outer", "inner"), "seq", None)
    flat = P(AXES)
    rows = P(("outer", "inner"), None)
    return jax.shard_map(
        shards,
        mesh=mesh,
        in_specs=(tokens,) + (flat,) * 13 + (tokens, rows, rows, P(("outer", "inner"))),
        out_specs=(tokens, tokens) + (flat,) * 13,
        check_vma=False,
    )
```
